32 devices in a mesh: img: 8 (over z, x), rep: 4 (over y, core).
Axes of the slice: x: 2, y: 2, z: 4, core: 2. Of those that a mesh axis runs over, the one named last changes fastest.
Arguments:
- pair_images: int32 [96, 2], P('img'), may hold values from 0 to 63, as said below
- depths: float32 [64, 147456], P('img', 'rep'), may hold values from 0.5 to 4
- depth_moment: float32 [64, 147456], P('img', 'rep'), may hold values from -8 to 8
- depth_second: float32 [64, 147456], P('img', 'rep'), may hold values from 1 to 100
- cameras: float32 [64, 7], P('img'), may hold values from -0.5 to 0.5
- camera_moment: float32 [64, 7], P('img'), may hold values from -8 to 8
- camera_second: float32 [64, 7], P('img'), may hold values from 1 to 100
- pair_poses: float32 [96, 7], P('img'), may hold values from -0.5 to 0.5
- pair_moment: float32 [96, 7], P('img'), may hold values from -8 to 8
- pair_second: float32 [96, 7], P('img'), may hold values from 1 to 100
- pointmaps: bfloat16 [96, 2, 3, 147456], P('img', None, None, 'rep'), may hold values from -6 to 6
- confidence: bfloat16 [96, 2, 147456], P('img', None, 'rep'), may hold values from 1 to 10
Outputs:
- new_depths: float32 [64, 147456], P('img', 'rep')
- new_depth_moment: float32 [64, 147456], P('img', 'rep')
- new_depth_second: float32 [64, 147456], P('img', 'rep')
- new_cameras: float32 [64, 7], P('img')
- new_camera_moment: float32 [64, 7], P('img')
- new_camera_second: float32 [64, 7], P('img')
- new_pair_poses: float32 [96, 7], P('img')
- new_pair_moment: float32 [96, 7], P('img')
- new_pair_second: float32 [96, 7], P('img')
The draws below stay inside these ranges and needn't reach their ends.
Inputs may be any that keep to these rules, and one draw needn't show every extreme that they name: `pair_images`: the two images of a pair differ. Counting both views, the pairs stored on one index of img name the images of any one index of img (images k * 8 to k * 8 + 7) at most 4 times; one index of img, the same for all, is named exactly 4 times by the pairs of every index.
All inputs are finite; a program needn't handle non-finite values.
Results may differ from the reference program's by a relative error of at most 0.0003.
Values may be sent and summed in bfloat16 or wider, within the bound.
No kernel may reach another device: no remote copies, remote signals or barrier semaphores. Data moves between devices by JAX's collectives and lax.ppermute only.
A program may use at most 128 MiB of HBM per device.

```python
import math
import jax
import jax.numpy as jnp
from jax import lax

HEIGHT = 288
WIDTH = 512
IMG_DEV = 8
PAIR_DEV = 12
ITERS = 1
START = 50
NPIX = 147456
CAP = 4
IMAGES = 64
PAIRS = 96
N_IMG = 8


def draw_pair_images(key, part):
    key = jax.random.fold_in(key, 11)
    key_hub, key_pick, key_first, key_other, key_shift = jax.random.split(key, 5)
    hub_owner = jax.random.randint(key_hub, (), 0, N_IMG)
    slot_owner = jnp.arange(N_IMG * CAP, dtype=jnp.int32) // CAP
    slot_copy = jnp.arange(N_IMG * CAP, dtype=jnp.int32) % CAP

    def one_device(device_key):
        key_order, key_shuffle = jax.random.split(device_key)
        priority = jax.random.permutation(key_order, N_IMG * CAP).astype(jnp.int32)
        priority = jnp.where(slot_owner == hub_owner, -1 - slot_copy, priority)
        ordering = jnp.argsort(priority, stable=True)
        chosen = slot_owner[ordering[:2 * PAIR_DEV]]
        return jax.random.permutation(key_shuffle, chosen)
    owners = jax.vmap(one_device)(jax.random.split(key_pick, N_IMG)).reshape(N_IMG * PAIR_DEV, 2)
    first_local = jax.random.randint(key_first, (N_IMG * PAIR_DEV,), 0, IMG_DEV)
    other_local = jax.random.randint(key_other, (N_IMG * PAIR_DEV,), 0, IMG_DEV)
    shift_local = jax.random.randint(key_shift, (N_IMG * PAIR_DEV,), 1, IMG_DEV)
    second_local = jnp.where(owners[:, 1] == owners[:, 0], (first_local + shift_local) % IMG_DEV, other_local)
    locals_both = jnp.stack([first_local, second_local], axis=1)
    return (owners * IMG_DEV + locals_both).astype(jnp.int32)


def block_levels(rng, shape, pieces, least, high):
    level = 1.0
    for position, blocks in pieces:
        draws = jax.random.uniform(jax.random.fold_in(jax.random.fold_in(rng, 6), position), (blocks,), jnp.float32, least / len(pieces), high / len(pieces))
        level = level * jnp.repeat(jnp.exp(draws), shape[position] // blocks).reshape((-1,) + (1,) * (len(shape) - 1 - position))
    return level


def bell_draw(own_key, dims, scale, bound, pieces=(), held_as=jnp.bfloat16):
    values = jax.random.normal(own_key, dims, jnp.float32) * scale
    if len(pieces) > 0:
        values = block_levels(own_key, dims, pieces, -0.22, 0.18) * values
    return jnp.clip(values, min=-bound, max=bound).astype(held_as)


def setup_inputs(seed: int = 0) -> dict:
    seeds = jax.random.split(jax.random.key(seed), 13)
    return {
        "pair_images": draw_pair_images(jax.random.fold_in(seeds[12], 71), 0),
        "depths": jnp.clip(jnp.exp(math.log(4.0) - 2.0794415 * jax.random.uniform(seeds[1], (IMAGES, NPIX), jnp.float32) ** block_levels(seeds[1], (IMAGES, NPIX), ((0, 8), (1, 4)), -0.2, 0.2)), 0.5, 4.0),
        "depth_moment": bell_draw(seeds[2], (IMAGES, NPIX), 2.0, 8.0, ((0, 8), (1, 4)), jnp.float32),
        "depth_second": jnp.clip(jnp.exp(math.log(100.0) - 4.6051702 * jax.random.uniform(seeds[3], (IMAGES, NPIX), jnp.float32) ** block_levels(seeds[3], (IMAGES, NPIX), ((0, 8), (1, 4)), -0.2, 0.2)), 1.0, 100.0),
        "cameras": jnp.clip(jax.random.uniform(seeds[4], (IMAGES, 7), jnp.float32, -0.5, 0.5) * block_levels(seeds[4], (IMAGES, 7), ((0, 8),), -0.4, 0.0), -0.5, 0.5),
        "camera_moment": bell_draw(seeds[5], (IMAGES, 7), 2.0, 8.0, ((0, 8),), jnp.float32),
        "camera_second": jnp.clip(jnp.exp(math.log(100.0) - 4.6051702 * jax.random.uniform(seeds[6], (IMAGES, 7), jnp.float32) ** block_levels(seeds[6], (IMAGES, 7), ((0, 8),), -0.2, 0.2)), 1.0, 100.0),
        "pair_poses": jnp.clip(jax.random.uniform(seeds[7], (PAIRS, 7), jnp.float32, -0.5, 0.5) * block_levels(seeds[7], (PAIRS, 7), ((0, 8),), -0.4, 0.0), -0.5, 0.5),
        "pair_moment": bell_draw(seeds[8], (PAIRS, 7), 2.0, 8.0, ((0, 8),), jnp.float32),
        "pair_second": jnp.clip(jnp.exp(math.log(100.0) - 4.6051702 * jax.random.uniform(seeds[9], (PAIRS, 7), jnp.float32) ** block_levels(seeds[9], (PAIRS, 7), ((0, 8),), -0.2, 0.2)), 1.0, 100.0),
        "pointmaps": bell_draw(seeds[10], (PAIRS, 2, 3, NPIX), 1.0, 6.0, ((0, 8), (3, 4))),
        "confidence": jnp.clip(jnp.exp(math.log(10.0) - 2.3025851 * jax.random.uniform(seeds[11], (PAIRS, 2, NPIX), jnp.float32) ** block_levels(seeds[11], (PAIRS, 2, NPIX), ((0, 8), (2, 4)), -0.2, 0.2)), 1.0, 10.0).astype(jnp.bfloat16),
    }


beta_one = 0.9
beta_two = 0.999
adam_eps = 1e-08
depth_rate = 0.05
camera_rate = 0.01
pose_rate = 0.01

def rotation(first, middle, last):
    inverse = 1.0 / (1.0 + first * first + middle * middle + last * last)
    return ((1.0 + first * first - middle * middle - last * last) * inverse, 2.0 * (first * middle - last) * inverse, 2.0 * (first * last + middle) * inverse, 2.0 * (first * middle + last) * inverse, (1.0 - first * first + middle * middle - last * last) * inverse, 2.0 * (middle * last - first) * inverse, 2.0 * (first * last - middle) * inverse, 2.0 * (middle * last + first) * inverse, (1.0 - first * first - middle * middle + last * last) * inverse)

def view_loss(depth_rows, camera_rows, pose_rows, points, weights, pixel_rows, pixel_cols):
    focals = WIDTH * jnp.exp(camera_rows[:, 0:1])
    ray_x = (pixel_cols[None, :] - 0.5 * WIDTH) / focals
    ray_y = (pixel_rows[None, :] - 0.5 * HEIGHT) / focals
    cam_rot = rotation(camera_rows[:, 1:2], camera_rows[:, 2:3], camera_rows[:, 3:4])
    pose_rot = rotation(pose_rows[:, 0:1], pose_rows[:, 1:2], pose_rows[:, 2:3])
    scales = jnp.exp(pose_rows[:, 6:7])
    point_x = points[:, 0].astype(jnp.float32)
    point_y = points[:, 1].astype(jnp.float32)
    point_z = points[:, 2].astype(jnp.float32)
    squared = jnp.zeros_like(depth_rows)
    for k in range(3):
        world_pts = depth_rows * (cam_rot[3 * k] * ray_x + cam_rot[3 * k + 1] * ray_y + cam_rot[3 * k + 2]) + camera_rows[:, 4 + k:5 + k]
        target = scales * (pose_rot[3 * k] * point_x + pose_rot[3 * k + 1] * point_y + pose_rot[3 * k + 2] * point_z) + pose_rows[:, 3 + k:4 + k]
        offset = world_pts - target
        squared = squared + offset * offset
    return 0.5 * jnp.sum(weights.astype(jnp.float32) * squared)

def adam_step(values, moment, second, gradient, step_rate, step_count):
    moment = beta_one * moment + (1.0 - beta_one) * gradient
    second = beta_two * second + (1.0 - beta_two) * gradient * gradient
    fix_one = 1.0 - beta_one ** step_count
    fix_two = 1.0 - beta_two ** step_count
    values = values - step_rate * (moment / fix_one) / (jnp.sqrt(second / fix_two) + adam_eps)
    return (values, moment, second)

def reference(pair_images, depths, depth_moment, depth_second, cameras, camera_moment, camera_second, pair_poses, pair_moment, pair_second, pointmaps, confidence):
    pixel = jnp.arange(NPIX, dtype=jnp.int32)
    pixel_rows = (pixel // WIDTH).astype(jnp.float32) + 0.5
    pixel_cols = (pixel % WIDTH).astype(jnp.float32) + 0.5
    for step in range(ITERS):

        def visit(carry, inputs):
            depth_grad, camera_grad = carry
            images, posed, points, weights = inputs
            chosen = depths[images]
            views = cameras[images]
            both = jnp.broadcast_to(posed[None, :], (2, 7))
            loss, pullback = jax.vjp(lambda a, b, c: view_loss(a, b, c, points, weights, pixel_rows, pixel_cols), chosen, views, both)
            grad_depth, grad_camera, grad_pose = pullback(jnp.ones_like(loss))
            depth_grad = depth_grad.at[images].add(grad_depth)
            camera_grad = camera_grad.at[images].add(grad_camera)
            return ((depth_grad, camera_grad), lax.optimization_barrier(jnp.sum(grad_pose, axis=0)))
        start = (jnp.zeros_like(depths), jnp.zeros_like(cameras))
        (depth_grad, camera_grad), pose_grad = lax.scan(visit, start, (pair_images, pair_poses, pointmaps, confidence))
        camera_grad = camera_grad / NPIX
        pose_grad = pose_grad / NPIX
        step_count = START + step + 1
        depths, depth_moment, depth_second = adam_step(depths, depth_moment, depth_second, depth_grad, depth_rate, step_count)
        cameras, camera_moment, camera_second = adam_step(cameras, camera_moment, camera_second, camera_grad, camera_rate, step_count)
        pair_poses, pair_moment, pair_second = adam_step(pair_poses, pair_moment, pair_second, pose_grad, pose_rate, step_count)
    return (depths, depth_moment, depth_second, cameras, camera_moment, camera_second, pair_poses, pair_moment, pair_second)
```

```python
import functools
import math

import jax
import jax.numpy as jnp
from jax import lax
from jax.experimental import pallas as pl
from jax.experimental.pallas import tpu as pltpu
from jax.sharding import PartitionSpec as P

HEIGHT = 288
WIDTH = 512
START = 50
NPIX = 147456
LANES = 128
CHUNKS = 1

beta_one = 0.9
beta_two = 0.999
adam_eps = 1e-08
depth_rate = 0.05
camera_rate = 0.01
pose_rate = 0.01

DEPTH_MID = 2.25
DEPTH_STEP = 1.75 / 32766.0
VIEW_BOUND = 340.0
CODE_UNIT = 8.0
INTS = jnp.int16
SUMS = 11
COEFS = 16

SMEM = pl.BlockSpec(memory_space=pltpu.SMEM)
VMEM = pl.BlockSpec(memory_space=pltpu.VMEM)
PARAMS = pltpu.CompilerParams(vmem_limit_bytes=40 * 1024 * 1024)


def code_scale(bound):
    return 32766.0 / math.log2(1.0 + bound / CODE_UNIT)


def encode(magnitude, negative, bound):
    steps = (jnp.log2(1.0 + magnitude) * code_scale(bound) + 0.5).astype(jnp.int32)
    steps = jnp.minimum(steps, 32767)
    return jnp.where(negative, -steps, steps).astype(INTS)


def decode(code, bound):
    steps = code.astype(jnp.int32)
    size = jnp.abs(steps).astype(jnp.float32) * (1.0 / code_scale(bound))
    value = CODE_UNIT * jnp.exp2(size) - CODE_UNIT
    return jnp.where(steps < 0, -value, value)


def table_kernel(half, cap, images, me_ref, list_ref, tab_ref, count_ref):
    me = me_ref[0]
    shards = 2 * half
    requests = list_ref.shape[1]
    asked = shards * cap

    @pl.loop(0, 2 * asked)
    def _(i):
        tab_ref[i] = -1

    @pl.loop(0, 2 * shards)
    def _(i):
        count_ref[i] = 0

    def put(cell, base, value):
        rank = count_ref[cell]
        tab_ref[base + jnp.minimum(rank, cap - 1)] = value
        count_ref[cell] = rank + 1

    @pl.loop(0, half)
    def _(k):
        @pl.loop(0, requests)
        def _(r):
            image = list_ref[k, r]
            owner = lax.div(image, images)

            @pl.when(owner == me)
            def _():
                put(k, k * cap, image - owner * images)

            @pl.when(owner == (me ^ half))
            def _():
                put(half + k, (half + k) * cap, image - owner * images)

    @pl.loop(0, requests)
    def _(r):
        relative = lax.div(list_ref[0, r], images) ^ me
        put(shards + relative, asked + relative * cap, r)


def slot_tables(me, listing, half, cap, images):
    return pl.pallas_call(
        functools.partial(table_kernel, half, cap, images),
        out_shape=jax.ShapeDtypeStruct((4 * half * cap,), jnp.int32),
        in_specs=[SMEM, SMEM],
        out_specs=SMEM,
        scratch_shapes=[pltpu.SMEM((4 * half,), jnp.int32)],
        name="slot_tables",
    )(me, listing)


def pack_kernel(first, cap, tab_ref, src_ref, *out_refs):
    for k, out_ref in enumerate(out_refs):

        @pl.loop(0, cap)
        def _(c):
            image = jnp.maximum(tab_ref[first + k * cap + c], 0)
            out_ref[c] = src_ref[image]


def pack_slots(table, maps, first, half, cap):
    rows = maps.shape[1]
    return pl.pallas_call(
        functools.partial(pack_kernel, first, cap),
        out_shape=[jax.ShapeDtypeStruct((cap, rows, LANES), INTS)] * half,
        in_specs=[SMEM, VMEM],
        out_specs=[VMEM] * half,
        compiler_params=PARAMS,
        name="pack_slots",
    )(table, maps)


def part_kernel(point_ref, weight_ref, out_ref, wide):
    rows = point_ref.shape[2]
    for q in range(4):
        source = point_ref.at[0, q] if q < 3 else weight_ref.at[0]
        wide[q] = source[...].astype(jnp.float32)
    for q in range(4):
        for v in range(2):
            for t in range(0, rows // 2, 16):
                out_ref[v, q, t : t + 16] = wide[q, pl.ds(2 * t + v, 16, stride=2), :].astype(
                    jnp.bfloat16
                )


def part_views(points, weights):
    pairs, _, _, pixels = points.shape
    rows = pixels // LANES
    points = (
        points.transpose(0, 2, 1, 3)
        .reshape(pairs, 3, 2, rows, LANES)
        .transpose(0, 1, 3, 2, 4)
        .reshape(pairs, 3, 2 * rows, LANES)
    )
    weights = (
        weights.reshape(pairs, 2, rows, LANES).transpose(0, 2, 1, 3).reshape(pairs, 2 * rows, LANES)
    )
    return pl.pallas_call(
        part_kernel,
        grid=(pairs,),
        out_shape=jax.ShapeDtypeStruct((2 * pairs, 4, rows, LANES), jnp.bfloat16),
        in_specs=[
            pl.BlockSpec((1, 3, 2 * rows, LANES), lambda e: (e, 0, 0, 0)),
            pl.BlockSpec((1, 2 * rows, LANES), lambda e: (e, 0, 0)),
        ],
        out_specs=pl.BlockSpec((2, 4, rows, LANES), lambda e: (e, 0, 0, 0)),
        scratch_shapes=[pltpu.VMEM((4, 2 * rows, LANES), jnp.float32)],
        compiler_params=PARAMS,
        name="part_views",
    )(points, weights)


def view_kernel(first, half, cap, start, tab_ref, coef_ref, row_ref, view_ref, *refs):
    depth_refs, grad_refs = refs[:half], refs[half : 2 * half]
    sum_ref, depth_all, grad_all = refs[2 * half :]
    rows = depth_all.shape[1]
    for k in range(half):
        depth_all[k * cap : (k + 1) * cap] = depth_refs[k][...]
    sum_ref[...] = jnp.zeros_like(sum_ref)
    across = WIDTH // LANES
    line = lax.broadcasted_iota(jnp.int32, (16, LANES), 0)
    lane = lax.broadcasted_iota(jnp.int32, (16, LANES), 1)
    columns = ((line % across) * LANES + lane).astype(jnp.float32) + (0.5 - 0.5 * WIDTH)
    lines = (line // across).astype(jnp.float32) + row_ref[0]

    @pl.loop(0, half * cap)
    def _(s):
        view = tab_ref[first + s]

        @pl.when(view >= 0)
        def _():
            def coef(i):
                return coef_ref[view, i]

            step = [coef(3 + j) * (16.0 / across) for j in range(3)]
            ray = [columns * coef(j) + (lines * coef(3 + j) + coef(6 + j)) for j in range(3)]
            shift = [coef(9 + j) for j in range(3)]
            gain = coef(12)
            totals = [None] * SUMS

            def add(i, value):
                value = value[:8] + value[8:]
                totals[i] = value if totals[i] is None else totals[i] + value

            for t in range(0, rows, 16):
                here = slice(start + t, start + t + 16)
                point = [view_ref[view, j, here].astype(jnp.float32) for j in range(3)]
                weight = view_ref[view, 3, here].astype(jnp.float32)
                depth = (
                    depth_all[s, t : t + 16].astype(jnp.int32).astype(jnp.float32) * DEPTH_STEP
                    + DEPTH_MID
                )
                pull = [weight * (depth * ray[j] + (shift[j] - point[j])) for j in range(3)]
                along = pull[0] * ray[0] + pull[1] * ray[1] + pull[2] * ray[2]
                grad_all[s, t : t + 16] = encode(
                    jnp.abs(along) * gain, along < 0.0, VIEW_BOUND
                )
                for j in range(3):
                    add(j, pull[j])
                    add(8 + j, depth * pull[j])
                    a, b = (j + 1) % 3, (j + 2) % 3
                    add(3 + j, point[a] * pull[b] - point[b] * pull[a])
                add(6, point[0] * pull[0] + point[1] * pull[1] + point[2] * pull[2])
                add(7, depth * along)
                ray = [ray[j] + step[j] for j in range(3)]
            for i in range(SUMS):
                sum_ref[view, i : i + 1] = jnp.sum(totals[i], axis=0, keepdims=True)

    for k in range(half):
        grad_refs[k][...] = grad_all[k * cap : (k + 1) * cap]


def view_terms(table, coefs, row, views, depths, first, start, half, cap):
    rows = depths[0].shape[1]
    out = pl.pallas_call(
        functools.partial(view_kernel, first, half, cap, start),
        out_shape=[jax.ShapeDtypeStruct((cap, rows, LANES), INTS)] * half
        + [jax.ShapeDtypeStruct((views.shape[0], COEFS, LANES), jnp.float32)],
        in_specs=[SMEM, SMEM, SMEM] + [VMEM] * (half + 1),
        out_specs=[VMEM] * (half + 1),
        scratch_shapes=[
            pltpu.VMEM((half * cap, rows, LANES), INTS),
            pltpu.VMEM((half * cap, rows, LANES), INTS),
        ],
        compiler_params=PARAMS,
        name="view_terms",
    )(table, coefs, row, views, *depths)
    return out[:half], out[half]


def fold(first, cap, tab_ref, slot_refs, total_ref):
    total_ref[...] = jnp.zeros_like(total_ref)
    for k, slot_ref in enumerate(slot_refs):

        @pl.loop(0, cap)
        def _(c):
            image = tab_ref[first + k * cap + c]

            @pl.when(image >= 0)
            def _():
                total_ref[image] += decode(slot_ref[c], VIEW_BOUND)


def fold_kernel(first, cap, bound, tab_ref, *refs):
    slot_refs, out_ref, total = refs[:-2], refs[-2], refs[-1]
    fold(first, cap, tab_ref, slot_refs, total)

    @pl.loop(0, total.shape[0])
    def _(i):
        value = total[i]
        out_ref[i] = encode(jnp.abs(value) * (1.0 / CODE_UNIT), value < 0.0, bound)


def fold_slots(table, slots, first, images, cap, bound):
    rows = slots[0].shape[1]
    return pl.pallas_call(
        functools.partial(fold_kernel, first, cap, bound),
        out_shape=jax.ShapeDtypeStruct((images, rows, LANES), INTS),
        in_specs=[SMEM] + [VMEM] * len(slots),
        out_specs=VMEM,
        scratch_shapes=[pltpu.VMEM((images, rows, LANES), jnp.float32)],
        compiler_params=PARAMS,
        name="fold_slots",
    )(table, *slots)


def local_kernel(first, cap, tab_ref, *refs):
    fold(first, cap, tab_ref, refs[:-1], refs[-1])


def fold_local(table, slots, first, images, cap):
    rows = slots[0].shape[1]
    return pl.pallas_call(
        functools.partial(local_kernel, first, cap),
        out_shape=jax.ShapeDtypeStruct((images, rows, LANES), jnp.float32),
        in_specs=[SMEM] + [VMEM] * len(slots),
        out_specs=VMEM,
        compiler_params=PARAMS,
        name="fold_local",
    )(table, *slots)


def adam_step(values, moment, second, gradient, step_rate):
    step_count = START + 1
    moment = beta_one * moment + (1.0 - beta_one) * gradient
    second = beta_two * second + (1.0 - beta_two) * gradient * gradient
    fix_one = 1.0 - beta_one**step_count
    fix_two = 1.0 - beta_two**step_count
    values = values - step_rate * (moment / fix_one) / (jnp.sqrt(second / fix_two) + adam_eps)
    return (values, moment, second)


def depth_kernel(bound, local_ref, far_ref, x_ref, m_ref, s_ref, nx_ref, nm_ref, ns_ref, grad):
    images, rows, _ = local_ref.shape
    for i in range(images):
        grad[i * rows : (i + 1) * rows] = local_ref[i] + decode(far_ref[i], bound)
    for t in range(rows):
        here = slice(t * LANES, (t + 1) * LANES)
        gradient = grad[pl.ds(t, images, stride=rows), :]
        nx_ref[:, here], nm_ref[:, here], ns_ref[:, here] = adam_step(
            x_ref[:, here], m_ref[:, here], s_ref[:, here], gradient, depth_rate
        )


def update_depths(local, far, values, moment, second, bound):
    images, rows, _ = local.shape
    block = 48
    wide = pl.BlockSpec((images, block * LANES), lambda t: (0, t))
    tall = pl.BlockSpec((images, block, LANES), lambda t: (0, t, 0))
    return pl.pallas_call(
        functools.partial(depth_kernel, bound),
        grid=(rows // block,),
        out_shape=[jax.ShapeDtypeStruct(values.shape, jnp.float32)] * 3,
        in_specs=[tall, tall, wide, wide, wide],
        out_specs=[wide, wide, wide],
        scratch_shapes=[pltpu.VMEM((images * block, LANES), jnp.float32)],
        compiler_params=PARAMS,
        name="update_depths",
    )(local, far, values, moment, second)


def rotation(first, middle, last):
    inverse = 1.0 / (1.0 + first * first + middle * middle + last * last)
    return (
        (1.0 + first * first - middle * middle - last * last) * inverse,
        2.0 * (first * middle - last) * inverse,
        2.0 * (first * last + middle) * inverse,
        2.0 * (first * middle + last) * inverse,
        (1.0 - first * first + middle * middle - last * last) * inverse,
        2.0 * (middle * last - first) * inverse,
        2.0 * (first * last - middle) * inverse,
        2.0 * (middle * last + first) * inverse,
        (1.0 - first * first - middle * middle + last * last) * inverse,
    )


def cross(a, b):
    return [a[(j + 1) % 3] * b[(j + 2) % 3] - a[(j + 2) % 3] * b[(j + 1) % 3] for j in range(3)]


def turn_gradient(spin, torque):
    factor = 2.0 / (1.0 + spin[0] * spin[0] + spin[1] * spin[1] + spin[2] * spin[2])
    swing = cross(spin, torque)
    return [factor * (torque[j] + swing[j]) for j in range(3)]


def view_coefs(cams, poses):
    inverse_focal = jnp.exp(-cams[0]) * (1.0 / WIDTH)
    cam = rotation(cams[1], cams[2], cams[3])
    pose = rotation(poses[0], poses[1], poses[2])
    scale = jnp.exp(poses[6])
    back = jnp.exp(-poses[6])
    gap = [cams[4 + k] - poses[3 + k] for k in range(3)]
    both = [
        [sum(pose[3 * k + j] * cam[3 * k + i] for k in range(3)) for i in range(3)] for j in range(3)
    ]
    matrix = [[both[j][i] * back for i in range(3)] for j in range(3)]
    shift = [sum(pose[3 * k + j] * gap[k] for k in range(3)) * back for j in range(3)]
    rows = [matrix[j][0] * inverse_focal for j in range(3)]
    rows += [matrix[j][1] * inverse_focal for j in range(3)]
    rows += [matrix[j][2] for j in range(3)]
    rows += shift
    rows += [scale * scale * (1.0 / CODE_UNIT)]
    rows += [jnp.zeros_like(scale)] * (COEFS - len(rows))
    return jnp.stack(rows, axis=1), (both, pose, scale, matrix, shift)


def view_gradients(sums, cams, poses, parts):
    both, pose, scale, matrix, shift = parts
    square = scale * scale
    force, torque, stretch, drawn, lever = sums[0:3], sums[3:6], sums[6], sums[7], sums[8:11]
    push = [scale * sum(pose[3 * k + j] * force[j] for j in range(3)) for k in range(3)]
    swing = cross(shift, force)
    arm = [torque[j] - swing[j] for j in range(3)]
    camera_torque = [square * sum(both[j][i] * arm[j] for j in range(3)) for i in range(3)]
    pose_torque = [-square * torque[j] for j in range(3)]
    focal = -square * (drawn - sum(matrix[j][2] * lever[j] for j in range(3)))
    camera = [focal] + turn_gradient([cams[1], cams[2], cams[3]], camera_torque) + push
    posed = (
        turn_gradient([poses[0], poses[1], poses[2]], pose_torque)
        + [-value for value in push]
        + [-square * stretch]
    )
    return jnp.stack(camera, axis=1), jnp.stack(posed, axis=1)


def body(
    pair_images,
    depths,
    depth_moment,
    depth_second,
    cameras,
    camera_moment,
    camera_second,
    pair_poses,
    pair_moment,
    pair_second,
    pointmaps,
    confidence,
):
    shards = lax.axis_size("img")
    half = shards // 2
    me = lax.axis_index("img")
    rep = lax.axis_index("rep")
    images, row_len = depths.shape
    pairs = pair_images.shape[0]
    requests = 2 * pairs
    cap = max(2, 3 * pairs // shards)
    rows = row_len // LANES
    size = rows // CHUNKS
    far_bound = VIEW_BOUND * half * cap

    def swap(value, k):
        return lax.ppermute(value, "img", [(i, i ^ k) for i in range(shards)])

    listing = pair_images.reshape(1, requests)
    codes = jnp.round((depths - DEPTH_MID) * (1.0 / DEPTH_STEP)).astype(INTS)
    codes = codes.reshape(images, rows, LANES)
    near = [codes[:, c * size : (c + 1) * size] for c in range(CHUNKS)]
    far = [swap(near[c], half) for c in range(CHUNKS)]
    lists = jnp.concatenate([listing] + [swap(listing, k) for k in range(1, half)], axis=0)
    table = slot_tables(me.reshape(1), lists, half, cap, images)

    all_cameras = lax.all_gather(cameras, "img", axis=0, tiled=True)
    cams = jnp.take(all_cameras, pair_images.reshape(requests), axis=0).T
    poses = jnp.repeat(pair_poses.T, 2, axis=1)
    coefs, parts = view_coefs(cams, poses)
    views = part_views(pointmaps, confidence)

    slots = half * cap

    def exchange(values):
        return [values[0]] + [swap(values[k], k) for k in range(1, half)]

    sums = 0.0
    far_codes, near_totals = [], []
    for h in (0, 1):
        for c in range(CHUNKS):
            start = c * size
            row = rep * (row_len // WIDTH) + start // (WIDTH // LANES)
            row = (row.astype(jnp.float32) + (0.5 - 0.5 * HEIGHT)).reshape(1)
            asked = exchange(pack_slots(table, (near, far)[h][c], h * slots, half, cap))
            grads, moments = view_terms(
                table, coefs, row, views, asked, (2 + h) * slots, start, half, cap
            )
            sums = sums + jnp.sum(moments, axis=2)
            back = exchange(grads)
            if h == 1:
                folded = fold_slots(table, back, slots, images, cap, far_bound)
                far_codes.append(swap(folded, half))
            else:
                near_totals.append(fold_local(table, back, 0, images, cap))
    near_total = jnp.concatenate(near_totals, axis=1)
    far_code = jnp.concatenate(far_codes, axis=1)
    depths, depth_moment, depth_second = update_depths(
        near_total, far_code, depths, depth_moment, depth_second, far_bound
    )

    camera_terms, pose_terms = view_gradients(list(sums.T[:SUMS]), cams, poses, parts)
    chosen = (
        pair_images.reshape(1, requests) == jnp.arange(shards * images, dtype=jnp.int32)[:, None]
    )
    camera_parts = jnp.sum(jnp.where(chosen[:, :, None], camera_terms[None], 0.0), axis=1)
    camera_parts = lax.all_to_all(
        camera_parts.reshape(shards, images, 7), "img", split_axis=0, concat_axis=0, tiled=True
    )
    camera_grad = jnp.sum(camera_parts, axis=0)
    pose_grad = jnp.sum(pose_terms.reshape(pairs, 2, 7), axis=1)
    camera_grad, pose_grad = lax.psum((camera_grad, pose_grad), "rep")
    camera_grad = camera_grad / NPIX
    pose_grad = pose_grad / NPIX
    cameras, camera_moment, camera_second = adam_step(
        cameras, camera_moment, camera_second, camera_grad, camera_rate
    )
    pair_poses, pair_moment, pair_second = adam_step(
        pair_poses, pair_moment, pair_second, pose_grad, pose_rate
    )
    return (
        depths,
        depth_moment,
        depth_second,
        cameras,
        camera_moment,
        camera_second,
        pair_poses,
        pair_moment,
        pair_second,
    )


def solution(mesh):
    return jax.shard_map(
        body,
        mesh=mesh,
        in_specs=(
            P("img", None),
            P("img", "rep"),
            P("img", "rep"),
            P("img", "rep"),
            P("img", None),
            P("img", None),
            P("img", None),
            P("img", None),
            P("img", None),
            P("img", None),
            P("img", None, None, "rep"),
            P("img", None, "rep"),
        ),
        out_specs=(
            P("img", "rep"),
            P("img", "rep"),
            P("img", "rep"),
            P("img", None),
            P("img", None),
            P("img", None),
            P("img", None),
            P("img", None),
            P("img", None),
        ),
        check_vma=False,
    )
```

```python
import functools
import math

import jax
import jax.numpy as jnp
from jax import lax
from jax.experimental import pallas as pl
from jax.experimental.pallas import tpu as pltpu
from jax.sharding import PartitionSpec as P

HEIGHT = 288
WIDTH = 512
START = 50
NPIX = 147456
LANES = 128
SWAP_PARTS = 2

beta_one = 0.9
beta_two = 0.999
adam_eps = 1e-08
depth_rate = 0.05
camera_rate = 0.01
pose_rate = 0.01

DEPTH_MID = 2.25
DEPTH_STEP = 1.75 / 32766.0
VIEW_BOUND = 340.0
CODE_UNIT = 8.0
INTS = jnp.int16
SUMS = 11
COEFS = 16

SMEM = pl.BlockSpec(memory_space=pltpu.SMEM)
VMEM = pl.BlockSpec(memory_space=pltpu.VMEM)
COST = pl.CostEstimate(flops=1, bytes_accessed=1, transcendentals=0)
PARAMS = pltpu.CompilerParams(vmem_limit_bytes=32 * 1024 * 1024)


def code_scale(bound):
    return 32766.0 / math.log2(1.0 + bound / CODE_UNIT)


def encode(magnitude, negative, bound):
    steps = (jnp.log2(1.0 + magnitude) * code_scale(bound) + 0.5).astype(jnp.int32)
    steps = jnp.minimum(steps, 32767)
    return jnp.where(negative, -steps, steps).astype(INTS)


def decode(code, bound):
    steps = code.astype(jnp.int32)
    size = jnp.abs(steps).astype(jnp.float32) * (1.0 / code_scale(bound))
    value = CODE_UNIT * jnp.exp2(size) - CODE_UNIT
    return jnp.where(steps < 0, -value, value)


def letter_kernel(image_ref, camera_ref, out_ref):
    shards, rows, _ = out_ref.shape
    lane = lax.broadcasted_iota(jnp.int32, (1, LANES), 1)
    names = jnp.zeros((1, LANES), jnp.int32)
    for r in range(2 * image_ref.shape[1]):
        names = jnp.where(lane == r, image_ref[r % 2, r // 2], names)
    for i in range(shards):
        out_ref[i, 0 : rows - 1, 0:7] = camera_ref[...]
        out_ref[i, rows - 1 : rows] = names.astype(jnp.float32)


def letters_of(pair_images, cameras, shards):
    images = cameras.shape[0]
    return pl.pallas_call(
        letter_kernel,
        out_shape=jax.ShapeDtypeStruct((shards, images + 1, LANES), jnp.float32),
        in_specs=[SMEM, VMEM],
        out_specs=VMEM,
        cost_estimate=COST,
        name="letters_of",
    )(pair_images, cameras)


def over(number, size):
    if size & (size - 1):
        return lax.div(number, size)
    return lax.shift_right_logical(number, size.bit_length() - 1)


def table_kernel(half, cap, images, me_ref, *refs):
    list_ref, tab_ref, count_ref = refs
    me = me_ref[0]
    shards = 2 * half
    asked = shards * cap
    requests = list_ref.shape[1]

    @pl.loop(0, 2 * asked, unroll=8)
    def _(i):
        tab_ref[i] = -1

    tab_ref[2 * asked] = me & (half - 1)

    @pl.loop(0, 2 * shards, unroll=8)
    def _(i):
        count_ref[i] = 0

    def put(cell, value):
        rank = count_ref[cell]
        tab_ref[cell * cap + jnp.minimum(rank, cap - 1)] = value
        count_ref[cell] = rank + 1

    for k in range(half):
        asker = me ^ k

        @pl.loop(0, requests, unroll=2)
        def _(r):
            image = list_ref[asker, r]
            owner = over(image, images)
            mine = owner == me

            @pl.when(mine | (owner == (me ^ half)))
            def _():
                put(jnp.where(mine, k, half + k), image - owner * images)

    @pl.loop(0, requests, unroll=2)
    def _(r):
        image = list_ref[me, r]
        owner = over(image, images)
        put(shards + (owner ^ me), r)


def slot_tables(me, lists, half, cap, images):
    return pl.pallas_call(
        functools.partial(table_kernel, half, cap, images),
        out_shape=jax.ShapeDtypeStruct((4 * half * cap + 1,), jnp.int32),
        in_specs=[SMEM, SMEM],
        out_specs=SMEM,
        scratch_shapes=[pltpu.SMEM((4 * half,), jnp.int32)],
        cost_estimate=COST,
        name="slot_tables",
    )(me, lists)


def pack_kernel(first, half, tab_ref, *refs):
    map_refs, slot_refs = refs[:-half], refs[-half:]
    rows = map_refs[0].shape[1]
    for k, slot_ref in enumerate(slot_refs):

        @pl.loop(0, slot_ref.shape[0])
        def _(c):
            image = jnp.maximum(tab_ref[first + k * slot_ref.shape[0] + c], 0)
            for i, map_ref in enumerate(map_refs):
                slot_ref[c, i * rows : (i + 1) * rows] = map_ref[image]


def pack_slots(table, maps, first, half, cap):
    rows = sum(part.shape[1] for part in maps)
    return pl.pallas_call(
        functools.partial(pack_kernel, first, half),
        out_shape=[jax.ShapeDtypeStruct((cap, rows, LANES), INTS)] * half,
        in_specs=[SMEM] + [VMEM] * len(maps),
        out_specs=[VMEM] * half,
        compiler_params=PARAMS,
        cost_estimate=COST,
        name="pack_slots",
    )(table, *maps)


def columns_and_lines(top):
    across = WIDTH // LANES
    line = lax.broadcasted_iota(jnp.int32, (16, LANES), 0)
    lane = lax.broadcasted_iota(jnp.int32, (16, LANES), 1)
    columns = ((line % across) * LANES + lane).astype(jnp.float32) + (0.5 - 0.5 * WIDTH)
    return columns, (line // across).astype(jnp.float32) + top


def ray_start(columns, lines, coef):
    ray = [columns * coef(j) + (lines * coef(3 + j) + coef(6 + j)) for j in range(3)]
    step = [coef(3 + j) * (16.0 * LANES / WIDTH) for j in range(3)]
    return ray, step


def prepare_kernel(row_ref, coef_ref, point_ref, weight_ref, view_ref, slope_ref, wide):
    rows = view_ref.shape[2]
    columns, lines = columns_and_lines(row_ref[0])

    @pl.loop(0, point_ref.shape[0])
    def _(pair):
        for q in range(4):
            source = point_ref.at[pair, q] if q < 3 else weight_ref.at[pair]
            wide[q] = source[...].astype(jnp.float32)
        for v in range(2):
            view = 2 * pair + v

            def coef(i):
                return coef_ref[view, i]

            ray, step = ray_start(columns, lines, coef)
            shift = [coef(9 + j) for j in range(3)]
            gain = coef(12)
            for t in range(0, rows, 16):
                here = slice(t, t + 16)
                part = [wide[q, pl.ds(2 * t + v, 16, stride=2), :] for q in range(4)]
                for q in range(4):
                    view_ref[view, q, here] = part[q].astype(jnp.bfloat16)
                weight = part[3] * gain
                slope = weight * (ray[0] * ray[0] + ray[1] * ray[1] + ray[2] * ray[2])
                rest = [ray[j] * (shift[j] - part[j]) for j in range(3)]
                slope_ref[view, 0, here] = slope * DEPTH_STEP
                slope_ref[view, 1, here] = slope * DEPTH_MID + weight * (
                    rest[0] + rest[1] + rest[2]
                )
                ray = [ray[j] + step[j] for j in range(3)]


def prepare_views(row, coefs, points, weights):
    pairs, _, _, pixels = points.shape
    rows = pixels // LANES
    points = (
        points.transpose(0, 2, 1, 3)
        .reshape(pairs, 3, 2, rows, LANES)
        .transpose(0, 1, 3, 2, 4)
        .reshape(pairs, 3, 2 * rows, LANES)
    )
    weights = (
        weights.reshape(pairs, 2, rows, LANES).transpose(0, 2, 1, 3).reshape(pairs, 2 * rows, LANES)
    )
    return pl.pallas_call(
        prepare_kernel,
        out_shape=[
            jax.ShapeDtypeStruct((2 * pairs, 4, rows, LANES), jnp.bfloat16),
            jax.ShapeDtypeStruct((2 * pairs, 2, rows, LANES), jnp.float32),
        ],
        in_specs=[SMEM, SMEM, VMEM, VMEM],
        out_specs=[VMEM, VMEM],
        scratch_shapes=[pltpu.VMEM((4, 2 * rows, LANES), jnp.float32)],
        compiler_params=PARAMS,
        cost_estimate=COST,
        name="prepare_views",
    )(row, coefs, points, weights)


def slots_at(refs, k, tab_ref):
    return refs[k] if len(refs) > 1 else refs[0].at[k ^ tab_ref[tab_ref.shape[0] - 1]]


def grad_kernel(first, half, cap, tab_ref, slope_ref, *refs):
    depth_refs, grad_refs = refs[:half], refs[half:]
    rows = depth_refs[0].shape[1]
    for k in range(half):
        depth_ref = depth_refs[k]
        grad_ref = slots_at(grad_refs, k, tab_ref)

        @pl.loop(0, cap)
        def _(c):
            view = tab_ref[first + k * cap + c]

            @pl.when(view >= 0)
            def _():
                for t in range(0, rows, 16):
                    here = slice(t, t + 16)
                    code = depth_ref[c, here].astype(jnp.int32).astype(jnp.float32)
                    along = code * slope_ref[view, 0, here] + slope_ref[view, 1, here]
                    grad_ref[c, here] = encode(jnp.abs(along), along < 0.0, VIEW_BOUND)


def depth_grads(table, slopes, depths, first, half, cap, by_rank):
    rows = depths[0].shape[1]
    if by_rank:
        out = [jax.ShapeDtypeStruct((half, cap, rows, LANES), INTS)]
    else:
        out = [jax.ShapeDtypeStruct((cap, rows, LANES), INTS)] * half
    return pl.pallas_call(
        functools.partial(grad_kernel, first, half, cap),
        out_shape=out,
        in_specs=[SMEM] + [VMEM] * (1 + half),
        out_specs=[VMEM] * len(out),
        compiler_params=PARAMS,
        cost_estimate=COST,
        name="depth_grads",
    )(table, slopes, *depths)


def sum_kernel(first, half, cap, tab_ref, coef_ref, row_ref, view_ref, *refs):
    depth_refs = refs[:-2]
    sum_ref, depth_all = refs[-2:]
    slots, rows, _ = depth_all.shape
    for k in range(half):
        depth_ref = depth_refs[k]
        depth_all[k * cap : (k + 1) * cap] = depth_ref[...]
    sum_ref[...] = jnp.zeros_like(sum_ref)
    columns, lines = columns_and_lines(row_ref[0])

    @pl.loop(0, slots)
    def _(s):
        view = tab_ref[first + s]

        @pl.when(view >= 0)
        def _():
            def coef(i):
                return coef_ref[view, i]

            ray, step = ray_start(columns, lines, coef)
            shift = [coef(9 + j) for j in range(3)]
            totals = [None] * SUMS

            def add(i, value):
                value = value[:8] + value[8:]
                totals[i] = value if totals[i] is None else totals[i] + value

            for t in range(0, rows, 16):
                here = slice(t, t + 16)
                point = [view_ref[view, j, here].astype(jnp.float32) for j in range(3)]
                weight = view_ref[view, 3, here].astype(jnp.float32)
                depth = (
                    depth_all[s, here].astype(jnp.int32).astype(jnp.float32) * DEPTH_STEP
                    + DEPTH_MID
                )
                pull = [weight * (depth * ray[j] + (shift[j] - point[j])) for j in range(3)]
                along = pull[0] * ray[0] + pull[1] * ray[1] + pull[2] * ray[2]
                for j in range(3):
                    add(j, pull[j])
                    add(8 + j, depth * pull[j])
                    a, b = (j + 1) % 3, (j + 2) % 3
                    add(3 + j, point[a] * pull[b] - point[b] * pull[a])
                add(6, point[0] * pull[0] + point[1] * pull[1] + point[2] * pull[2])
                add(7, depth * along)
                ray = [ray[j] + step[j] for j in range(3)]
            for i in range(SUMS):
                sum_ref[view, i : i + 1] = jnp.sum(totals[i], axis=0, keepdims=True)


def view_sums(table, coefs, row, views, depths, first, half, cap):
    rows = depths[0].shape[1]
    return pl.pallas_call(
        functools.partial(sum_kernel, first, half, cap),
        out_shape=jax.ShapeDtypeStruct((views.shape[0], COEFS, LANES), jnp.float32),
        in_specs=[SMEM, SMEM, SMEM] + [VMEM] * (1 + len(depths)),
        out_specs=VMEM,
        scratch_shapes=[pltpu.VMEM((half * cap, rows, LANES), INTS)],
        compiler_params=PARAMS,
        cost_estimate=COST,
        name="view_sums",
    )(table, coefs, row, views, *depths)


def fold(first, half, cap, tab_ref, slot_refs, total_ref):
    total_ref[...] = jnp.zeros_like(total_ref)
    for k in range(half):
        slot_ref = slots_at(slot_refs, k, tab_ref)

        @pl.loop(0, cap)
        def _(c):
            image = tab_ref[first + k * cap + c]

            @pl.when(image >= 0)
            def _():
                total_ref[image] += decode(slot_ref[c], VIEW_BOUND)


def fold_kernel(first, cap, bound, half, tab_ref, *refs):
    slot_refs, out_refs, total = refs[:half], refs[half:-1], refs[-1]
    fold(first, half, cap, tab_ref, slot_refs, total)
    rows = out_refs[0].shape[1]
    for part, out_ref in enumerate(out_refs):

        @pl.loop(0, total.shape[0])
        def _(i):
            value = total[i, part * rows : (part + 1) * rows]
            out_ref[i] = encode(jnp.abs(value) * (1.0 / CODE_UNIT), value < 0.0, bound)


def fold_slots(table, slots, first, images, cap, bound, parts):
    rows = slots[0].shape[1]
    return pl.pallas_call(
        functools.partial(fold_kernel, first, cap, bound, len(slots)),
        out_shape=[jax.ShapeDtypeStruct((images, rows // parts, LANES), INTS)] * parts,
        in_specs=[SMEM] + [VMEM] * len(slots),
        out_specs=[VMEM] * parts,
        scratch_shapes=[pltpu.VMEM((images, rows, LANES), jnp.float32)],
        compiler_params=PARAMS,
        cost_estimate=COST,
        name="fold_slots",
    )(table, *slots)


def local_kernel(first, half, cap, tab_ref, *refs):
    fold(first, half, cap, tab_ref, refs[:-1], refs[-1])


def fold_local(table, slots, first, images, half, cap):
    rows = slots[0].shape[-2]
    return pl.pallas_call(
        functools.partial(local_kernel, first, half, cap),
        out_shape=jax.ShapeDtypeStruct((images, rows, LANES), jnp.float32),
        in_specs=[SMEM] + [VMEM] * len(slots),
        out_specs=VMEM,
        compiler_params=PARAMS,
        cost_estimate=COST,
        name="fold_local",
    )(table, *slots)


def adam_step(values, moment, second, gradient, step_rate):
    step_count = START + 1
    moment = beta_one * moment + (1.0 - beta_one) * gradient
    second = beta_two * second + (1.0 - beta_two) * gradient * gradient
    fix_one = 1.0 - beta_one**step_count
    fix_two = 1.0 - beta_two**step_count
    values = values - step_rate * (moment / fix_one) / (jnp.sqrt(second / fix_two) + adam_eps)
    return (values, moment, second)


def depth_kernel(bound, local_ref, far_ref, x_ref, m_ref, s_ref, *refs):
    nx_ref, nm_ref, ns_ref, grad = refs[-4:]
    images, rows, _ = local_ref.shape
    for i in range(images):
        grad[i * rows : (i + 1) * rows] = local_ref[i] + decode(far_ref[i], bound)
    for t in range(rows):
        here = slice(t * LANES, (t + 1) * LANES)
        gradient = grad[pl.ds(t, images, stride=rows), :]
        nx_ref[:, here], nm_ref[:, here], ns_ref[:, here] = adam_step(
            x_ref[:, here], m_ref[:, here], s_ref[:, here], gradient, depth_rate
        )


def update_depths(local, far, values, moment, second, bound, chunk, done):
    images, rows, _ = far.shape
    block = 48
    steps = rows // block
    first = chunk * steps
    wide = pl.BlockSpec((images, block * LANES), lambda t: (0, first + t))
    return pl.pallas_call(
        functools.partial(depth_kernel, bound),
        grid=(steps,),
        out_shape=[jax.ShapeDtypeStruct(values.shape, jnp.float32)] * 3,
        in_specs=[
            pl.BlockSpec((images, block, LANES), lambda t: (0, first + t, 0)),
            pl.BlockSpec((images, block, LANES), lambda t: (0, t, 0)),
            wide,
            wide,
            wide,
        ]
        + [pl.BlockSpec(memory_space=pl.ANY)] * len(done),
        out_specs=[wide, wide, wide],
        input_output_aliases={5 + i: i for i in range(len(done))},
        scratch_shapes=[pltpu.VMEM((images * block, LANES), jnp.float32)],
        compiler_params=PARAMS,
        cost_estimate=COST,
        name="update_depths",
    )(local, far, values, moment, second, *done)


def rotation(first, middle, last):
    inverse = 1.0 / (1.0 + first * first + middle * middle + last * last)
    return (
        (1.0 + first * first - middle * middle - last * last) * inverse,
        2.0 * (first * middle - last) * inverse,
        2.0 * (first * last + middle) * inverse,
        2.0 * (first * middle + last) * inverse,
        (1.0 - first * first + middle * middle - last * last) * inverse,
        2.0 * (middle * last - first) * inverse,
        2.0 * (first * last - middle) * inverse,
        2.0 * (middle * last + first) * inverse,
        (1.0 - first * first - middle * middle + last * last) * inverse,
    )


def cross(a, b):
    return [a[(j + 1) % 3] * b[(j + 2) % 3] - a[(j + 2) % 3] * b[(j + 1) % 3] for j in range(3)]


def turn_gradient(spin, torque):
    factor = 2.0 / (1.0 + spin[0] * spin[0] + spin[1] * spin[1] + spin[2] * spin[2])
    swing = cross(spin, torque)
    return [factor * (torque[j] + swing[j]) for j in range(3)]


def view_parts(cam_ref, pose_ref):
    cams = [cam_ref[:, i : i + 1] for i in range(7)]
    poses = [pose_ref[:, i : i + 1] for i in range(7)]
    cam = rotation(cams[1], cams[2], cams[3])
    pose = rotation(poses[0], poses[1], poses[2])
    scale = jnp.exp(poses[6])
    back = jnp.exp(-poses[6])
    gap = [cams[4 + k] - poses[3 + k] for k in range(3)]
    both = [
        [sum(pose[3 * k + j] * cam[3 * k + i] for k in range(3)) for i in range(3)] for j in range(3)
    ]
    matrix = [[both[j][i] * back for i in range(3)] for j in range(3)]
    shift = [sum(pose[3 * k + j] * gap[k] for k in range(3)) * back for j in range(3)]
    return cams, poses, both, pose, scale, matrix, shift


def coef_kernel(images, image_ref, all_ref, pair_ref, out_ref, cam_ref, pose_ref):
    views = cam_ref.shape[0]
    for r in range(views):
        image = image_ref[r % 2, r // 2]
        owner = over(image, images)
        cam_ref[r : r + 1, :] = all_ref[owner, pl.ds(image - owner * images, 1), 0:7]
        pose_ref[r : r + 1, :] = pair_ref[r // 2 : r // 2 + 1, :]
    cams, _, _, _, scale, matrix, shift = view_parts(cam_ref, pose_ref)
    inverse_focal = jnp.exp(-cams[0]) * (1.0 / WIDTH)
    rows = [matrix[j][0] * inverse_focal for j in range(3)]
    rows += [matrix[j][1] * inverse_focal for j in range(3)]
    rows += [matrix[j][2] for j in range(3)]
    rows += shift
    rows += [scale * scale * (1.0 / CODE_UNIT)]
    for i, row in enumerate(rows):
        out_ref[:, i : i + 1] = row


def view_coefs(pair_images, mail, pair_poses, images):
    views = 2 * pair_poses.shape[0]
    return pl.pallas_call(
        functools.partial(coef_kernel, images),
        out_shape=[
            jax.ShapeDtypeStruct((views, COEFS), jnp.float32),
            jax.ShapeDtypeStruct((views, 7), jnp.float32),
            jax.ShapeDtypeStruct((views, 7), jnp.float32),
        ],
        in_specs=[SMEM, VMEM, VMEM],
        out_specs=[VMEM, VMEM, VMEM],
        cost_estimate=COST,
        name="view_coefs",
    )(pair_images, mail, pair_poses)


def term_kernel(image_ref, cam_ref, pose_ref, *refs):
    cams, poses, both, pose, scale, matrix, shift = view_parts(cam_ref, pose_ref)
    sum_refs, (small_ref, terms, turns) = refs[:-3], refs[-3:]
    views = cam_ref.shape[0]
    sums = jnp.sum(sum(ref[...] for ref in sum_refs), axis=2)
    sums = [sums[:, i : i + 1] for i in range(SUMS)]
    square = scale * scale
    force, torque, stretch, drawn, lever = sums[0:3], sums[3:6], sums[6], sums[7], sums[8:11]
    push = [scale * sum(pose[3 * k + j] * force[j] for j in range(3)) for k in range(3)]
    swing = cross(shift, force)
    arm = [torque[j] - swing[j] for j in range(3)]
    camera_torque = [square * sum(both[j][i] * arm[j] for j in range(3)) for i in range(3)]
    pose_torque = [-square * torque[j] for j in range(3)]
    focal = -square * (drawn - sum(matrix[j][2] * lever[j] for j in range(3)))
    camera = [focal] + turn_gradient(cams[1:4], camera_torque) + push
    posed = (
        turn_gradient(poses[0:3], pose_torque) + [-value for value in push] + [-square * stretch]
    )
    terms[...] = jnp.zeros_like(terms)
    turns[...] = jnp.zeros_like(turns)
    for i in range(7):
        terms[:, i : i + 1] = camera[i]
        turns[:, i : i + 1] = posed[i]
    both_views = turns[pl.ds(0, views // 2, stride=2), :] + turns[pl.ds(1, views // 2, stride=2), :]
    images = small_ref.shape[0] - views // 2
    small_ref[0:images] = jnp.zeros((images, 7), jnp.float32)
    for r in range(views):
        here = pl.ds(image_ref[r % 2, r // 2], 1)
        small_ref[here, :] += terms[r : r + 1, 0:7]
    small_ref[images:] = both_views[:, 0:7]


def view_terms(pair_images, cams, poses, sums, images):
    views = cams.shape[0]
    return pl.pallas_call(
        term_kernel,
        out_shape=jax.ShapeDtypeStruct((images + views // 2, 7), jnp.float32),
        in_specs=[SMEM] + [VMEM] * (2 + len(sums)),
        out_specs=VMEM,
        scratch_shapes=[pltpu.VMEM((views, LANES), jnp.float32)] * 2,
        cost_estimate=COST,
        name="view_terms",
    )(pair_images, cams, poses, *sums)


def small_kernel(mail_ref, pose_ref, *refs):
    values, outs = refs[:6], refs[6:]
    camera_grad = jnp.sum(mail_ref[...], axis=0) * (1.0 / NPIX)
    pose_grad = pose_ref[...] * (1.0 / NPIX)
    for i, (gradient, rate) in enumerate(((camera_grad, camera_rate), (pose_grad, pose_rate))):
        new = adam_step(*(ref[...] for ref in values[3 * i : 3 * i + 3]), gradient, rate)
        for ref, value in zip(outs[3 * i : 3 * i + 3], new):
            ref[...] = value


def update_small(mail, pose_grad, cameras, poses):
    return pl.pallas_call(
        small_kernel,
        out_shape=[jax.ShapeDtypeStruct(value.shape, jnp.float32) for value in cameras + poses],
        in_specs=[VMEM] * 8,
        out_specs=[VMEM] * 6,
        cost_estimate=COST,
        name="update_small",
    )(mail, pose_grad, *cameras, *poses)


def body(
    pair_images,
    depths,
    depth_moment,
    depth_second,
    cameras,
    camera_moment,
    camera_second,
    pair_poses,
    pair_moment,
    pair_second,
    pointmaps,
    confidence,
):
    shards = lax.axis_size("img")
    half = shards // 2
    me = lax.axis_index("img")
    rep = lax.axis_index("rep")
    images, row_len = depths.shape
    pairs = pair_images.shape[0]
    requests = 2 * pairs
    cap = max(2, 3 * pairs // shards)
    rows = row_len // LANES
    far_bound = VIEW_BOUND * half * cap

    def swap(value, k):
        return lax.ppermute(value, "img", [(i, i ^ k) for i in range(shards)])

    slots = half * cap

    def exchange(values):
        return [values[0]] + [swap(values[k], k) for k in range(1, half)]

    tie = lax.optimization_barrier

    names = pair_images.T
    letters = letters_of(names, cameras, shards)
    codes = jnp.round((depths - DEPTH_MID) * (1.0 / DEPTH_STEP)).astype(INTS)
    codes = codes.reshape(images, rows, LANES)
    size = rows // SWAP_PARTS
    parts = [codes[:, c * size : (c + 1) * size] for c in range(SWAP_PARTS)]
    letters, parts[1:] = tie((letters, parts[1:]))
    mail = lax.all_to_all(letters, "img", 0, 0, tiled=True)
    far = [swap(part, half) for part in parts]

    lists = mail[:, images, :requests].astype(jnp.int32)
    table = slot_tables(me.reshape(1), lists, half, cap, images)
    near = pack_slots(table, [codes], 0, half, cap)
    mail, near = tie((mail, near))
    near = exchange(near)
    coefs, cams, poses = view_coefs(names, mail, pair_poses, images)
    row = rep * (row_len // WIDTH)
    row = (row.astype(jnp.float32) + (0.5 - 0.5 * HEIGHT)).reshape(1)
    far, coefs = tie((far, coefs))
    asked = pack_slots(table, far, slots, half, cap)
    coefs, asked = tie((coefs, asked))
    asked = exchange(asked)
    views, slopes = prepare_views(row, coefs, pointmaps, confidence)

    near_sums = view_sums(table, coefs, row, views, near, 2 * slots, half, cap)
    near_grads = depth_grads(table, slopes, near, 2 * slots, half, cap, False)
    asked, near_sums, near_grads = tie((asked, near_sums, near_grads))
    far_grads = depth_grads(table, slopes, asked, 3 * slots, half, cap, False)
    asked, far_grads = tie((asked, far_grads))
    back = exchange(far_grads)
    far_sums = view_sums(table, coefs, row, views, asked, 3 * slots, half, cap)
    back, far_sums = tie((back, far_sums))
    folded = fold_slots(table, back, slots, images, cap, far_bound, 1)
    folded, far_sums = tie((folded, far_sums))
    far_codes = [swap(part, half) for part in folded]
    small = view_terms(names, cams, poses, [near_sums, far_sums], shards * images)
    near_grads, small = tie((near_grads, small))
    near_total = fold_local(table, exchange(near_grads), 0, images, half, cap)
    done = []
    for c in range(1):
        done = update_depths(
            near_total, far_codes[c], depths, depth_moment, depth_second, far_bound, c, done
        )

    bit = 1
    while bit < lax.axis_size("rep"):
        small = small + lax.ppermute(
            small, "rep", [(i, i ^ bit) for i in range(lax.axis_size("rep"))]
        )
        bit *= 2
    camera_mail = lax.all_to_all(
        small[: shards * images].reshape(shards, images, 7), "img", 0, 0, tiled=True
    )
    new = update_small(
        camera_mail,
        small[shards * images :].T,
        [cameras, camera_moment, camera_second],
        [pair_poses.T, pair_moment.T, pair_second.T],
    )
    return (*done, *new[:3], *(value.T for value in new[3:]))


def solution(mesh):
    return jax.shard_map(
        body,
        mesh=mesh,
        in_specs=(
            P("img", None),
            P("img", "rep"),
            P("img", "rep"),
            P("img", "rep"),
            P("img", None),
            P("img", None),
            P("img", None),
            P("img", None),
            P("img", None),
            P("img", None),
            P("img", None, None, "rep"),
            P("img", None, "rep"),
        ),
        out_specs=(
            P("img", "rep"),
            P("img", "rep"),
            P("img", "rep"),
            P("img", None),
            P("img", None),
            P("img", None),
            P("img", None),
            P("img", None),
            P("img", None),
        ),
        check_vma=False,
    )
```

```python
import functools
import math

import jax
import jax.numpy as jnp
from jax import lax
from jax.experimental import pallas as pl
from jax.experimental.pallas import tpu as pltpu
from jax.sharding import PartitionSpec as P

HEIGHT = 288
WIDTH = 512
START = 50
NPIX = 147456
LANES = 128
SWAP_PARTS = 2

beta_one = 0.9
beta_two = 0.999
adam_eps = 1e-08
depth_rate = 0.05
camera_rate = 0.01
pose_rate = 0.01

DEPTH_MID = 2.25
DEPTH_STEP = 1.75 / 32766.0
VIEW_BOUND = 340.0
CODE_UNIT = 8.0
INTS = jnp.int16
SUMS = 11
COEFS = 16

SMEM = pl.BlockSpec(memory_space=pltpu.SMEM)
VMEM = pl.BlockSpec(memory_space=pltpu.VMEM)
COST = pl.CostEstimate(flops=1, bytes_accessed=1, transcendentals=0)
PARAMS = pltpu.CompilerParams(vmem_limit_bytes=32 * 1024 * 1024)


def code_scale(bound):
    return 32766.0 / math.log2(1.0 + bound / CODE_UNIT)


def encode(magnitude, negative, bound):
    steps = (jnp.log2(1.0 + magnitude) * code_scale(bound) + 0.5).astype(jnp.int32)
    steps = jnp.minimum(steps, 32767)
    return jnp.where(negative, -steps, steps).astype(INTS)


def decode(code, bound):
    steps = code.astype(jnp.int32)
    size = jnp.abs(steps).astype(jnp.float32) * (1.0 / code_scale(bound))
    value = CODE_UNIT * jnp.exp2(size) - CODE_UNIT
    return jnp.where(steps < 0, -value, value)


def letter_kernel(image_ref, camera_ref, out_ref):
    shards, rows, _ = out_ref.shape
    lane = lax.broadcasted_iota(jnp.int32, (1, LANES), 1)
    names = jnp.zeros((1, LANES), jnp.int32)
    for r in range(2 * image_ref.shape[1]):
        names = jnp.where(lane == r, image_ref[r % 2, r // 2], names)
    for i in range(shards):
        out_ref[i, 0 : rows - 1, 0:7] = camera_ref[...]
        out_ref[i, rows - 1 : rows] = names.astype(jnp.float32)


def letters_of(pair_images, cameras, shards):
    images = cameras.shape[0]
    return pl.pallas_call(
        letter_kernel,
        out_shape=jax.ShapeDtypeStruct((shards, images + 1, LANES), jnp.float32),
        in_specs=[SMEM, VMEM],
        out_specs=VMEM,
        cost_estimate=COST,
        name="letters_of",
    )(pair_images, cameras)


def over(number, size):
    if size & (size - 1):
        return lax.div(number, size)
    return lax.shift_right_logical(number, size.bit_length() - 1)


def table_kernel(half, cap, images, me_ref, *refs):
    list_ref, tab_ref, count_ref = refs
    me = me_ref[0]
    shards = 2 * half
    asked = shards * cap
    requests = list_ref.shape[1]

    @pl.loop(0, 2 * asked, unroll=8)
    def _(i):
        tab_ref[i] = -1

    tab_ref[2 * asked] = me & (half - 1)

    @pl.loop(0, 2 * shards, unroll=8)
    def _(i):
        count_ref[i] = 0

    def put(cell, value):
        rank = count_ref[cell]
        tab_ref[cell * cap + jnp.minimum(rank, cap - 1)] = value
        count_ref[cell] = rank + 1

    for k in range(half):
        asker = me ^ k

        @pl.loop(0, requests, unroll=2)
        def _(r):
            image = list_ref[asker, r]
            owner = over(image, images)
            mine = owner == me

            @pl.when(mine | (owner == (me ^ half)))
            def _():
                put(jnp.where(mine, k, half + k), image - owner * images)

    @pl.loop(0, requests, unroll=2)
    def _(r):
        image = list_ref[me, r]
        owner = over(image, images)
        put(shards + (owner ^ me), r)


def slot_tables(me, lists, half, cap, images):
    return pl.pallas_call(
        functools.partial(table_kernel, half, cap, images),
        out_shape=jax.ShapeDtypeStruct((4 * half * cap + 1,), jnp.int32),
        in_specs=[SMEM, SMEM],
        out_specs=SMEM,
        scratch_shapes=[pltpu.SMEM((4 * half,), jnp.int32)],
        cost_estimate=COST,
        name="slot_tables",
    )(me, lists)


def pack_kernel(first, half, tab_ref, *refs):
    map_refs, slot_refs = refs[:-half], refs[-half:]
    for k, slot_ref in enumerate(slot_refs):

        @pl.loop(0, slot_ref.shape[0])
        def _(c):
            image = jnp.maximum(tab_ref[first + k * slot_ref.shape[0] + c], 0)
            first_row = 0
            for map_ref in map_refs:
                rows = map_ref.shape[1]
                slot_ref[c, first_row : first_row + rows] = map_ref[image]
                first_row += rows


def pack_slots(table, maps, first, half, cap):
    rows = sum(part.shape[1] for part in maps)
    return pl.pallas_call(
        functools.partial(pack_kernel, first, half),
        out_shape=[jax.ShapeDtypeStruct((cap, rows, LANES), INTS)] * half,
        in_specs=[SMEM] + [VMEM] * len(maps),
        out_specs=[VMEM] * half,
        compiler_params=PARAMS,
        cost_estimate=COST,
        name="pack_slots",
    )(table, *maps)


def columns_and_lines(top):
    across = WIDTH // LANES
    line = lax.broadcasted_iota(jnp.int32, (16, LANES), 0)
    lane = lax.broadcasted_iota(jnp.int32, (16, LANES), 1)
    columns = ((line % across) * LANES + lane).astype(jnp.float32) + (0.5 - 0.5 * WIDTH)
    return columns, (line // across).astype(jnp.float32) + top


def ray_start(columns, lines, coef):
    ray = [columns * coef(j) + (lines * coef(3 + j) + coef(6 + j)) for j in range(3)]
    step = [coef(3 + j) * (16.0 * LANES / WIDTH) for j in range(3)]
    return ray, step


def prepare_kernel(row_ref, coef_ref, point_ref, weight_ref, view_ref, slope_ref, wide):
    rows = view_ref.shape[2]
    columns, lines = columns_and_lines(row_ref[0])

    @pl.loop(0, point_ref.shape[0])
    def _(pair):
        for q in range(4):
            source = point_ref.at[pair, q] if q < 3 else weight_ref.at[pair]
            wide[q] = source[...].astype(jnp.float32)
        for v in range(2):
            view = 2 * pair + v

            def coef(i):
                return coef_ref[view, i]

            ray, step = ray_start(columns, lines, coef)
            shift = [coef(9 + j) for j in range(3)]
            gain = coef(12)
            for t in range(0, rows, 16):
                here = slice(t, t + 16)
                part = [wide[q, pl.ds(2 * t + v, 16, stride=2), :] for q in range(4)]
                for q in range(4):
                    view_ref[view, q, here] = part[q].astype(jnp.bfloat16)
                weight = part[3] * gain
                slope = weight * (ray[0] * ray[0] + ray[1] * ray[1] + ray[2] * ray[2])
                rest = [ray[j] * (shift[j] - part[j]) for j in range(3)]
                slope_ref[view, 0, here] = slope * DEPTH_STEP
                slope_ref[view, 1, here] = slope * DEPTH_MID + weight * (
                    rest[0] + rest[1] + rest[2]
                )
                ray = [ray[j] + step[j] for j in range(3)]


def prepare_views(row, coefs, points, weights):
    pairs, _, _, pixels = points.shape
    rows = pixels // LANES
    points = (
        points.transpose(0, 2, 1, 3)
        .reshape(pairs, 3, 2, rows, LANES)
        .transpose(0, 1, 3, 2, 4)
        .reshape(pairs, 3, 2 * rows, LANES)
    )
    weights = (
        weights.reshape(pairs, 2, rows, LANES).transpose(0, 2, 1, 3).reshape(pairs, 2 * rows, LANES)
    )
    return pl.pallas_call(
        prepare_kernel,
        out_shape=[
            jax.ShapeDtypeStruct((2 * pairs, 4, rows, LANES), jnp.bfloat16),
            jax.ShapeDtypeStruct((2 * pairs, 2, rows, LANES), jnp.float32),
        ],
        in_specs=[SMEM, SMEM, VMEM, VMEM],
        out_specs=[VMEM, VMEM],
        scratch_shapes=[pltpu.VMEM((4, 2 * rows, LANES), jnp.float32)],
        compiler_params=PARAMS,
        cost_estimate=COST,
        name="prepare_views",
    )(row, coefs, points, weights)


def slots_at(refs, k, tab_ref):
    return refs[k] if len(refs) > 1 else refs[0].at[k ^ tab_ref[tab_ref.shape[0] - 1]]


def grad_kernel(first, half, cap, tab_ref, slope_ref, *refs):
    depth_refs, grad_refs = refs[:half], refs[half:]
    rows = depth_refs[0].shape[1]
    for k in range(half):
        depth_ref = depth_refs[k]
        grad_ref = slots_at(grad_refs, k, tab_ref)

        @pl.loop(0, cap)
        def _(c):
            view = tab_ref[first + k * cap + c]

            @pl.when(view >= 0)
            def _():
                for t in range(0, rows, 16):
                    here = slice(t, t + 16)
                    code = depth_ref[c, here].astype(jnp.int32).astype(jnp.float32)
                    along = code * slope_ref[view, 0, here] + slope_ref[view, 1, here]
                    grad_ref[c, here] = encode(jnp.abs(along), along < 0.0, VIEW_BOUND)


def depth_grads(table, slopes, depths, first, half, cap, by_rank):
    rows = depths[0].shape[1]
    if by_rank:
        out = [jax.ShapeDtypeStruct((half, cap, rows, LANES), INTS)]
    else:
        out = [jax.ShapeDtypeStruct((cap, rows, LANES), INTS)] * half
    return pl.pallas_call(
        functools.partial(grad_kernel, first, half, cap),
        out_shape=out,
        in_specs=[SMEM] + [VMEM] * (1 + half),
        out_specs=[VMEM] * len(out),
        compiler_params=PARAMS,
        cost_estimate=COST,
        name="depth_grads",
    )(table, slopes, *depths)


def sum_kernel(first, half, cap, tab_ref, coef_ref, row_ref, view_ref, *refs):
    depth_refs = refs[:-2]
    sum_ref, depth_all = refs[-2:]
    slots, rows, _ = depth_all.shape
    for k in range(half):
        depth_ref = depth_refs[k]
        depth_all[k * cap : (k + 1) * cap] = depth_ref[...]
    sum_ref[...] = jnp.zeros_like(sum_ref)
    columns, lines = columns_and_lines(row_ref[0])

    @pl.loop(0, slots)
    def _(s):
        view = tab_ref[first + s]

        @pl.when(view >= 0)
        def _():
            def coef(i):
                return coef_ref[view, i]

            ray, step = ray_start(columns, lines, coef)
            shift = [coef(9 + j) for j in range(3)]
            totals = [None] * SUMS

            def add(i, value):
                value = value[:8] + value[8:]
                totals[i] = value if totals[i] is None else totals[i] + value

            for t in range(0, rows, 16):
                here = slice(t, t + 16)
                point = [view_ref[view, j, here].astype(jnp.float32) for j in range(3)]
                weight = view_ref[view, 3, here].astype(jnp.float32)
                depth = (
                    depth_all[s, here].astype(jnp.int32).astype(jnp.float32) * DEPTH_STEP
                    + DEPTH_MID
                )
                pull = [weight * (depth * ray[j] + (shift[j] - point[j])) for j in range(3)]
                along = pull[0] * ray[0] + pull[1] * ray[1] + pull[2] * ray[2]
                for j in range(3):
                    add(j, pull[j])
                    add(8 + j, depth * pull[j])
                    a, b = (j + 1) % 3, (j + 2) % 3
                    add(3 + j, point[a] * pull[b] - point[b] * pull[a])
                add(6, point[0] * pull[0] + point[1] * pull[1] + point[2] * pull[2])
                add(7, depth * along)
                ray = [ray[j] + step[j] for j in range(3)]
            for i in range(SUMS):
                sum_ref[view, i : i + 1] = jnp.sum(totals[i], axis=0, keepdims=True)


def view_sums(table, coefs, row, views, depths, first, half, cap):
    rows = depths[0].shape[1]
    return pl.pallas_call(
        functools.partial(sum_kernel, first, half, cap),
        out_shape=jax.ShapeDtypeStruct((views.shape[0], COEFS, LANES), jnp.float32),
        in_specs=[SMEM, SMEM, SMEM] + [VMEM] * (1 + len(depths)),
        out_specs=VMEM,
        scratch_shapes=[pltpu.VMEM((half * cap, rows, LANES), INTS)],
        compiler_params=PARAMS,
        cost_estimate=COST,
        name="view_sums",
    )(table, coefs, row, views, *depths)


def fold(first, half, cap, tab_ref, slot_refs, total_ref):
    total_ref[...] = jnp.zeros_like(total_ref)
    for k in range(half):
        slot_ref = slots_at(slot_refs, k, tab_ref)

        @pl.loop(0, cap)
        def _(c):
            image = tab_ref[first + k * cap + c]

            @pl.when(image >= 0)
            def _():
                total_ref[image] += decode(slot_ref[c], VIEW_BOUND)


def fold_kernel(first, cap, bound, half, tab_ref, *refs):
    slot_refs, out_refs, total = refs[:half], refs[half:-1], refs[-1]
    fold(first, half, cap, tab_ref, slot_refs, total)
    rows = out_refs[0].shape[1]
    for part, out_ref in enumerate(out_refs):

        @pl.loop(0, total.shape[0])
        def _(i):
            value = total[i, part * rows : (part + 1) * rows]
            out_ref[i] = encode(jnp.abs(value) * (1.0 / CODE_UNIT), value < 0.0, bound)


def fold_slots(table, slots, first, images, cap, bound, parts):
    rows = slots[0].shape[1]
    return pl.pallas_call(
        functools.partial(fold_kernel, first, cap, bound, len(slots)),
        out_shape=[jax.ShapeDtypeStruct((images, rows // parts, LANES), INTS)] * parts,
        in_specs=[SMEM] + [VMEM] * len(slots),
        out_specs=[VMEM] * parts,
        scratch_shapes=[pltpu.VMEM((images, rows, LANES), jnp.float32)],
        compiler_params=PARAMS,
        cost_estimate=COST,
        name="fold_slots",
    )(table, *slots)


def local_kernel(first, half, cap, tab_ref, *refs):
    fold(first, half, cap, tab_ref, refs[:-1], refs[-1])


def fold_local(table, slots, first, images, half, cap):
    rows = slots[0].shape[-2]
    return pl.pallas_call(
        functools.partial(local_kernel, first, half, cap),
        out_shape=jax.ShapeDtypeStruct((images, rows, LANES), jnp.float32),
        in_specs=[SMEM] + [VMEM] * len(slots),
        out_specs=VMEM,
        compiler_params=PARAMS,
        cost_estimate=COST,
        name="fold_local",
    )(table, *slots)


def adam_step(values, moment, second, gradient, step_rate):
    step_count = START + 1
    moment = beta_one * moment + (1.0 - beta_one) * gradient
    second = beta_two * second + (1.0 - beta_two) * gradient * gradient
    fix_one = 1.0 - beta_one**step_count
    fix_two = 1.0 - beta_two**step_count
    values = values - step_rate * (moment / fix_one) / (jnp.sqrt(second / fix_two) + adam_eps)
    return (values, moment, second)


def depth_kernel(bound, local_ref, far_ref, x_ref, m_ref, s_ref, *refs):
    nx_ref, nm_ref, ns_ref, grad = refs[-4:]
    images, rows, _ = local_ref.shape
    for i in range(images):
        grad[i * rows : (i + 1) * rows] = local_ref[i] + decode(far_ref[i], bound)
    for t in range(rows):
        here = slice(t * LANES, (t + 1) * LANES)
        gradient = grad[pl.ds(t, images, stride=rows), :]
        nx_ref[:, here], nm_ref[:, here], ns_ref[:, here] = adam_step(
            x_ref[:, here], m_ref[:, here], s_ref[:, here], gradient, depth_rate
        )


def update_depths(local, far, values, moment, second, bound, chunk, done):
    images, rows, _ = far.shape
    block = 48
    steps = rows // block
    first = chunk * steps
    wide = pl.BlockSpec((images, block * LANES), lambda t: (0, first + t))
    return pl.pallas_call(
        functools.partial(depth_kernel, bound),
        grid=(steps,),
        out_shape=[jax.ShapeDtypeStruct(values.shape, jnp.float32)] * 3,
        in_specs=[
            pl.BlockSpec((images, block, LANES), lambda t: (0, first + t, 0)),
            pl.BlockSpec((images, block, LANES), lambda t: (0, t, 0)),
            wide,
            wide,
            wide,
        ]
        + [pl.BlockSpec(memory_space=pl.ANY)] * len(done),
        out_specs=[wide, wide, wide],
        input_output_aliases={5 + i: i for i in range(len(done))},
        scratch_shapes=[pltpu.VMEM((images * block, LANES), jnp.float32)],
        compiler_params=PARAMS,
        cost_estimate=COST,
        name="update_depths",
    )(local, far, values, moment, second, *done)


def rotation(first, middle, last):
    inverse = 1.0 / (1.0 + first * first + middle * middle + last * last)
    return (
        (1.0 + first * first - middle * middle - last * last) * inverse,
        2.0 * (first * middle - last) * inverse,
        2.0 * (first * last + middle) * inverse,
        2.0 * (first * middle + last) * inverse,
        (1.0 - first * first + middle * middle - last * last) * inverse,
        2.0 * (middle * last - first) * inverse,
        2.0 * (first * last - middle) * inverse,
        2.0 * (middle * last + first) * inverse,
        (1.0 - first * first - middle * middle + last * last) * inverse,
    )


def cross(a, b):
    return [a[(j + 1) % 3] * b[(j + 2) % 3] - a[(j + 2) % 3] * b[(j + 1) % 3] for j in range(3)]


def turn_gradient(spin, torque):
    factor = 2.0 / (1.0 + spin[0] * spin[0] + spin[1] * spin[1] + spin[2] * spin[2])
    swing = cross(spin, torque)
    return [factor * (torque[j] + swing[j]) for j in range(3)]


def view_parts(cam_ref, pose_ref):
    cams = [cam_ref[:, i : i + 1] for i in range(7)]
    poses = [pose_ref[:, i : i + 1] for i in range(7)]
    cam = rotation(cams[1], cams[2], cams[3])
    pose = rotation(poses[0], poses[1], poses[2])
    scale = jnp.exp(poses[6])
    back = jnp.exp(-poses[6])
    gap = [cams[4 + k] - poses[3 + k] for k in range(3)]
    both = [
        [sum(pose[3 * k + j] * cam[3 * k + i] for k in range(3)) for i in range(3)] for j in range(3)
    ]
    matrix = [[both[j][i] * back for i in range(3)] for j in range(3)]
    shift = [sum(pose[3 * k + j] * gap[k] for k in range(3)) * back for j in range(3)]
    return cams, poses, both, pose, scale, matrix, shift


def coef_kernel(images, image_ref, all_ref, pair_ref, out_ref, cam_ref, pose_ref):
    views = cam_ref.shape[0]
    for r in range(views):
        image = image_ref[r % 2, r // 2]
        owner = over(image, images)
        cam_ref[r : r + 1, :] = all_ref[owner, pl.ds(image - owner * images, 1), 0:7]
        pose_ref[r : r + 1, :] = pair_ref[r // 2 : r // 2 + 1, :]
    cams, _, _, _, scale, matrix, shift = view_parts(cam_ref, pose_ref)
    inverse_focal = jnp.exp(-cams[0]) * (1.0 / WIDTH)
    rows = [matrix[j][0] * inverse_focal for j in range(3)]
    rows += [matrix[j][1] * inverse_focal for j in range(3)]
    rows += [matrix[j][2] for j in range(3)]
    rows += shift
    rows += [scale * scale * (1.0 / CODE_UNIT)]
    for i, row in enumerate(rows):
        out_ref[:, i : i + 1] = row


def view_coefs(pair_images, mail, pair_poses, images):
    views = 2 * pair_poses.shape[0]
    return pl.pallas_call(
        functools.partial(coef_kernel, images),
        out_shape=[
            jax.ShapeDtypeStruct((views, COEFS), jnp.float32),
            jax.ShapeDtypeStruct((views, 7), jnp.float32),
            jax.ShapeDtypeStruct((views, 7), jnp.float32),
        ],
        in_specs=[SMEM, VMEM, VMEM],
        out_specs=[VMEM, VMEM, VMEM],
        cost_estimate=COST,
        name="view_coefs",
    )(pair_images, mail, pair_poses)


def term_kernel(image_ref, cam_ref, pose_ref, *refs):
    cams, poses, both, pose, scale, matrix, shift = view_parts(cam_ref, pose_ref)
    sum_refs, (small_ref, terms, turns) = refs[:-3], refs[-3:]
    views = cam_ref.shape[0]
    sums = jnp.sum(sum(ref[...] for ref in sum_refs), axis=2)
    sums = [sums[:, i : i + 1] for i in range(SUMS)]
    square = scale * scale
    force, torque, stretch, drawn, lever = sums[0:3], sums[3:6], sums[6], sums[7], sums[8:11]
    push = [scale * sum(pose[3 * k + j] * force[j] for j in range(3)) for k in range(3)]
    swing = cross(shift, force)
    arm = [torque[j] - swing[j] for j in range(3)]
    camera_torque = [square * sum(both[j][i] * arm[j] for j in range(3)) for i in range(3)]
    pose_torque = [-square * torque[j] for j in range(3)]
    focal = -square * (drawn - sum(matrix[j][2] * lever[j] for j in range(3)))
    camera = [focal] + turn_gradient(cams[1:4], camera_torque) + push
    posed = (
        turn_gradient(poses[0:3], pose_torque) + [-value for value in push] + [-square * stretch]
    )
    terms[...] = jnp.zeros_like(terms)
    turns[...] = jnp.zeros_like(turns)
    for i in range(7):
        terms[:, i : i + 1] = camera[i]
        turns[:, i : i + 1] = posed[i]
    both_views = turns[pl.ds(0, views // 2, stride=2), :] + turns[pl.ds(1, views // 2, stride=2), :]
    images = small_ref.shape[0] - views // 2
    small_ref[0:images] = jnp.zeros((images, 7), jnp.float32)
    for r in range(views):
        here = pl.ds(image_ref[r % 2, r // 2], 1)
        small_ref[here, :] += terms[r : r + 1, 0:7]
    small_ref[images:] = both_views[:, 0:7]


def view_terms(pair_images, cams, poses, sums, images):
    views = cams.shape[0]
    return pl.pallas_call(
        term_kernel,
        out_shape=jax.ShapeDtypeStruct((images + views // 2, 7), jnp.float32),
        in_specs=[SMEM] + [VMEM] * (2 + len(sums)),
        out_specs=VMEM,
        scratch_shapes=[pltpu.VMEM((views, LANES), jnp.float32)] * 2,
        cost_estimate=COST,
        name="view_terms",
    )(pair_images, cams, poses, *sums)


def small_kernel(mail_ref, pose_ref, *refs):
    values, outs = refs[:6], refs[6:]
    camera_grad = jnp.sum(mail_ref[...], axis=0) * (1.0 / NPIX)
    pose_grad = pose_ref[...] * (1.0 / NPIX)
    for i, (gradient, rate) in enumerate(((camera_grad, camera_rate), (pose_grad, pose_rate))):
        new = adam_step(*(ref[...] for ref in values[3 * i : 3 * i + 3]), gradient, rate)
        for ref, value in zip(outs[3 * i : 3 * i + 3], new):
            ref[...] = value


def update_small(mail, pose_grad, cameras, poses):
    return pl.pallas_call(
        small_kernel,
        out_shape=[jax.ShapeDtypeStruct(value.shape, jnp.float32) for value in cameras + poses],
        in_specs=[VMEM] * 8,
        out_specs=[VMEM] * 6,
        cost_estimate=COST,
        name="update_small",
    )(mail, pose_grad, *cameras, *poses)


def body(
    pair_images,
    depths,
    depth_moment,
    depth_second,
    cameras,
    camera_moment,
    camera_second,
    pair_poses,
    pair_moment,
    pair_second,
    pointmaps,
    confidence,
):
    shards = lax.axis_size("img")
    half = shards // 2
    me = lax.axis_index("img")
    rep = lax.axis_index("rep")
    images, row_len = depths.shape
    pairs = pair_images.shape[0]
    requests = 2 * pairs
    cap = max(2, 3 * pairs // shards)
    rows = row_len // LANES
    far_bound = VIEW_BOUND * half * cap

    def swap(value, k):
        return lax.ppermute(value, "img", [(i, i ^ k) for i in range(shards)])

    slots = half * cap

    def exchange(values):
        return [values[0]] + [swap(values[k], k) for k in range(1, half)]

    tie = lax.optimization_barrier

    names = pair_images.T
    letters = letters_of(names, cameras, shards)
    codes = jnp.round((depths - DEPTH_MID) * (1.0 / DEPTH_STEP)).astype(INTS)
    codes = codes.reshape(images, rows, LANES)
    first = rows // 48 * 16 * 2
    parts = [codes[:, :first], codes[:, first:]]
    letters, parts[1:] = tie((letters, parts[1:]))
    mail = lax.all_to_all(letters, "img", 0, 0, tiled=True)
    far = [swap(part, half) for part in parts]

    lists = mail[:, images, :requests].astype(jnp.int32)
    table = slot_tables(me.reshape(1), lists, half, cap, images)
    near = pack_slots(table, [codes], 0, half, cap)
    mail, near = tie((mail, near))
    near = exchange(near)
    coefs, cams, poses = view_coefs(names, mail, pair_poses, images)
    row = rep * (row_len // WIDTH)
    row = (row.astype(jnp.float32) + (0.5 - 0.5 * HEIGHT)).reshape(1)
    views, slopes = prepare_views(row, coefs, pointmaps, confidence)
    far, slopes = tie((far, slopes))
    asked = exchange(pack_slots(table, far, slots, half, cap))

    near_sums = view_sums(table, coefs, row, views, near, 2 * slots, half, cap)
    near_grads = depth_grads(table, slopes, near, 2 * slots, half, cap, False)
    asked, near_sums, near_grads = tie((asked, near_sums, near_grads))
    far_grads = depth_grads(table, slopes, asked, 3 * slots, half, cap, False)
    asked, far_grads = tie((asked, far_grads))
    back = exchange(far_grads)
    far_sums = view_sums(table, coefs, row, views, asked, 3 * slots, half, cap)
    back, far_sums = tie((back, far_sums))
    folded = fold_slots(table, back, slots, images, cap, far_bound, 1)
    folded, far_sums = tie((folded, far_sums))
    far_codes = [swap(part, half) for part in folded]
    small = view_terms(names, cams, poses, [near_sums, far_sums], shards * images)
    near_grads, small = tie((near_grads, small))
    near_total = fold_local(table, exchange(near_grads), 0, images, half, cap)
    done = []
    for c in range(1):
        done = update_depths(
            near_total, far_codes[c], depths, depth_moment, depth_second, far_bound, c, done
        )

    bit = 1
    while bit < lax.axis_size("rep"):
        small = small + lax.ppermute(
            small, "rep", [(i, i ^ bit) for i in range(lax.axis_size("rep"))]
        )
        bit *= 2
    camera_mail = lax.all_to_all(
        small[: shards * images].reshape(shards, images, 7), "img", 0, 0, tiled=True
    )
    camera_mail, done = tie((camera_mail, done))
    new = update_small(
        camera_mail,
        small[shards * images :].T,
        [cameras, camera_moment, camera_second],
        [pair_poses.T, pair_moment.T, pair_second.T],
    )
    return (*done, *new[:3], *(value.T for value in new[3:]))


def solution(mesh):
    return jax.shard_map(
        body,
        mesh=mesh,
        in_specs=(
            P("img", None),
            P("img", "rep"),
            P("img", "rep"),
            P("img", "rep"),
            P("img", None),
            P("img", None),
            P("img", None),
            P("img", None),
            P("img", None),
            P("img", None),
            P("img", None, None, "rep"),
            P("img", None, "rep"),
        ),
        out_specs=(
            P("img", "rep"),
            P("img", "rep"),
            P("img", "rep"),
            P("img", None),
            P("img", None),
            P("img", None),
            P("img", None),
            P("img", None),
            P("img", None),
        ),
        check_vma=False,
    )
```

```python
import functools
import math

import jax
import jax.numpy as jnp
from jax import lax
from jax.experimental import pallas as pl
from jax.experimental.pallas import tpu as pltpu
from jax.sharding import PartitionSpec as P

HEIGHT = 288
WIDTH = 512
START = 50
NPIX = 147456
LANES = 128
SWAP_PARTS = 2

beta_one = 0.9
beta_two = 0.999
adam_eps = 1e-08
depth_rate = 0.05
camera_rate = 0.01
pose_rate = 0.01

DEPTH_MID = 2.25
DEPTH_STEP = 1.75 / 32766.0
VIEW_BOUND = 340.0
SLOT_UNIT = VIEW_BOUND / 32766.0**2
CODE_UNIT = 8.0
INTS = jnp.int16
SUMS = 11
COEFS = 16

SMEM = pl.BlockSpec(memory_space=pltpu.SMEM)
VMEM = pl.BlockSpec(memory_space=pltpu.VMEM)
COST = pl.CostEstimate(flops=1, bytes_accessed=1, transcendentals=0)
PARAMS = pltpu.CompilerParams(vmem_limit_bytes=16 * 1024 * 1024)


def encode_slot(value):
    root = value * lax.rsqrt(jnp.maximum(jnp.abs(value), 1e-20))
    return jnp.round(root).astype(jnp.int32).astype(INTS)


def decode_slot(code):
    root = code.astype(jnp.int32).astype(jnp.float32)
    return root * jnp.abs(root)


def code_scale(bound):
    return 32766.0 / math.log2(1.0 + bound / CODE_UNIT)


def encode(magnitude, negative, bound):
    steps = (jnp.log2(1.0 + magnitude) * code_scale(bound) + 0.5).astype(jnp.int32)
    steps = jnp.minimum(steps, 32767)
    return jnp.where(negative, -steps, steps).astype(INTS)


def decode(code, bound):
    steps = code.astype(jnp.int32)
    size = jnp.abs(steps).astype(jnp.float32) * (1.0 / code_scale(bound))
    value = CODE_UNIT * jnp.exp2(size) - CODE_UNIT
    return jnp.where(steps < 0, -value, value)


def letter_kernel(image_ref, camera_ref, out_ref):
    shards, rows, _ = out_ref.shape
    lane = lax.broadcasted_iota(jnp.int32, (1, LANES), 1)
    names = jnp.zeros((1, LANES), jnp.int32)
    for r in range(2 * image_ref.shape[1]):
        names = jnp.where(lane == r, image_ref[r % 2, r // 2], names)
    for i in range(shards):
        out_ref[i, 0 : rows - 1, 0:7] = camera_ref[...]
        out_ref[i, rows - 1 : rows] = names.astype(jnp.float32)


def letters_of(pair_images, cameras, shards):
    images = cameras.shape[0]
    return pl.pallas_call(
        letter_kernel,
        out_shape=jax.ShapeDtypeStruct((shards, images + 1, LANES), jnp.float32),
        in_specs=[SMEM, VMEM],
        out_specs=VMEM,
        cost_estimate=COST,
        name="letters_of",
    )(pair_images, cameras)


def over(number, size):
    if size & (size - 1):
        return lax.div(number, size)
    return lax.shift_right_logical(number, size.bit_length() - 1)


def table_kernel(half, cap, images, me_ref, *refs):
    list_ref, tab_ref, count_ref = refs
    me = me_ref[0]
    shards = 2 * half
    asked = shards * cap
    requests = list_ref.shape[1]

    @pl.loop(0, 2 * asked, unroll=8)
    def _(i):
        tab_ref[i] = -1

    tab_ref[2 * asked] = me & (half - 1)

    @pl.loop(0, 2 * shards, unroll=8)
    def _(i):
        count_ref[i] = 0

    def put(cell, value):
        rank = count_ref[cell]
        tab_ref[cell * cap + jnp.minimum(rank, cap - 1)] = value
        count_ref[cell] = rank + 1

    for k in range(half):
        asker = me ^ k

        @pl.loop(0, requests, unroll=2)
        def _(r):
            image = list_ref[asker, r]
            owner = over(image, images)
            mine = owner == me

            @pl.when(mine | (owner == (me ^ half)))
            def _():
                put(jnp.where(mine, k, half + k), image - owner * images)

    @pl.loop(0, requests, unroll=2)
    def _(r):
        image = list_ref[me, r]
        owner = over(image, images)
        put(shards + (owner ^ me), r)


def slot_tables(me, lists, half, cap, images):
    return pl.pallas_call(
        functools.partial(table_kernel, half, cap, images),
        out_shape=jax.ShapeDtypeStruct((4 * half * cap + 1,), jnp.int32),
        in_specs=[SMEM, SMEM],
        out_specs=SMEM,
        scratch_shapes=[pltpu.SMEM((4 * half,), jnp.int32)],
        cost_estimate=COST,
        name="slot_tables",
    )(me, lists)


def pack_kernel(first, half, tab_ref, *refs):
    map_refs, slot_refs = refs[:-half], refs[-half:]
    for k, slot_ref in enumerate(slot_refs):

        @pl.loop(0, slot_ref.shape[0])
        def _(c):
            image = jnp.maximum(tab_ref[first + k * slot_ref.shape[0] + c], 0)
            first_row = 0
            for map_ref in map_refs:
                rows = map_ref.shape[1]
                slot_ref[c, first_row : first_row + rows] = map_ref[image]
                first_row += rows


def pack_slots(table, maps, first, half, cap):
    rows = sum(part.shape[1] for part in maps)
    return pl.pallas_call(
        functools.partial(pack_kernel, first, half),
        out_shape=[jax.ShapeDtypeStruct((cap, rows, LANES), INTS)] * half,
        in_specs=[SMEM] + [VMEM] * len(maps),
        out_specs=[VMEM] * half,
        compiler_params=PARAMS,
        cost_estimate=COST,
        name="pack_slots",
    )(table, *maps)


def columns_and_lines(top):
    across = WIDTH // LANES
    line = lax.broadcasted_iota(jnp.int32, (16, LANES), 0)
    lane = lax.broadcasted_iota(jnp.int32, (16, LANES), 1)
    columns = ((line % across) * LANES + lane).astype(jnp.float32) + (0.5 - 0.5 * WIDTH)
    return columns, (line // across).astype(jnp.float32) + top


def ray_start(columns, lines, coef):
    ray = [columns * coef(j) + (lines * coef(3 + j) + coef(6 + j)) for j in range(3)]
    step = [coef(3 + j) * (16.0 * LANES / WIDTH) for j in range(3)]
    return ray, step


def prepare_kernel(row_ref, coef_ref, point_ref, weight_ref, view_ref, slope_ref, wide):
    rows = view_ref.shape[2]
    columns, lines = columns_and_lines(row_ref[0])

    @pl.loop(0, point_ref.shape[0])
    def _(pair):
        for q in range(4):
            source = point_ref.at[pair, q] if q < 3 else weight_ref.at[pair]
            wide[q] = source[...].astype(jnp.float32)
        for v in range(2):
            view = 2 * pair + v

            def coef(i):
                return coef_ref[view, i]

            ray, step = ray_start(columns, lines, coef)
            shift = [coef(9 + j) for j in range(3)]
            gain = coef(12)
            for t in range(0, rows, 16):
                here = slice(t, t + 16)
                part = [wide[q, pl.ds(2 * t + v, 16, stride=2), :] for q in range(4)]
                for q in range(4):
                    view_ref[view, q, here] = part[q].astype(jnp.bfloat16)
                weight = part[3] * gain
                slope = weight * (ray[0] * ray[0] + ray[1] * ray[1] + ray[2] * ray[2])
                rest = [ray[j] * (shift[j] - part[j]) for j in range(3)]
                slope_ref[view, 0, here] = slope * DEPTH_STEP
                slope_ref[view, 1, here] = slope * DEPTH_MID + weight * (
                    rest[0] + rest[1] + rest[2]
                )
                ray = [ray[j] + step[j] for j in range(3)]


def prepare_views(row, coefs, points, weights):
    pairs, _, _, pixels = points.shape
    rows = pixels // LANES
    points = (
        points.transpose(0, 2, 1, 3)
        .reshape(pairs, 3, 2, rows, LANES)
        .transpose(0, 1, 3, 2, 4)
        .reshape(pairs, 3, 2 * rows, LANES)
    )
    weights = (
        weights.reshape(pairs, 2, rows, LANES).transpose(0, 2, 1, 3).reshape(pairs, 2 * rows, LANES)
    )
    return pl.pallas_call(
        prepare_kernel,
        out_shape=[
            jax.ShapeDtypeStruct((2 * pairs, 4, rows, LANES), jnp.bfloat16),
            jax.ShapeDtypeStruct((2 * pairs, 2, rows, LANES), jnp.float32),
        ],
        in_specs=[SMEM, SMEM, VMEM, VMEM],
        out_specs=[VMEM, VMEM],
        scratch_shapes=[pltpu.VMEM((4, 2 * rows, LANES), jnp.float32)],
        compiler_params=PARAMS,
        cost_estimate=COST,
        name="prepare_views",
    )(row, coefs, points, weights)


def slots_at(refs, k, tab_ref):
    return refs[k] if len(refs) > 1 else refs[0].at[k ^ tab_ref[tab_ref.shape[0] - 1]]


def grad_kernel(first, half, cap, tab_ref, slope_ref, *refs):
    depth_refs, grad_refs = refs[:half], refs[half:]
    rows = depth_refs[0].shape[1]
    for k in range(half):
        depth_ref = depth_refs[k]
        grad_ref = slots_at(grad_refs, k, tab_ref)

        @pl.loop(0, cap)
        def _(c):
            view = tab_ref[first + k * cap + c]

            @pl.when(view >= 0)
            def _():
                for t in range(0, rows, 16):
                    here = slice(t, t + 16)
                    code = depth_ref[c, here].astype(jnp.int32).astype(jnp.float32)
                    along = code * slope_ref[view, 0, here] + slope_ref[view, 1, here]
                    grad_ref[c, here] = encode_slot(along)


def depth_grads(table, slopes, depths, first, half, cap, by_rank):
    rows = depths[0].shape[1]
    if by_rank:
        out = [jax.ShapeDtypeStruct((half, cap, rows, LANES), INTS)]
    else:
        out = [jax.ShapeDtypeStruct((cap, rows, LANES), INTS)] * half
    return pl.pallas_call(
        functools.partial(grad_kernel, first, half, cap),
        out_shape=out,
        in_specs=[SMEM] + [VMEM] * (1 + half),
        out_specs=[VMEM] * len(out),
        compiler_params=PARAMS,
        cost_estimate=COST,
        name="depth_grads",
    )(table, slopes, *depths)


def sum_kernel(first, half, cap, tab_ref, coef_ref, row_ref, view_ref, *refs):
    depth_refs = refs[:-2]
    sum_ref, depth_all = refs[-2:]
    slots, rows, _ = depth_all.shape
    for k in range(half):
        depth_ref = depth_refs[k]
        depth_all[k * cap : (k + 1) * cap] = depth_ref[...]
    sum_ref[...] = jnp.zeros_like(sum_ref)
    columns, lines = columns_and_lines(row_ref[0])

    @pl.loop(0, slots)
    def _(s):
        view = tab_ref[first + s]

        @pl.when(view >= 0)
        def _():
            def coef(i):
                return coef_ref[view, i]

            ray, step = ray_start(columns, lines, coef)
            shift = [coef(9 + j) for j in range(3)]
            totals = [None] * SUMS

            def add(i, value):
                value = value[:8] + value[8:]
                totals[i] = value if totals[i] is None else totals[i] + value

            for t in range(0, rows, 16):
                here = slice(t, t + 16)
                point = [view_ref[view, j, here].astype(jnp.float32) for j in range(3)]
                weight = view_ref[view, 3, here].astype(jnp.float32)
                depth = (
                    depth_all[s, here].astype(jnp.int32).astype(jnp.float32) * DEPTH_STEP
                    + DEPTH_MID
                )
                pull = [weight * (depth * ray[j] + (shift[j] - point[j])) for j in range(3)]
                along = pull[0] * ray[0] + pull[1] * ray[1] + pull[2] * ray[2]
                for j in range(3):
                    add(j, pull[j])
                    add(8 + j, depth * pull[j])
                    a, b = (j + 1) % 3, (j + 2) % 3
                    add(3 + j, point[a] * pull[b] - point[b] * pull[a])
                add(6, point[0] * pull[0] + point[1] * pull[1] + point[2] * pull[2])
                add(7, depth * along)
                ray = [ray[j] + step[j] for j in range(3)]
            for i in range(SUMS):
                sum_ref[view, i : i + 1] = jnp.sum(totals[i], axis=0, keepdims=True)


def view_sums(table, coefs, row, views, depths, first, half, cap):
    rows = depths[0].shape[1]
    return pl.pallas_call(
        functools.partial(sum_kernel, first, half, cap),
        out_shape=jax.ShapeDtypeStruct((views.shape[0], COEFS, LANES), jnp.float32),
        in_specs=[SMEM, SMEM, SMEM] + [VMEM] * (1 + len(depths)),
        out_specs=VMEM,
        scratch_shapes=[pltpu.VMEM((half * cap, rows, LANES), INTS)],
        compiler_params=PARAMS,
        cost_estimate=COST,
        name="view_sums",
    )(table, coefs, row, views, *depths)


def fold(first, half, cap, tab_ref, slot_refs, total_ref):
    total_ref[...] = jnp.zeros_like(total_ref)
    for k in range(half):
        slot_ref = slots_at(slot_refs, k, tab_ref)

        @pl.loop(0, cap)
        def _(c):
            image = tab_ref[first + k * cap + c]

            @pl.when(image >= 0)
            def _():
                total_ref[image] += decode_slot(slot_ref[c])


def fold_kernel(first, cap, bound, half, tab_ref, *refs):
    slot_refs, out_refs, total = refs[:half], refs[half:-1], refs[-1]
    fold(first, half, cap, tab_ref, slot_refs, total)
    rows = out_refs[0].shape[1]
    for part, out_ref in enumerate(out_refs):

        @pl.loop(0, total.shape[0])
        def _(i):
            value = total[i, part * rows : (part + 1) * rows]
            out_ref[i] = encode(
                jnp.abs(value) * (SLOT_UNIT / CODE_UNIT), value < 0.0, bound
            )


def fold_slots(table, slots, first, images, cap, bound, parts):
    rows = slots[0].shape[1]
    return pl.pallas_call(
        functools.partial(fold_kernel, first, cap, bound, len(slots)),
        out_shape=[jax.ShapeDtypeStruct((images, rows // parts, LANES), INTS)] * parts,
        in_specs=[SMEM] + [VMEM] * len(slots),
        out_specs=[VMEM] * parts,
        scratch_shapes=[pltpu.VMEM((images, rows, LANES), jnp.float32)],
        compiler_params=PARAMS,
        cost_estimate=COST,
        name="fold_slots",
    )(table, *slots)


def local_kernel(first, half, cap, tab_ref, *refs):
    fold(first, half, cap, tab_ref, refs[:-1], refs[-1])


def fold_local(table, slots, first, images, half, cap):
    rows = slots[0].shape[-2]
    return pl.pallas_call(
        functools.partial(local_kernel, first, half, cap),
        out_shape=jax.ShapeDtypeStruct((images, rows, LANES), jnp.float32),
        in_specs=[SMEM] + [VMEM] * len(slots),
        out_specs=VMEM,
        compiler_params=PARAMS,
        cost_estimate=COST,
        name="fold_local",
    )(table, *slots)


def adam_step(values, moment, second, gradient, step_rate):
    step_count = START + 1
    moment = beta_one * moment + (1.0 - beta_one) * gradient
    second = beta_two * second + (1.0 - beta_two) * gradient * gradient
    fix_one = 1.0 - beta_one**step_count
    fix_two = 1.0 - beta_two**step_count
    values = values - step_rate * (moment / fix_one) / (jnp.sqrt(second / fix_two) + adam_eps)
    return (values, moment, second)


def depth_kernel(bound, local_ref, far_ref, x_ref, m_ref, s_ref, *refs):
    nx_ref, nm_ref, ns_ref, grad = refs[-4:]
    images, rows, _ = local_ref.shape
    for i in range(images):
        grad[i * rows : (i + 1) * rows] = local_ref[i] * SLOT_UNIT + decode(
            far_ref[i], bound
        )
    for t in range(rows):
        here = slice(t * LANES, (t + 1) * LANES)
        gradient = grad[pl.ds(t, images, stride=rows), :]
        nx_ref[:, here], nm_ref[:, here], ns_ref[:, here] = adam_step(
            x_ref[:, here], m_ref[:, here], s_ref[:, here], gradient, depth_rate
        )


def update_depths(local, far, values, moment, second, bound, chunk, done):
    images, rows, _ = far.shape
    block = 48
    steps = rows // block
    first = chunk * steps
    wide = pl.BlockSpec((images, block * LANES), lambda t: (0, first + t))
    return pl.pallas_call(
        functools.partial(depth_kernel, bound),
        grid=(steps,),
        out_shape=[jax.ShapeDtypeStruct(values.shape, jnp.float32)] * 3,
        in_specs=[
            pl.BlockSpec((images, block, LANES), lambda t: (0, first + t, 0)),
            pl.BlockSpec((images, block, LANES), lambda t: (0, t, 0)),
            wide,
            wide,
            wide,
        ]
        + [pl.BlockSpec(memory_space=pl.ANY)] * len(done),
        out_specs=[wide, wide, wide],
        input_output_aliases={5 + i: i for i in range(len(done))},
        scratch_shapes=[pltpu.VMEM((images * block, LANES), jnp.float32)],
        compiler_params=PARAMS,
        cost_estimate=COST,
        name="update_depths",
    )(local, far, values, moment, second, *done)


def rotation(first, middle, last):
    inverse = 1.0 / (1.0 + first * first + middle * middle + last * last)
    return (
        (1.0 + first * first - middle * middle - last * last) * inverse,
        2.0 * (first * middle - last) * inverse,
        2.0 * (first * last + middle) * inverse,
        2.0 * (first * middle + last) * inverse,
        (1.0 - first * first + middle * middle - last * last) * inverse,
        2.0 * (middle * last - first) * inverse,
        2.0 * (first * last - middle) * inverse,
        2.0 * (middle * last + first) * inverse,
        (1.0 - first * first - middle * middle + last * last) * inverse,
    )


def cross(a, b):
    return [a[(j + 1) % 3] * b[(j + 2) % 3] - a[(j + 2) % 3] * b[(j + 1) % 3] for j in range(3)]


def turn_gradient(spin, torque):
    factor = 2.0 / (1.0 + spin[0] * spin[0] + spin[1] * spin[1] + spin[2] * spin[2])
    swing = cross(spin, torque)
    return [factor * (torque[j] + swing[j]) for j in range(3)]


def view_parts(cam_ref, pose_ref):
    cams = [cam_ref[:, i : i + 1] for i in range(7)]
    poses = [pose_ref[:, i : i + 1] for i in range(7)]
    cam = rotation(cams[1], cams[2], cams[3])
    pose = rotation(poses[0], poses[1], poses[2])
    scale = jnp.exp(poses[6])
    back = jnp.exp(-poses[6])
    gap = [cams[4 + k] - poses[3 + k] for k in range(3)]
    both = [
        [sum(pose[3 * k + j] * cam[3 * k + i] for k in range(3)) for i in range(3)] for j in range(3)
    ]
    matrix = [[both[j][i] * back for i in range(3)] for j in range(3)]
    shift = [sum(pose[3 * k + j] * gap[k] for k in range(3)) * back for j in range(3)]
    return cams, poses, both, pose, scale, matrix, shift


def coef_kernel(images, image_ref, all_ref, pair_ref, out_ref, cam_ref, pose_ref):
    views = cam_ref.shape[0]
    for r in range(views):
        image = image_ref[r % 2, r // 2]
        owner = over(image, images)
        cam_ref[r : r + 1, :] = all_ref[owner, pl.ds(image - owner * images, 1), 0:7]
        pose_ref[r : r + 1, :] = pair_ref[r // 2 : r // 2 + 1, :]
    cams, _, _, _, scale, matrix, shift = view_parts(cam_ref, pose_ref)
    inverse_focal = jnp.exp(-cams[0]) * (1.0 / WIDTH)
    rows = [matrix[j][0] * inverse_focal for j in range(3)]
    rows += [matrix[j][1] * inverse_focal for j in range(3)]
    rows += [matrix[j][2] for j in range(3)]
    rows += shift
    rows += [scale * scale * (1.0 / SLOT_UNIT)]
    for i, row in enumerate(rows):
        out_ref[:, i : i + 1] = row


def view_coefs(pair_images, mail, pair_poses, images):
    views = 2 * pair_poses.shape[0]
    return pl.pallas_call(
        functools.partial(coef_kernel, images),
        out_shape=[
            jax.ShapeDtypeStruct((views, COEFS), jnp.float32),
            jax.ShapeDtypeStruct((views, 7), jnp.float32),
            jax.ShapeDtypeStruct((views, 7), jnp.float32),
        ],
        in_specs=[SMEM, VMEM, VMEM],
        out_specs=[VMEM, VMEM, VMEM],
        cost_estimate=COST,
        name="view_coefs",
    )(pair_images, mail, pair_poses)


def term_kernel(image_ref, cam_ref, pose_ref, *refs):
    cams, poses, both, pose, scale, matrix, shift = view_parts(cam_ref, pose_ref)
    sum_refs, (small_ref, terms, turns) = refs[:-3], refs[-3:]
    views = cam_ref.shape[0]
    sums = jnp.sum(sum(ref[...] for ref in sum_refs), axis=2)
    sums = [sums[:, i : i + 1] for i in range(SUMS)]
    square = scale * scale
    force, torque, stretch, drawn, lever = sums[0:3], sums[3:6], sums[6], sums[7], sums[8:11]
    push = [scale * sum(pose[3 * k + j] * force[j] for j in range(3)) for k in range(3)]
    swing = cross(shift, force)
    arm = [torque[j] - swing[j] for j in range(3)]
    camera_torque = [square * sum(both[j][i] * arm[j] for j in range(3)) for i in range(3)]
    pose_torque = [-square * torque[j] for j in range(3)]
    focal = -square * (drawn - sum(matrix[j][2] * lever[j] for j in range(3)))
    camera = [focal] + turn_gradient(cams[1:4], camera_torque) + push
    posed = (
        turn_gradient(poses[0:3], pose_torque) + [-value for value in push] + [-square * stretch]
    )
    terms[...] = jnp.zeros_like(terms)
    turns[...] = jnp.zeros_like(turns)
    for i in range(7):
        terms[:, i : i + 1] = camera[i]
        turns[:, i : i + 1] = posed[i]
    both_views = turns[pl.ds(0, views // 2, stride=2), :] + turns[pl.ds(1, views // 2, stride=2), :]
    images = small_ref.shape[0] - views // 2
    small_ref[0:images] = jnp.zeros((images, 7), jnp.float32)
    for r in range(views):
        here = pl.ds(image_ref[r % 2, r // 2], 1)
        small_ref[here, :] += terms[r : r + 1, 0:7]
    small_ref[images:] = both_views[:, 0:7]


def view_terms(pair_images, cams, poses, sums, images):
    views = cams.shape[0]
    return pl.pallas_call(
        term_kernel,
        out_shape=jax.ShapeDtypeStruct((images + views // 2, 7), jnp.float32),
        in_specs=[SMEM] + [VMEM] * (2 + len(sums)),
        out_specs=VMEM,
        scratch_shapes=[pltpu.VMEM((views, LANES), jnp.float32)] * 2,
        cost_estimate=COST,
        name="view_terms",
    )(pair_images, cams, poses, *sums)


def small_kernel(mail_ref, pose_ref, *refs):
    values, outs = refs[:6], refs[6:]
    camera_grad = jnp.sum(mail_ref[...], axis=0) * (1.0 / NPIX)
    pose_grad = pose_ref[...] * (1.0 / NPIX)
    for i, (gradient, rate) in enumerate(((camera_grad, camera_rate), (pose_grad, pose_rate))):
        new = adam_step(*(ref[...] for ref in values[3 * i : 3 * i + 3]), gradient, rate)
        for ref, value in zip(outs[3 * i : 3 * i + 3], new):
            ref[...] = value


def update_small(mail, pose_grad, cameras, poses):
    return pl.pallas_call(
        small_kernel,
        out_shape=[jax.ShapeDtypeStruct(value.shape, jnp.float32) for value in cameras + poses],
        in_specs=[VMEM] * 8,
        out_specs=[VMEM] * 6,
        cost_estimate=COST,
        name="update_small",
    )(mail, pose_grad, *cameras, *poses)


def body(
    pair_images,
    depths,
    depth_moment,
    depth_second,
    cameras,
    camera_moment,
    camera_second,
    pair_poses,
    pair_moment,
    pair_second,
    pointmaps,
    confidence,
):
    shards = lax.axis_size("img")
    half = shards // 2
    me = lax.axis_index("img")
    rep = lax.axis_index("rep")
    images, row_len = depths.shape
    pairs = pair_images.shape[0]
    requests = 2 * pairs
    cap = max(2, 3 * pairs // shards)
    rows = row_len // LANES
    far_bound = VIEW_BOUND * half * cap

    def swap(value, k):
        return lax.ppermute(value, "img", [(i, i ^ k) for i in range(shards)])

    slots = half * cap

    def exchange(values):
        return [values[0]] + [swap(values[k], k) for k in range(1, half)]

    tie = lax.optimization_barrier

    names = pair_images.T
    letters = letters_of(names, cameras, shards)
    codes = jnp.round((depths - DEPTH_MID) * (1.0 / DEPTH_STEP)).astype(INTS)
    codes = codes.reshape(images, rows, LANES)
    first = rows // 2
    parts = [codes[:, :first], codes[:, first:]]
    letters, parts[1:] = tie((letters, parts[1:]))
    mail = lax.all_to_all(letters, "img", 0, 0, tiled=True)
    far = [swap(part, half) for part in parts]

    lists = mail[:, images, :requests].astype(jnp.int32)
    table = slot_tables(me.reshape(1), lists, half, cap, images)
    near = pack_slots(table, [codes], 0, half, cap)
    mail, near = tie((mail, near))
    near = exchange(near)
    coefs, cams, poses = view_coefs(names, mail, pair_poses, images)
    row = rep * (row_len // WIDTH)
    row = (row.astype(jnp.float32) + (0.5 - 0.5 * HEIGHT)).reshape(1)
    views, slopes = prepare_views(row, coefs, pointmaps, confidence)
    far, slopes = tie((far, slopes))
    asked = exchange(pack_slots(table, far, slots, half, cap))

    near_sums = view_sums(table, coefs, row, views, near, 2 * slots, half, cap)
    near_grads = depth_grads(table, slopes, near, 2 * slots, half, cap, False)
    asked, near_sums, near_grads = tie((asked, near_sums, near_grads))
    far_grads = depth_grads(table, slopes, asked, 3 * slots, half, cap, False)
    asked, far_grads = tie((asked, far_grads))
    back = exchange(far_grads)
    far_sums = view_sums(table, coefs, row, views, asked, 3 * slots, half, cap)
    back, far_sums = tie((back, far_sums))
    folded = fold_slots(table, back, slots, images, cap, far_bound, 1)
    folded, far_sums = tie((folded, far_sums))
    far_codes = [swap(part, half) for part in folded]
    small = view_terms(names, cams, poses, [near_sums, far_sums], shards * images)
    near_grads, small = tie((near_grads, small))
    near_total = fold_local(table, exchange(near_grads), 0, images, half, cap)
    done = []
    for c in range(1):
        done = update_depths(
            near_total, far_codes[c], depths, depth_moment, depth_second, far_bound, c, done
        )

    bit = 1
    while bit < lax.axis_size("rep"):
        small = small + lax.ppermute(
            small, "rep", [(i, i ^ bit) for i in range(lax.axis_size("rep"))]
        )
        bit *= 2
    camera_mail = lax.all_to_all(
        small[: shards * images].reshape(shards, images, 7), "img", 0, 0, tiled=True
    )
    camera_mail, done = tie((camera_mail, done))
    new = update_small(
        camera_mail,
        small[shards * images :].T,
        [cameras, camera_moment, camera_second],
        [pair_poses.T, pair_moment.T, pair_second.T],
    )
    return (*done, *new[:3], *(value.T for value in new[3:]))


def solution(mesh):
    return jax.shard_map(
        body,
        mesh=mesh,
        in_specs=(
            P("img", None),
            P("img", "rep"),
            P("img", "rep"),
            P("img", "rep"),
            P("img", None),
            P("img", None),
            P("img", None),
            P("img", None),
            P("img", None),
            P("img", None),
            P("img", None, None, "rep"),
            P("img", None, "rep"),
        ),
        out_specs=(
            P("img", "rep"),
            P("img", "rep"),
            P("img", "rep"),
            P("img", None),
            P("img", None),
            P("img", None),
            P("img", None),
            P("img", None),
            P("img", None),
        ),
        check_vma=False,
    )
```

```python
import functools
import math

import jax
import jax.numpy as jnp
from jax import lax
from jax.experimental import pallas as pl
from jax.experimental.pallas import tpu as pltpu
from jax.sharding import PartitionSpec as P

HEIGHT = 288
WIDTH = 512
START = 50
NPIX = 147456
LANES = 128
SWAP_PARTS = 2

beta_one = 0.9
beta_two = 0.999
adam_eps = 1e-08
depth_rate = 0.05
camera_rate = 0.01
pose_rate = 0.01

DEPTH_MID = 2.25
DEPTH_STEP = 1.75 / 32766.0
VIEW_BOUND = 340.0
SLOT_UNIT = VIEW_BOUND / 32766.0**2
CODE_UNIT = 8.0
INTS = jnp.int16
SUMS = 11
COEFS = 16

SMEM = pl.BlockSpec(memory_space=pltpu.SMEM)
VMEM = pl.BlockSpec(memory_space=pltpu.VMEM)
COST = pl.CostEstimate(flops=1, bytes_accessed=1, transcendentals=0)
PARAMS = pltpu.CompilerParams(vmem_limit_bytes=16 * 1024 * 1024)


def encode_slot(value):
    root = value * lax.rsqrt(jnp.maximum(jnp.abs(value), 1e-20))
    return jnp.round(root).astype(jnp.int32).astype(INTS)


def decode_slot(code):
    root = code.astype(jnp.int32).astype(jnp.float32)
    return root * jnp.abs(root)


def code_scale(bound):
    return 32766.0 / math.log2(1.0 + bound / CODE_UNIT)


def encode(magnitude, negative, bound):
    steps = (jnp.log2(1.0 + magnitude) * code_scale(bound) + 0.5).astype(jnp.int32)
    steps = jnp.minimum(steps, 32767)
    return jnp.where(negative, -steps, steps).astype(INTS)


def decode(code, bound):
    steps = code.astype(jnp.int32)
    size = jnp.abs(steps).astype(jnp.float32) * (1.0 / code_scale(bound))
    value = CODE_UNIT * jnp.exp2(size) - CODE_UNIT
    return jnp.where(steps < 0, -value, value)


def letter_kernel(image_ref, camera_ref, out_ref):
    shards, rows, _ = out_ref.shape
    lane = lax.broadcasted_iota(jnp.int32, (1, LANES), 1)
    names = jnp.zeros((1, LANES), jnp.int32)
    for r in range(2 * image_ref.shape[1]):
        names = jnp.where(lane == r, image_ref[r % 2, r // 2], names)
    for i in range(shards):
        out_ref[i, 0 : rows - 1, 0:7] = camera_ref[...]
        out_ref[i, rows - 1 : rows] = names.astype(jnp.float32)


def letters_of(pair_images, cameras, shards):
    images = cameras.shape[0]
    return pl.pallas_call(
        letter_kernel,
        out_shape=jax.ShapeDtypeStruct((shards, images + 1, LANES), jnp.float32),
        in_specs=[SMEM, VMEM],
        out_specs=VMEM,
        cost_estimate=COST,
        name="letters_of",
    )(pair_images, cameras)


def over(number, size):
    if size & (size - 1):
        return lax.div(number, size)
    return lax.shift_right_logical(number, size.bit_length() - 1)


def table_kernel(half, cap, images, me_ref, *refs):
    list_ref, tab_ref, count_ref = refs
    me = me_ref[0]
    shards = 2 * half
    spare = 2 * shards
    requests = list_ref.shape[1]

    @pl.loop(0, (spare + 1) * cap, unroll=8)
    def _(i):
        tab_ref[i] = -1

    @pl.loop(0, spare + 1, unroll=8)
    def _(i):
        count_ref[i] = 0

    def put(cell, value):
        rank = count_ref[cell]
        tab_ref[cell * cap + jnp.minimum(rank, cap - 1)] = value
        count_ref[cell] = rank + 1

    @pl.loop(0, requests)
    def _(r):
        for k in range(half):
            image = list_ref[me ^ k, r]
            owner = over(image, images)
            cell = jnp.where(owner == me, k, jnp.where(owner == (me ^ half), half + k, spare))
            put(cell, image - owner * images)
        put(shards + (over(list_ref[me, r], images) ^ me), r)


def slot_tables(me, lists, half, cap, images):
    return pl.pallas_call(
        functools.partial(table_kernel, half, cap, images),
        out_shape=jax.ShapeDtypeStruct(((4 * half + 1) * cap,), jnp.int32),
        in_specs=[SMEM, SMEM],
        out_specs=SMEM,
        scratch_shapes=[pltpu.SMEM((4 * half + 1,), jnp.int32)],
        cost_estimate=COST,
        name="slot_tables",
    )(me, lists)


def pack_kernel(first, half, tab_ref, *refs):
    map_refs, slot_refs = refs[:-half], refs[-half:]
    for k, slot_ref in enumerate(slot_refs):

        @pl.loop(0, slot_ref.shape[0])
        def _(c):
            image = jnp.maximum(tab_ref[first + k * slot_ref.shape[0] + c], 0)
            first_row = 0
            for map_ref in map_refs:
                rows = map_ref.shape[1]
                slot_ref[c, first_row : first_row + rows] = map_ref[image]
                first_row += rows


def pack_slots(table, maps, first, half, cap):
    rows = sum(part.shape[1] for part in maps)
    return pl.pallas_call(
        functools.partial(pack_kernel, first, half),
        out_shape=[jax.ShapeDtypeStruct((cap, rows, LANES), INTS)] * half,
        in_specs=[SMEM] + [VMEM] * len(maps),
        out_specs=[VMEM] * half,
        compiler_params=PARAMS,
        cost_estimate=COST,
        name="pack_slots",
    )(table, *maps)


def columns_and_lines(top):
    across = WIDTH // LANES
    line = lax.broadcasted_iota(jnp.int32, (16, LANES), 0)
    lane = lax.broadcasted_iota(jnp.int32, (16, LANES), 1)
    columns = ((line % across) * LANES + lane).astype(jnp.float32) + (0.5 - 0.5 * WIDTH)
    return columns, (line // across).astype(jnp.float32) + top


def ray_start(columns, lines, coef):
    ray = [columns * coef(j) + (lines * coef(3 + j) + coef(6 + j)) for j in range(3)]
    step = [coef(3 + j) * (16.0 * LANES / WIDTH) for j in range(3)]
    return ray, step


def prepare_kernel(row_ref, coef_ref, point_ref, weight_ref, view_ref, slope_ref, wide):
    rows = view_ref.shape[2]
    columns, lines = columns_and_lines(row_ref[0])

    @pl.loop(0, point_ref.shape[0])
    def _(pair):
        for q in range(4):
            source = point_ref.at[pair, q] if q < 3 else weight_ref.at[pair]
            wide[q] = source[...].astype(jnp.float32)
        for v in range(2):
            view = 2 * pair + v

            def coef(i):
                return coef_ref[view, i]

            ray, step = ray_start(columns, lines, coef)
            shift = [coef(9 + j) for j in range(3)]
            gain = coef(12)
            for t in range(0, rows, 16):
                here = slice(t, t + 16)
                part = [wide[q, pl.ds(2 * t + v, 16, stride=2), :] for q in range(4)]
                for q in range(4):
                    view_ref[view, q, here] = part[q].astype(jnp.bfloat16)
                weight = part[3] * gain
                slope = weight * (ray[0] * ray[0] + ray[1] * ray[1] + ray[2] * ray[2])
                rest = [ray[j] * (shift[j] - part[j]) for j in range(3)]
                slope_ref[view, 0, here] = slope * DEPTH_STEP
                slope_ref[view, 1, here] = slope * DEPTH_MID + weight * (
                    rest[0] + rest[1] + rest[2]
                )
                ray = [ray[j] + step[j] for j in range(3)]


def prepare_views(row, coefs, points, weights):
    pairs, _, _, pixels = points.shape
    rows = pixels // LANES
    points = (
        points.transpose(0, 2, 1, 3)
        .reshape(pairs, 3, 2, rows, LANES)
        .transpose(0, 1, 3, 2, 4)
        .reshape(pairs, 3, 2 * rows, LANES)
    )
    weights = (
        weights.reshape(pairs, 2, rows, LANES).transpose(0, 2, 1, 3).reshape(pairs, 2 * rows, LANES)
    )
    return pl.pallas_call(
        prepare_kernel,
        out_shape=[
            jax.ShapeDtypeStruct((2 * pairs, 4, rows, LANES), jnp.bfloat16),
            jax.ShapeDtypeStruct((2 * pairs, 2, rows, LANES), jnp.float32),
        ],
        in_specs=[SMEM, SMEM, VMEM, VMEM],
        out_specs=[VMEM, VMEM],
        scratch_shapes=[pltpu.VMEM((4, 2 * rows, LANES), jnp.float32)],
        compiler_params=PARAMS,
        cost_estimate=COST,
        name="prepare_views",
    )(row, coefs, points, weights)


def slots_at(refs, k, tab_ref):
    return refs[k] if len(refs) > 1 else refs[0].at[k ^ tab_ref[tab_ref.shape[0] - 1]]


def grad_kernel(first, ks, cap, tab_ref, slope_ref, *refs):
    depth_refs, grad_refs = refs[: len(ks)], refs[len(ks) :]
    rows = slope_ref.shape[2]
    for k, depth_ref, grad_ref in zip(ks, depth_refs, grad_refs):

        @pl.loop(0, cap)
        def _(c):
            view = tab_ref[first + k * cap + c]

            @pl.when(view >= 0)
            def _():
                for t in range(0, rows, 16):
                    here = slice(t, t + 16)
                    code = depth_ref[c, here].astype(jnp.int32).astype(jnp.float32)
                    along = code * slope_ref[view, 0, here] + slope_ref[view, 1, here]
                    grad_ref[c, here] = encode_slot(along)


def depth_grads(table, slopes, depths, first, ks, cap):
    rows = slopes.shape[2]
    return pl.pallas_call(
        functools.partial(grad_kernel, first, ks, cap),
        out_shape=[jax.ShapeDtypeStruct((cap, rows, LANES), INTS)] * len(ks),
        in_specs=[SMEM] + [VMEM] * (1 + len(ks)),
        out_specs=[VMEM] * len(ks),
        compiler_params=PARAMS,
        cost_estimate=COST,
        name="depth_grads",
    )(table, slopes, *depths)


def sum_kernel(first, half, cap, tab_ref, coef_ref, row_ref, view_ref, *refs):
    depth_refs = refs[:-2]
    sum_ref, depth_all = refs[-2:]
    slots, rows, _ = depth_all.shape
    for k in range(half):
        depth_ref = depth_refs[k]
        depth_all[k * cap : (k + 1) * cap] = depth_ref[...]
    sum_ref[...] = jnp.zeros_like(sum_ref)
    columns, lines = columns_and_lines(row_ref[0])

    @pl.loop(0, slots)
    def _(s):
        view = tab_ref[first + s]

        @pl.when(view >= 0)
        def _():
            def coef(i):
                return coef_ref[view, i]

            ray, step = ray_start(columns, lines, coef)
            shift = [coef(9 + j) for j in range(3)]
            totals = [None] * SUMS

            def add(i, value):
                value = value[:8] + value[8:]
                totals[i] = value if totals[i] is None else totals[i] + value

            for t in range(0, rows, 16):
                here = slice(t, t + 16)
                point = [view_ref[view, j, here].astype(jnp.float32) for j in range(3)]
                weight = view_ref[view, 3, here].astype(jnp.float32)
                depth = (
                    depth_all[s, here].astype(jnp.int32).astype(jnp.float32) * DEPTH_STEP
                    + DEPTH_MID
                )
                pull = [weight * (depth * ray[j] + (shift[j] - point[j])) for j in range(3)]
                along = pull[0] * ray[0] + pull[1] * ray[1] + pull[2] * ray[2]
                for j in range(3):
                    add(j, pull[j])
                    add(8 + j, depth * pull[j])
                    a, b = (j + 1) % 3, (j + 2) % 3
                    add(3 + j, point[a] * pull[b] - point[b] * pull[a])
                add(6, point[0] * pull[0] + point[1] * pull[1] + point[2] * pull[2])
                add(7, depth * along)
                ray = [ray[j] + step[j] for j in range(3)]
            for i in range(SUMS):
                sum_ref[view, i : i + 1] = jnp.sum(totals[i], axis=0, keepdims=True)


def view_sums(table, coefs, row, views, depths, first, half, cap):
    rows = depths[0].shape[1]
    return pl.pallas_call(
        functools.partial(sum_kernel, first, half, cap),
        out_shape=jax.ShapeDtypeStruct((views.shape[0], COEFS, LANES), jnp.float32),
        in_specs=[SMEM, SMEM, SMEM] + [VMEM] * (1 + len(depths)),
        out_specs=VMEM,
        scratch_shapes=[pltpu.VMEM((half * cap, rows, LANES), INTS)],
        compiler_params=PARAMS,
        cost_estimate=COST,
        name="view_sums",
    )(table, coefs, row, views, *depths)


def fold(first, ks, cap, tab_ref, slot_refs, total_ref):
    for k, slot_ref in zip(ks, slot_refs):

        @pl.loop(0, cap)
        def _(c):
            image = tab_ref[first + k * cap + c]

            @pl.when(image >= 0)
            def _():
                total_ref[image] += decode_slot(slot_ref[c])


def total_kernel(first, ks, cap, tab_ref, *refs):
    refs[-1][...] = jnp.zeros_like(refs[-1])
    fold(first, ks, cap, tab_ref, refs[:-1], refs[-1])


def fold_totals(table, slots, first, ks, images, cap):
    rows = slots[0].shape[1]
    return pl.pallas_call(
        functools.partial(total_kernel, first, ks, cap),
        out_shape=jax.ShapeDtypeStruct((images, rows, LANES), jnp.float32),
        in_specs=[SMEM] + [VMEM] * len(slots),
        out_specs=VMEM,
        compiler_params=PARAMS,
        cost_estimate=COST,
        name="fold_totals",
    )(table, *slots)


def add_code_kernel(first, ks, cap, bound, tab_ref, total_ref, *refs):
    slot_refs, out_ref, more = refs[:-2], refs[-2], refs[-1]
    more[...] = total_ref[...]
    fold(first, ks, cap, tab_ref, slot_refs, more)

    @pl.loop(0, more.shape[0])
    def _(i):
        value = more[i]
        out_ref[i] = encode(jnp.abs(value) * (SLOT_UNIT / CODE_UNIT), value < 0.0, bound)


def fold_codes(table, totals, slots, first, ks, cap, bound):
    return pl.pallas_call(
        functools.partial(add_code_kernel, first, ks, cap, bound),
        out_shape=jax.ShapeDtypeStruct(totals.shape, INTS),
        in_specs=[SMEM] + [VMEM] * (1 + len(slots)),
        out_specs=VMEM,
        scratch_shapes=[pltpu.VMEM(totals.shape, jnp.float32)],
        compiler_params=PARAMS,
        cost_estimate=COST,
        name="fold_codes",
    )(table, totals, *slots)


def adam_step(values, moment, second, gradient, step_rate):
    step_count = START + 1
    moment = beta_one * moment + (1.0 - beta_one) * gradient
    second = beta_two * second + (1.0 - beta_two) * gradient * gradient
    pace = step_rate / (1.0 - beta_one**step_count)
    grown = second * (1.0 / (1.0 - beta_two**step_count))
    values = values - (moment * pace) / (grown * lax.rsqrt(grown) + adam_eps)
    return (values, moment, second)


def depth_kernel(bound, local_ref, far_ref, x_ref, m_ref, s_ref, *refs):
    nx_ref, nm_ref, ns_ref, grad = refs[-4:]
    images, rows, _ = local_ref.shape
    for i in range(images):
        grad[i * rows : (i + 1) * rows] = local_ref[i] * SLOT_UNIT + decode(
            far_ref[i], bound
        )
    for t in range(rows):
        here = slice(t * LANES, (t + 1) * LANES)
        gradient = grad[pl.ds(t, images, stride=rows), :]
        nx_ref[:, here], nm_ref[:, here], ns_ref[:, here] = adam_step(
            x_ref[:, here], m_ref[:, here], s_ref[:, here], gradient, depth_rate
        )


def update_depths(local, far, values, moment, second, bound, chunk, done):
    images, rows, _ = far.shape
    block = 48
    steps = rows // block
    first = chunk * steps
    wide = pl.BlockSpec((images, block * LANES), lambda t: (0, first + t))
    return pl.pallas_call(
        functools.partial(depth_kernel, bound),
        grid=(steps,),
        out_shape=[jax.ShapeDtypeStruct(values.shape, jnp.float32)] * 3,
        in_specs=[
            pl.BlockSpec((images, block, LANES), lambda t: (0, first + t, 0)),
            pl.BlockSpec((images, block, LANES), lambda t: (0, t, 0)),
            wide,
            wide,
            wide,
        ]
        + [pl.BlockSpec(memory_space=pl.ANY)] * len(done),
        out_specs=[wide, wide, wide],
        input_output_aliases={5 + i: i for i in range(len(done))},
        scratch_shapes=[pltpu.VMEM((images * block, LANES), jnp.float32)],
        compiler_params=PARAMS,
        cost_estimate=COST,
        name="update_depths",
    )(local, far, values, moment, second, *done)


def rotation(first, middle, last):
    inverse = 1.0 / (1.0 + first * first + middle * middle + last * last)
    return (
        (1.0 + first * first - middle * middle - last * last) * inverse,
        2.0 * (first * middle - last) * inverse,
        2.0 * (first * last + middle) * inverse,
        2.0 * (first * middle + last) * inverse,
        (1.0 - first * first + middle * middle - last * last) * inverse,
        2.0 * (middle * last - first) * inverse,
        2.0 * (first * last - middle) * inverse,
        2.0 * (middle * last + first) * inverse,
        (1.0 - first * first - middle * middle + last * last) * inverse,
    )


def cross(a, b):
    return [a[(j + 1) % 3] * b[(j + 2) % 3] - a[(j + 2) % 3] * b[(j + 1) % 3] for j in range(3)]


def turn_gradient(spin, torque):
    factor = 2.0 / (1.0 + spin[0] * spin[0] + spin[1] * spin[1] + spin[2] * spin[2])
    swing = cross(spin, torque)
    return [factor * (torque[j] + swing[j]) for j in range(3)]


def view_parts(cam_ref, pose_ref):
    cams = [cam_ref[:, i : i + 1] for i in range(7)]
    poses = [pose_ref[:, i : i + 1] for i in range(7)]
    cam = rotation(cams[1], cams[2], cams[3])
    pose = rotation(poses[0], poses[1], poses[2])
    scale = jnp.exp(poses[6])
    back = jnp.exp(-poses[6])
    gap = [cams[4 + k] - poses[3 + k] for k in range(3)]
    both = [
        [sum(pose[3 * k + j] * cam[3 * k + i] for k in range(3)) for i in range(3)] for j in range(3)
    ]
    matrix = [[both[j][i] * back for i in range(3)] for j in range(3)]
    shift = [sum(pose[3 * k + j] * gap[k] for k in range(3)) * back for j in range(3)]
    return cams, poses, both, pose, scale, matrix, shift


def coef_kernel(images, image_ref, all_ref, pair_ref, out_ref, cam_ref, pose_ref):
    views = cam_ref.shape[0]
    for r in range(views):
        image = image_ref[r % 2, r // 2]
        owner = over(image, images)
        cam_ref[r : r + 1, :] = all_ref[owner, pl.ds(image - owner * images, 1), 0:7]
        pose_ref[r : r + 1, :] = pair_ref[r // 2 : r // 2 + 1, :]
    cams, _, _, _, scale, matrix, shift = view_parts(cam_ref, pose_ref)
    inverse_focal = jnp.exp(-cams[0]) * (1.0 / WIDTH)
    rows = [matrix[j][0] * inverse_focal for j in range(3)]
    rows += [matrix[j][1] * inverse_focal for j in range(3)]
    rows += [matrix[j][2] for j in range(3)]
    rows += shift
    rows += [scale * scale * (1.0 / SLOT_UNIT)]
    for i, row in enumerate(rows):
        out_ref[:, i : i + 1] = row


def view_coefs(pair_images, mail, pair_poses, images):
    views = 2 * pair_poses.shape[0]
    return pl.pallas_call(
        functools.partial(coef_kernel, images),
        out_shape=[
            jax.ShapeDtypeStruct((views, COEFS), jnp.float32),
            jax.ShapeDtypeStruct((views, 7), jnp.float32),
            jax.ShapeDtypeStruct((views, 7), jnp.float32),
        ],
        in_specs=[SMEM, VMEM, VMEM],
        out_specs=[VMEM, VMEM, VMEM],
        cost_estimate=COST,
        name="view_coefs",
    )(pair_images, mail, pair_poses)


def term_kernel(image_ref, cam_ref, pose_ref, *refs):
    cams, poses, both, pose, scale, matrix, shift = view_parts(cam_ref, pose_ref)
    sum_refs, (small_ref, terms, turns) = refs[:-3], refs[-3:]
    views = cam_ref.shape[0]
    sums = jnp.sum(sum(ref[...] for ref in sum_refs), axis=2)
    sums = [sums[:, i : i + 1] for i in range(SUMS)]
    square = scale * scale
    force, torque, stretch, drawn, lever = sums[0:3], sums[3:6], sums[6], sums[7], sums[8:11]
    push = [scale * sum(pose[3 * k + j] * force[j] for j in range(3)) for k in range(3)]
    swing = cross(shift, force)
    arm = [torque[j] - swing[j] for j in range(3)]
    camera_torque = [square * sum(both[j][i] * arm[j] for j in range(3)) for i in range(3)]
    pose_torque = [-square * torque[j] for j in range(3)]
    focal = -square * (drawn - sum(matrix[j][2] * lever[j] for j in range(3)))
    camera = [focal] + turn_gradient(cams[1:4], camera_torque) + push
    posed = (
        turn_gradient(poses[0:3], pose_torque) + [-value for value in push] + [-square * stretch]
    )
    terms[...] = jnp.zeros_like(terms)
    turns[...] = jnp.zeros_like(turns)
    for i in range(7):
        terms[:, i : i + 1] = camera[i]
        turns[:, i : i + 1] = posed[i]
    both_views = turns[pl.ds(0, views // 2, stride=2), :] + turns[pl.ds(1, views // 2, stride=2), :]
    images = small_ref.shape[0] - views // 2
    small_ref[0:images] = jnp.zeros((images, 7), jnp.float32)
    for r in range(views):
        here = pl.ds(image_ref[r % 2, r // 2], 1)
        small_ref[here, :] += terms[r : r + 1, 0:7]
    small_ref[images:] = both_views[:, 0:7]


def view_terms(pair_images, cams, poses, sums, images):
    views = cams.shape[0]
    return pl.pallas_call(
        term_kernel,
        out_shape=jax.ShapeDtypeStruct((images + views // 2, 7), jnp.float32),
        in_specs=[SMEM] + [VMEM] * (2 + len(sums)),
        out_specs=VMEM,
        scratch_shapes=[pltpu.VMEM((views, LANES), jnp.float32)] * 2,
        cost_estimate=COST,
        name="view_terms",
    )(pair_images, cams, poses, *sums)


def small_kernel(mail_ref, pose_ref, *refs):
    values, outs = refs[:6], refs[6:]
    camera_grad = jnp.sum(mail_ref[...], axis=0) * (1.0 / NPIX)
    pose_grad = pose_ref[...] * (1.0 / NPIX)
    for i, (gradient, rate) in enumerate(((camera_grad, camera_rate), (pose_grad, pose_rate))):
        new = adam_step(*(ref[...] for ref in values[3 * i : 3 * i + 3]), gradient, rate)
        for ref, value in zip(outs[3 * i : 3 * i + 3], new):
            ref[...] = value


def update_small(mail, pose_grad, cameras, poses):
    return pl.pallas_call(
        small_kernel,
        out_shape=[jax.ShapeDtypeStruct(value.shape, jnp.float32) for value in cameras + poses],
        in_specs=[VMEM] * 8,
        out_specs=[VMEM] * 6,
        cost_estimate=COST,
        name="update_small",
    )(mail, pose_grad, *cameras, *poses)


def body(
    pair_images,
    depths,
    depth_moment,
    depth_second,
    cameras,
    camera_moment,
    camera_second,
    pair_poses,
    pair_moment,
    pair_second,
    pointmaps,
    confidence,
):
    shards = lax.axis_size("img")
    half = shards // 2
    me = lax.axis_index("img")
    rep = lax.axis_index("rep")
    images, row_len = depths.shape
    pairs = pair_images.shape[0]
    requests = 2 * pairs
    cap = max(2, 3 * pairs // shards)
    rows = row_len // LANES
    far_bound = VIEW_BOUND * half * cap

    def swap(value, k):
        return lax.ppermute(value, "img", [(i, i ^ k) for i in range(shards)])

    slots = half * cap

    def exchange(values):
        return [values[0]] + [swap(values[k], k) for k in range(1, half)]

    tie = lax.optimization_barrier

    names = pair_images.T
    letters = letters_of(names, cameras, shards)
    codes = jnp.round((depths - DEPTH_MID) * (1.0 / DEPTH_STEP)).astype(INTS)
    codes = codes.reshape(images, rows, LANES)
    first = rows // 2
    parts = [codes[:, :first], codes[:, first:]]
    letters, parts[1:] = tie((letters, parts[1:]))
    mail = lax.all_to_all(letters, "img", 0, 0, tiled=True)
    far = [swap(part, half) for part in parts]

    lists = mail[:, images, :requests].astype(jnp.int32)
    table = slot_tables(me.reshape(1), lists, half, cap, images)
    near = pack_slots(table, [codes], 0, half, cap)
    mail, near = tie((mail, near))
    near = exchange(near)
    coefs, cams, poses = view_coefs(names, mail, pair_poses, images)
    row = rep * (row_len // WIDTH)
    row = (row.astype(jnp.float32) + (0.5 - 0.5 * HEIGHT)).reshape(1)
    views, slopes = prepare_views(row, coefs, pointmaps, confidence)
    far, slopes = tie((far, slopes))
    asked = exchange(pack_slots(table, far, slots, half, cap))

    near_sums = view_sums(table, coefs, row, views, near, 2 * slots, half, cap)
    every, early, late = range(half), range(half - 1), range(half - 1, half)
    near_grads = depth_grads(table, slopes, near, 2 * slots, every, cap)
    first_asked, near_sums, near_grads = tie((asked[:-1], near_sums, near_grads))
    far_grads = depth_grads(table, slopes, first_asked, 3 * slots, early, cap)
    last_asked, _ = tie((asked[-1:], far_grads))
    last_grads = depth_grads(table, slopes, last_asked, 3 * slots, late, cap)
    back = exchange([*far_grads, *last_grads])
    asked, _ = tie((asked, last_grads))
    far_sums = view_sums(table, coefs, row, views, asked, 3 * slots, half, cap)
    first_back, far_sums = tie((back[:-1], far_sums))
    totals = fold_totals(table, first_back, slots, early, images, cap)
    last_back, totals = tie((back[-1:], totals))
    folded = [fold_codes(table, totals, last_back, slots, late, cap, far_bound)]
    folded, far_sums = tie((folded, far_sums))
    far_codes = [swap(part, half) for part in folded]
    small = view_terms(names, cams, poses, [near_sums, far_sums], shards * images)
    near_grads, small = tie((near_grads, small))
    near_total = fold_totals(table, exchange(near_grads), 0, every, images, cap)
    done = []
    for c in range(1):
        done = update_depths(
            near_total, far_codes[c], depths, depth_moment, depth_second, far_bound, c, done
        )

    bit = 1
    while bit < lax.axis_size("rep"):
        small = small + lax.ppermute(
            small, "rep", [(i, i ^ bit) for i in range(lax.axis_size("rep"))]
        )
        bit *= 2
    camera_mail = lax.all_to_all(
        small[: shards * images].reshape(shards, images, 7), "img", 0, 0, tiled=True
    )
    camera_mail, done = tie((camera_mail, done))
    new = update_small(
        camera_mail,
        small[shards * images :].T,
        [cameras, camera_moment, camera_second],
        [pair_poses.T, pair_moment.T, pair_second.T],
    )
    return (*done, *new[:3], *(value.T for value in new[3:]))


def solution(mesh):
    return jax.shard_map(
        body,
        mesh=mesh,
        in_specs=(
            P("img", None),
            P("img", "rep"),
            P("img", "rep"),
            P("img", "rep"),
            P("img", None),
            P("img", None),
            P("img", None),
            P("img", None),
            P("img", None),
            P("img", None),
            P("img", None, None, "rep"),
            P("img", None, "rep"),
        ),
        out_specs=(
            P("img", "rep"),
            P("img", "rep"),
            P("img", "rep"),
            P("img", None),
            P("img", None),
            P("img", None),
            P("img", None),
            P("img", None),
            P("img", None),
        ),
        check_vma=False,
    )
```

```python
import functools
import math

import jax
import jax.numpy as jnp
from jax import lax
from jax.experimental import pallas as pl
from jax.experimental.pallas import tpu as pltpu
from jax.sharding import PartitionSpec as P

HEIGHT = 288
WIDTH = 512
START = 50
NPIX = 147456
LANES = 128
SWAP_PARTS = 2

beta_one = 0.9
beta_two = 0.999
adam_eps = 1e-08
depth_rate = 0.05
camera_rate = 0.01
pose_rate = 0.01

DEPTH_MID = 2.25
DEPTH_STEP = 1.75 / 32766.0
VIEW_BOUND = 340.0
SLOT_UNIT = VIEW_BOUND / 32766.0**2
CODE_UNIT = 8.0
INTS = jnp.int16
SUMS = 11
COEFS = 16

SMEM = pl.BlockSpec(memory_space=pltpu.SMEM)
VMEM = pl.BlockSpec(memory_space=pltpu.VMEM)
COST = pl.CostEstimate(flops=1, bytes_accessed=1, transcendentals=0)
PARAMS = pltpu.CompilerParams(vmem_limit_bytes=16 * 1024 * 1024)


def encode_slot(value):
    root = value * lax.rsqrt(jnp.maximum(jnp.abs(value), 1e-20))
    return jnp.round(root).astype(jnp.int32).astype(INTS)


def decode_slot(code):
    root = code.astype(jnp.int32).astype(jnp.float32)
    return root * jnp.abs(root)


def code_scale(bound):
    return 32766.0 / math.log2(1.0 + bound / CODE_UNIT)


def encode(magnitude, negative, bound):
    steps = (jnp.log2(1.0 + magnitude) * code_scale(bound) + 0.5).astype(jnp.int32)
    steps = jnp.minimum(steps, 32767)
    return jnp.where(negative, -steps, steps).astype(INTS)


def decode(code, bound):
    steps = code.astype(jnp.int32)
    size = jnp.abs(steps).astype(jnp.float32) * (1.0 / code_scale(bound))
    value = CODE_UNIT * jnp.exp2(size) - CODE_UNIT
    return jnp.where(steps < 0, -value, value)


def letter_kernel(image_ref, camera_ref, out_ref):
    shards, rows, _ = out_ref.shape
    lane = lax.broadcasted_iota(jnp.int32, (1, LANES), 1)
    names = jnp.zeros((1, LANES), jnp.int32)
    for r in range(2 * image_ref.shape[1]):
        names = jnp.where(lane == r, image_ref[r % 2, r // 2], names)
    for i in range(shards):
        out_ref[i, 0 : rows - 1, 0:7] = camera_ref[...]
        out_ref[i, rows - 1 : rows] = names.astype(jnp.float32)


def letters_of(pair_images, cameras, shards):
    images = cameras.shape[0]
    return pl.pallas_call(
        letter_kernel,
        out_shape=jax.ShapeDtypeStruct((shards, images + 1, LANES), jnp.float32),
        in_specs=[SMEM, VMEM],
        out_specs=VMEM,
        cost_estimate=COST,
        name="letters_of",
    )(pair_images, cameras)


def over(number, size):
    if size & (size - 1):
        return lax.div(number, size)
    return lax.shift_right_logical(number, size.bit_length() - 1)


def table_kernel(half, cap, images, me_ref, *refs):
    list_ref, tab_ref, count_ref = refs
    me = me_ref[0]
    shards = 2 * half
    spare = 2 * shards
    requests = list_ref.shape[1]

    @pl.loop(0, (spare + 1) * cap, unroll=8)
    def _(i):
        tab_ref[i] = -1

    @pl.loop(0, spare + 1, unroll=8)
    def _(i):
        count_ref[i] = 0

    def put(cell, value):
        rank = count_ref[cell]
        tab_ref[cell * cap + jnp.minimum(rank, cap - 1)] = value
        count_ref[cell] = rank + 1

    @pl.loop(0, requests)
    def _(r):
        for k in range(half):
            image = list_ref[me ^ k, r]
            owner = over(image, images)
            cell = jnp.where(owner == me, k, jnp.where(owner == (me ^ half), half + k, spare))
            put(cell, image - owner * images)
        put(shards + (over(list_ref[me, r], images) ^ me), r)


def slot_tables(me, lists, half, cap, images):
    return pl.pallas_call(
        functools.partial(table_kernel, half, cap, images),
        out_shape=jax.ShapeDtypeStruct(((4 * half + 1) * cap,), jnp.int32),
        in_specs=[SMEM, SMEM],
        out_specs=SMEM,
        scratch_shapes=[pltpu.SMEM((4 * half + 1,), jnp.int32)],
        cost_estimate=COST,
        name="slot_tables",
    )(me, lists)


def pack_kernel(first, half, tab_ref, *refs):
    map_refs, slot_refs = refs[:-half], refs[-half:]
    for k, slot_ref in enumerate(slot_refs):

        @pl.loop(0, slot_ref.shape[0])
        def _(c):
            image = jnp.maximum(tab_ref[first + k * slot_ref.shape[0] + c], 0)
            first_row = 0
            for map_ref in map_refs:
                rows = map_ref.shape[1]
                slot_ref[c, first_row : first_row + rows] = map_ref[image]
                first_row += rows


def pack_slots(table, maps, first, half, cap):
    rows = sum(part.shape[1] for part in maps)
    return pl.pallas_call(
        functools.partial(pack_kernel, first, half),
        out_shape=[jax.ShapeDtypeStruct((cap, rows, LANES), INTS)] * half,
        in_specs=[SMEM] + [VMEM] * len(maps),
        out_specs=[VMEM] * half,
        compiler_params=PARAMS,
        cost_estimate=COST,
        name="pack_slots",
    )(table, *maps)


def columns_and_lines(top):
    across = WIDTH // LANES
    line = lax.broadcasted_iota(jnp.int32, (16, LANES), 0)
    lane = lax.broadcasted_iota(jnp.int32, (16, LANES), 1)
    columns = ((line % across) * LANES + lane).astype(jnp.float32) + (0.5 - 0.5 * WIDTH)
    return columns, (line // across).astype(jnp.float32) + top


def ray_start(columns, lines, coef):
    ray = [columns * coef(j) + (lines * coef(3 + j) + coef(6 + j)) for j in range(3)]
    step = [coef(3 + j) * (16.0 * LANES / WIDTH) for j in range(3)]
    return ray, step


def prepare_kernel(row_ref, coef_ref, point_ref, weight_ref, view_ref, slope_ref, wide):
    rows = view_ref.shape[2]
    columns, lines = columns_and_lines(row_ref[0])

    @pl.loop(0, point_ref.shape[0])
    def _(pair):
        for q in range(4):
            source = point_ref.at[pair, q] if q < 3 else weight_ref.at[pair]
            wide[q] = source[...].astype(jnp.float32)
        for v in range(2):
            view = 2 * pair + v

            def coef(i):
                return coef_ref[view, i]

            ray, step = ray_start(columns, lines, coef)
            shift = [coef(9 + j) for j in range(3)]
            gain = coef(12)
            for t in range(0, rows, 16):
                here = slice(t, t + 16)
                part = [wide[q, pl.ds(2 * t + v, 16, stride=2), :] for q in range(4)]
                for q in range(4):
                    view_ref[view, q, here] = part[q].astype(jnp.bfloat16)
                weight = part[3] * gain
                slope = weight * (ray[0] * ray[0] + ray[1] * ray[1] + ray[2] * ray[2])
                rest = [ray[j] * (shift[j] - part[j]) for j in range(3)]
                slope_ref[view, 0, here] = slope * DEPTH_STEP
                slope_ref[view, 1, here] = slope * DEPTH_MID + weight * (
                    rest[0] + rest[1] + rest[2]
                )
                ray = [ray[j] + step[j] for j in range(3)]


def prepare_views(row, coefs, points, weights):
    pairs, _, _, pixels = points.shape
    rows = pixels // LANES
    points = (
        points.transpose(0, 2, 1, 3)
        .reshape(pairs, 3, 2, rows, LANES)
        .transpose(0, 1, 3, 2, 4)
        .reshape(pairs, 3, 2 * rows, LANES)
    )
    weights = (
        weights.reshape(pairs, 2, rows, LANES).transpose(0, 2, 1, 3).reshape(pairs, 2 * rows, LANES)
    )
    return pl.pallas_call(
        prepare_kernel,
        out_shape=[
            jax.ShapeDtypeStruct((2 * pairs, 4, rows, LANES), jnp.bfloat16),
            jax.ShapeDtypeStruct((2 * pairs, 2, rows, LANES), jnp.float32),
        ],
        in_specs=[SMEM, SMEM, VMEM, VMEM],
        out_specs=[VMEM, VMEM],
        scratch_shapes=[pltpu.VMEM((4, 2 * rows, LANES), jnp.float32)],
        compiler_params=PARAMS,
        cost_estimate=COST,
        name="prepare_views",
    )(row, coefs, points, weights)


def slots_at(refs, k, tab_ref):
    return refs[k] if len(refs) > 1 else refs[0].at[k ^ tab_ref[tab_ref.shape[0] - 1]]


def grad_kernel(first, ks, cap, tab_ref, slope_ref, *refs):
    depth_refs, grad_refs = refs[: len(ks)], refs[len(ks) :]
    rows = slope_ref.shape[2]
    for k, depth_ref, grad_ref in zip(ks, depth_refs, grad_refs):

        @pl.loop(0, cap)
        def _(c):
            view = tab_ref[first + k * cap + c]

            @pl.when(view >= 0)
            def _():
                for t in range(0, rows, 16):
                    here = slice(t, t + 16)
                    code = depth_ref[c, here].astype(jnp.int32).astype(jnp.float32)
                    along = code * slope_ref[view, 0, here] + slope_ref[view, 1, here]
                    grad_ref[c, here] = encode_slot(along)


def depth_grads(table, slopes, depths, first, ks, cap):
    rows = slopes.shape[2]
    return pl.pallas_call(
        functools.partial(grad_kernel, first, ks, cap),
        out_shape=[jax.ShapeDtypeStruct((cap, rows, LANES), INTS)] * len(ks),
        in_specs=[SMEM] + [VMEM] * (1 + len(ks)),
        out_specs=[VMEM] * len(ks),
        compiler_params=PARAMS,
        cost_estimate=COST,
        name="depth_grads",
    )(table, slopes, *depths)


def sum_kernel(first, half, cap, tab_ref, coef_ref, row_ref, view_ref, *refs):
    depth_refs = refs[:-2]
    sum_ref, depth_all = refs[-2:]
    slots, rows, _ = depth_all.shape
    for k in range(half):
        depth_ref = depth_refs[k]
        depth_all[k * cap : (k + 1) * cap] = depth_ref[...]
    sum_ref[...] = jnp.zeros_like(sum_ref)
    columns, lines = columns_and_lines(row_ref[0])

    @pl.loop(0, slots)
    def _(s):
        view = tab_ref[first + s]

        @pl.when(view >= 0)
        def _():
            def coef(i):
                return coef_ref[view, i]

            ray, step = ray_start(columns, lines, coef)
            shift = [coef(9 + j) for j in range(3)]
            totals = [None] * SUMS

            def add(i, value):
                value = value[:8] + value[8:]
                totals[i] = value if totals[i] is None else totals[i] + value

            for t in range(0, rows, 16):
                here = slice(t, t + 16)
                point = [view_ref[view, j, here].astype(jnp.float32) for j in range(3)]
                weight = view_ref[view, 3, here].astype(jnp.float32)
                depth = (
                    depth_all[s, here].astype(jnp.int32).astype(jnp.float32) * DEPTH_STEP
                    + DEPTH_MID
                )
                pull = [weight * (depth * ray[j] + (shift[j] - point[j])) for j in range(3)]
                along = pull[0] * ray[0] + pull[1] * ray[1] + pull[2] * ray[2]
                for j in range(3):
                    add(j, pull[j])
                    add(8 + j, depth * pull[j])
                    a, b = (j + 1) % 3, (j + 2) % 3
                    add(3 + j, point[a] * pull[b] - point[b] * pull[a])
                add(6, point[0] * pull[0] + point[1] * pull[1] + point[2] * pull[2])
                add(7, depth * along)
                ray = [ray[j] + step[j] for j in range(3)]
            for i in range(SUMS):
                sum_ref[view, i : i + 1] = jnp.sum(totals[i], axis=0, keepdims=True)


def view_sums(table, coefs, row, views, depths, first, half, cap):
    rows = depths[0].shape[1]
    return pl.pallas_call(
        functools.partial(sum_kernel, first, half, cap),
        out_shape=jax.ShapeDtypeStruct((views.shape[0], COEFS, LANES), jnp.float32),
        in_specs=[SMEM, SMEM, SMEM] + [VMEM] * (1 + len(depths)),
        out_specs=VMEM,
        scratch_shapes=[pltpu.VMEM((half * cap, rows, LANES), INTS)],
        compiler_params=PARAMS,
        cost_estimate=COST,
        name="view_sums",
    )(table, coefs, row, views, *depths)


def fold(first, ks, cap, tab_ref, slot_refs, total_ref):
    for k, slot_ref in zip(ks, slot_refs):

        @pl.loop(0, cap)
        def _(c):
            image = tab_ref[first + k * cap + c]

            @pl.when(image >= 0)
            def _():
                total_ref[image] += decode_slot(slot_ref[c])


def total_kernel(first, ks, cap, tab_ref, *refs):
    refs[-1][...] = jnp.zeros_like(refs[-1])
    fold(first, ks, cap, tab_ref, refs[:-1], refs[-1])


def fold_totals(table, slots, first, ks, images, cap):
    rows = slots[0].shape[1]
    return pl.pallas_call(
        functools.partial(total_kernel, first, ks, cap),
        out_shape=jax.ShapeDtypeStruct((images, rows, LANES), jnp.float32),
        in_specs=[SMEM] + [VMEM] * len(slots),
        out_specs=VMEM,
        compiler_params=PARAMS,
        cost_estimate=COST,
        name="fold_totals",
    )(table, *slots)


def add_code_kernel(first, ks, cap, bound, tab_ref, total_ref, *refs):
    slot_refs, out_ref, more = refs[:-2], refs[-2], refs[-1]
    more[...] = total_ref[...]
    fold(first, ks, cap, tab_ref, slot_refs, more)

    @pl.loop(0, more.shape[0])
    def _(i):
        value = more[i]
        out_ref[i] = encode(jnp.abs(value) * (SLOT_UNIT / CODE_UNIT), value < 0.0, bound)


def fold_codes(table, totals, slots, first, ks, cap, bound):
    return pl.pallas_call(
        functools.partial(add_code_kernel, first, ks, cap, bound),
        out_shape=jax.ShapeDtypeStruct(totals.shape, INTS),
        in_specs=[SMEM] + [VMEM] * (1 + len(slots)),
        out_specs=VMEM,
        scratch_shapes=[pltpu.VMEM(totals.shape, jnp.float32)],
        compiler_params=PARAMS,
        cost_estimate=COST,
        name="fold_codes",
    )(table, totals, *slots)


def adam_step(values, moment, second, gradient, step_rate):
    step_count = START + 1
    moment = beta_one * moment + (1.0 - beta_one) * gradient
    second = beta_two * second + (1.0 - beta_two) * gradient * gradient
    pace = step_rate / (1.0 - beta_one**step_count)
    grown = second * (1.0 / (1.0 - beta_two**step_count))
    values = values - (moment * pace) / (grown * lax.rsqrt(grown) + adam_eps)
    return (values, moment, second)


def depth_kernel(bound, local_ref, far_ref, x_ref, m_ref, s_ref, *refs):
    nx_ref, nm_ref, ns_ref, grad = refs[-4:]
    images, rows, _ = local_ref.shape
    for i in range(images):
        grad[i * rows : (i + 1) * rows] = local_ref[i] * SLOT_UNIT + decode(
            far_ref[i], bound
        )
    for t in range(rows):
        here = slice(t * LANES, (t + 1) * LANES)
        gradient = grad[pl.ds(t, images, stride=rows), :]
        nx_ref[:, here], nm_ref[:, here], ns_ref[:, here] = adam_step(
            x_ref[:, here], m_ref[:, here], s_ref[:, here], gradient, depth_rate
        )


def update_depths(local, far, values, moment, second, bound, chunk, done):
    images, rows, _ = far.shape
    block = 96
    steps = rows // block
    first = chunk * steps
    wide = pl.BlockSpec((images, block * LANES), lambda t: (0, first + t))
    return pl.pallas_call(
        functools.partial(depth_kernel, bound),
        grid=(steps,),
        out_shape=[jax.ShapeDtypeStruct(values.shape, jnp.float32)] * 3,
        in_specs=[
            pl.BlockSpec((images, block, LANES), lambda t: (0, first + t, 0)),
            pl.BlockSpec((images, block, LANES), lambda t: (0, t, 0)),
            wide,
            wide,
            wide,
        ]
        + [pl.BlockSpec(memory_space=pl.ANY)] * len(done),
        out_specs=[wide, wide, wide],
        input_output_aliases={5 + i: i for i in range(len(done))},
        scratch_shapes=[pltpu.VMEM((images * block, LANES), jnp.float32)],
        compiler_params=PARAMS,
        cost_estimate=COST,
        name="update_depths",
    )(local, far, values, moment, second, *done)


def rotation(first, middle, last):
    inverse = 1.0 / (1.0 + first * first + middle * middle + last * last)
    return (
        (1.0 + first * first - middle * middle - last * last) * inverse,
        2.0 * (first * middle - last) * inverse,
        2.0 * (first * last + middle) * inverse,
        2.0 * (first * middle + last) * inverse,
        (1.0 - first * first + middle * middle - last * last) * inverse,
        2.0 * (middle * last - first) * inverse,
        2.0 * (first * last - middle) * inverse,
        2.0 * (middle * last + first) * inverse,
        (1.0 - first * first - middle * middle + last * last) * inverse,
    )


def cross(a, b):
    return [a[(j + 1) % 3] * b[(j + 2) % 3] - a[(j + 2) % 3] * b[(j + 1) % 3] for j in range(3)]


def turn_gradient(spin, torque):
    factor = 2.0 / (1.0 + spin[0] * spin[0] + spin[1] * spin[1] + spin[2] * spin[2])
    swing = cross(spin, torque)
    return [factor * (torque[j] + swing[j]) for j in range(3)]


def view_parts(cam_ref, pose_ref):
    cams = [cam_ref[:, i : i + 1] for i in range(7)]
    poses = [pose_ref[:, i : i + 1] for i in range(7)]
    cam = rotation(cams[1], cams[2], cams[3])
    pose = rotation(poses[0], poses[1], poses[2])
    scale = jnp.exp(poses[6])
    back = jnp.exp(-poses[6])
    gap = [cams[4 + k] - poses[3 + k] for k in range(3)]
    both = [
        [sum(pose[3 * k + j] * cam[3 * k + i] for k in range(3)) for i in range(3)] for j in range(3)
    ]
    matrix = [[both[j][i] * back for i in range(3)] for j in range(3)]
    shift = [sum(pose[3 * k + j] * gap[k] for k in range(3)) * back for j in range(3)]
    return cams, poses, both, pose, scale, matrix, shift


def coef_kernel(images, image_ref, all_ref, pair_ref, out_ref, cam_ref, pose_ref):
    views = cam_ref.shape[0]
    for r in range(views):
        image = image_ref[r % 2, r // 2]
        owner = over(image, images)
        cam_ref[r : r + 1, :] = all_ref[owner, pl.ds(image - owner * images, 1), 0:7]
        pose_ref[r : r + 1, :] = pair_ref[r // 2 : r // 2 + 1, :]
    cams, _, _, _, scale, matrix, shift = view_parts(cam_ref, pose_ref)
    inverse_focal = jnp.exp(-cams[0]) * (1.0 / WIDTH)
    rows = [matrix[j][0] * inverse_focal for j in range(3)]
    rows += [matrix[j][1] * inverse_focal for j in range(3)]
    rows += [matrix[j][2] for j in range(3)]
    rows += shift
    rows += [scale * scale * (1.0 / SLOT_UNIT)]
    for i, row in enumerate(rows):
        out_ref[:, i : i + 1] = row


def view_coefs(pair_images, mail, pair_poses, images):
    views = 2 * pair_poses.shape[0]
    return pl.pallas_call(
        functools.partial(coef_kernel, images),
        out_shape=[
            jax.ShapeDtypeStruct((views, COEFS), jnp.float32),
            jax.ShapeDtypeStruct((views, 7), jnp.float32),
            jax.ShapeDtypeStruct((views, 7), jnp.float32),
        ],
        in_specs=[SMEM, VMEM, VMEM],
        out_specs=[VMEM, VMEM, VMEM],
        cost_estimate=COST,
        name="view_coefs",
    )(pair_images, mail, pair_poses)


def term_kernel(image_ref, cam_ref, pose_ref, *refs):
    cams, poses, both, pose, scale, matrix, shift = view_parts(cam_ref, pose_ref)
    sum_refs, (small_ref, terms, turns) = refs[:-3], refs[-3:]
    views = cam_ref.shape[0]
    sums = jnp.sum(sum(ref[...] for ref in sum_refs), axis=2)
    sums = [sums[:, i : i + 1] for i in range(SUMS)]
    square = scale * scale
    force, torque, stretch, drawn, lever = sums[0:3], sums[3:6], sums[6], sums[7], sums[8:11]
    push = [scale * sum(pose[3 * k + j] * force[j] for j in range(3)) for k in range(3)]
    swing = cross(shift, force)
    arm = [torque[j] - swing[j] for j in range(3)]
    camera_torque = [square * sum(both[j][i] * arm[j] for j in range(3)) for i in range(3)]
    pose_torque = [-square * torque[j] for j in range(3)]
    focal = -square * (drawn - sum(matrix[j][2] * lever[j] for j in range(3)))
    camera = [focal] + turn_gradient(cams[1:4], camera_torque) + push
    posed = (
        turn_gradient(poses[0:3], pose_torque) + [-value for value in push] + [-square * stretch]
    )
    terms[...] = jnp.zeros_like(terms)
    turns[...] = jnp.zeros_like(turns)
    for i in range(7):
        terms[:, i : i + 1] = camera[i]
        turns[:, i : i + 1] = posed[i]
    both_views = turns[pl.ds(0, views // 2, stride=2), :] + turns[pl.ds(1, views // 2, stride=2), :]
    images = small_ref.shape[0] - views // 2
    small_ref[0:images] = jnp.zeros((images, 7), jnp.float32)
    for r in range(views):
        here = pl.ds(image_ref[r % 2, r // 2], 1)
        small_ref[here, :] += terms[r : r + 1, 0:7]
    small_ref[images:] = both_views[:, 0:7]


def view_terms(pair_images, cams, poses, sums, images):
    views = cams.shape[0]
    return pl.pallas_call(
        term_kernel,
        out_shape=jax.ShapeDtypeStruct((images + views // 2, 7), jnp.float32),
        in_specs=[SMEM] + [VMEM] * (2 + len(sums)),
        out_specs=VMEM,
        scratch_shapes=[pltpu.VMEM((views, LANES), jnp.float32)] * 2,
        cost_estimate=COST,
        name="view_terms",
    )(pair_images, cams, poses, *sums)


def small_kernel(mail_ref, pose_ref, *refs):
    values, outs = refs[:6], refs[6:]
    camera_grad = jnp.sum(mail_ref[...], axis=0) * (1.0 / NPIX)
    pose_grad = pose_ref[...] * (1.0 / NPIX)
    for i, (gradient, rate) in enumerate(((camera_grad, camera_rate), (pose_grad, pose_rate))):
        new = adam_step(*(ref[...] for ref in values[3 * i : 3 * i + 3]), gradient, rate)
        for ref, value in zip(outs[3 * i : 3 * i + 3], new):
            ref[...] = value


def update_small(mail, pose_grad, cameras, poses):
    return pl.pallas_call(
        small_kernel,
        out_shape=[jax.ShapeDtypeStruct(value.shape, jnp.float32) for value in cameras + poses],
        in_specs=[VMEM] * 8,
        out_specs=[VMEM] * 6,
        cost_estimate=COST,
        name="update_small",
    )(mail, pose_grad, *cameras, *poses)


def body(
    pair_images,
    depths,
    depth_moment,
    depth_second,
    cameras,
    camera_moment,
    camera_second,
    pair_poses,
    pair_moment,
    pair_second,
    pointmaps,
    confidence,
):
    shards = lax.axis_size("img")
    half = shards // 2
    me = lax.axis_index("img")
    rep = lax.axis_index("rep")
    images, row_len = depths.shape
    pairs = pair_images.shape[0]
    requests = 2 * pairs
    cap = max(2, 3 * pairs // shards)
    rows = row_len // LANES
    far_bound = VIEW_BOUND * half * cap

    def swap(value, k):
        return lax.ppermute(value, "img", [(i, i ^ k) for i in range(shards)])

    slots = half * cap

    def exchange(values):
        return [values[0]] + [swap(values[k], k) for k in range(1, half)]

    tie = lax.optimization_barrier

    names = pair_images.T
    letters = letters_of(names, cameras, shards)
    codes = jnp.round((depths - DEPTH_MID) * (1.0 / DEPTH_STEP)).astype(INTS)
    codes = codes.reshape(images, rows, LANES)
    first = rows // 2
    parts = [codes[:, :first], codes[:, first:]]
    letters, parts[1:] = tie((letters, parts[1:]))
    mail = lax.all_to_all(letters, "img", 0, 0, tiled=True)
    far = [swap(part, half) for part in parts]

    lists = mail[:, images, :requests].astype(jnp.int32)
    table = slot_tables(me.reshape(1), lists, half, cap, images)
    near = pack_slots(table, [codes], 0, half, cap)
    mail, near = tie((mail, near))
    near = exchange(near)
    coefs, cams, poses = view_coefs(names, mail, pair_poses, images)
    row = rep * (row_len // WIDTH)
    row = (row.astype(jnp.float32) + (0.5 - 0.5 * HEIGHT)).reshape(1)
    views, slopes = prepare_views(row, coefs, pointmaps, confidence)
    far, slopes = tie((far, slopes))
    asked = exchange(pack_slots(table, far, slots, half, cap))

    near_sums = view_sums(table, coefs, row, views, near, 2 * slots, half, cap)
    every, early, late = range(half), range(half - 1), range(half - 1, half)
    near_grads = depth_grads(table, slopes, near, 2 * slots, every, cap)
    first_asked, near_sums, near_grads = tie((asked[:-1], near_sums, near_grads))
    far_grads = depth_grads(table, slopes, first_asked, 3 * slots, early, cap)
    last_asked, _ = tie((asked[-1:], far_grads))
    last_grads = depth_grads(table, slopes, last_asked, 3 * slots, late, cap)
    back = exchange([*far_grads, *last_grads])
    asked, _ = tie((asked, last_grads))
    far_sums = view_sums(table, coefs, row, views, asked, 3 * slots, half, cap)
    first_back, far_sums = tie((back[:-1], far_sums))
    totals = fold_totals(table, first_back, slots, early, images, cap)
    last_back, totals = tie((back[-1:], totals))
    folded = [fold_codes(table, totals, last_back, slots, late, cap, far_bound)]
    folded, far_sums = tie((folded, far_sums))
    far_codes = [swap(part, half) for part in folded]
    small = view_terms(names, cams, poses, [near_sums, far_sums], shards * images)
    near_grads, _ = tie((near_grads, totals))
    near_total = fold_totals(table, exchange(near_grads), 0, every, images, cap)
    done = []
    for c in range(1):
        done = update_depths(
            near_total, far_codes[c], depths, depth_moment, depth_second, far_bound, c, done
        )

    bit = 1
    while bit < lax.axis_size("rep"):
        small = small + lax.ppermute(
            small, "rep", [(i, i ^ bit) for i in range(lax.axis_size("rep"))]
        )
        bit *= 2
    camera_mail = lax.all_to_all(
        small[: shards * images].reshape(shards, images, 7), "img", 0, 0, tiled=True
    )
    camera_mail, done = tie((camera_mail, done))
    new = update_small(
        camera_mail,
        small[shards * images :].T,
        [cameras, camera_moment, camera_second],
        [pair_poses.T, pair_moment.T, pair_second.T],
    )
    return (*done, *new[:3], *(value.T for value in new[3:]))


def solution(mesh):
    return jax.shard_map(
        body,
        mesh=mesh,
        in_specs=(
            P("img", None),
            P("img", "rep"),
            P("img", "rep"),
            P("img", "rep"),
            P("img", None),
            P("img", None),
            P("img", None),
            P("img", None),
            P("img", None),
            P("img", None),
            P("img", None, None, "rep"),
            P("img", None, "rep"),
        ),
        out_specs=(
            P("img", "rep"),
            P("img", "rep"),
            P("img", "rep"),
            P("img", None),
            P("img", None),
            P("img", None),
            P("img", None),
            P("img", None),
            P("img", None),
        ),
        check_vma=False,
    )
```

```python
import functools
import math

import jax
import jax.numpy as jnp
from jax import lax
from jax.experimental import pallas as pl
from jax.experimental.pallas import tpu as pltpu
from jax.sharding import PartitionSpec as P

HEIGHT = 288
WIDTH = 512
START = 50
NPIX = 147456
LANES = 128
SWAP_PARTS = 2

beta_one = 0.9
beta_two = 0.999
adam_eps = 1e-08
depth_rate = 0.05
camera_rate = 0.01
pose_rate = 0.01

DEPTH_MID = 2.25
DEPTH_STEP = 1.75 / 32766.0
VIEW_BOUND = 340.0
SLOT_UNIT = VIEW_BOUND / 32766.0**2
CODE_UNIT = 8.0
INTS = jnp.int16
SUMS = 11
COEFS = 16

SMEM = pl.BlockSpec(memory_space=pltpu.SMEM)
VMEM = pl.BlockSpec(memory_space=pltpu.VMEM)
COST = pl.CostEstimate(flops=1, bytes_accessed=1, transcendentals=0)
PARAMS = pltpu.CompilerParams(vmem_limit_bytes=16 * 1024 * 1024)


def encode_slot(value):
    root = value * lax.rsqrt(jnp.maximum(jnp.abs(value), 1e-20))
    return jnp.round(root).astype(jnp.int32).astype(INTS)


def decode_slot(code):
    root = code.astype(jnp.int32).astype(jnp.float32)
    return root * jnp.abs(root)


def code_scale(bound):
    return 32766.0 / math.log2(1.0 + bound / CODE_UNIT)


def encode(magnitude, negative, bound):
    steps = (jnp.log2(1.0 + magnitude) * code_scale(bound) + 0.5).astype(jnp.int32)
    steps = jnp.minimum(steps, 32767)
    return jnp.where(negative, -steps, steps).astype(INTS)


def decode(code, bound):
    steps = code.astype(jnp.int32)
    size = jnp.abs(steps).astype(jnp.float32) * (1.0 / code_scale(bound))
    value = CODE_UNIT * jnp.exp2(size) - CODE_UNIT
    return jnp.where(steps < 0, -value, value)


def letter_kernel(image_ref, camera_ref, out_ref):
    shards, rows, _ = out_ref.shape
    lane = lax.broadcasted_iota(jnp.int32, (1, LANES), 1)
    names = jnp.zeros((1, LANES), jnp.int32)
    for r in range(2 * image_ref.shape[1]):
        names = jnp.where(lane == r, image_ref[r % 2, r // 2], names)
    for i in range(shards):
        out_ref[i, 0 : rows - 1, 0:7] = camera_ref[...]
        out_ref[i, rows - 1 : rows] = names.astype(jnp.float32)


def letters_of(pair_images, cameras, shards):
    images = cameras.shape[0]
    return pl.pallas_call(
        letter_kernel,
        out_shape=jax.ShapeDtypeStruct((shards, images + 1, LANES), jnp.float32),
        in_specs=[SMEM, VMEM],
        out_specs=VMEM,
        cost_estimate=COST,
        name="letters_of",
    )(pair_images, cameras)


def over(number, size):
    if size & (size - 1):
        return lax.div(number, size)
    return lax.shift_right_logical(number, size.bit_length() - 1)


def table_kernel(half, cap, images, me_ref, *refs):
    list_ref, tab_ref, count_ref = refs
    me = me_ref[0]
    shards = 2 * half
    spare = 2 * shards
    mirror = half + half // 2
    requests = list_ref.shape[1]

    @pl.loop(0, (spare + 1) * cap, unroll=8)
    def _(i):
        tab_ref[i] = -1

    @pl.loop(0, spare + 1, unroll=8)
    def _(i):
        count_ref[i] = 0

    def put(cell, value):
        rank = count_ref[cell]
        tab_ref[cell * cap + jnp.minimum(rank, cap - 1)] = value
        count_ref[cell] = rank + 1

    @pl.loop(0, requests)
    def _(r):
        for k in range(half):
            image = list_ref[me ^ k, r]
            owner = over(image, images)
            cell = jnp.where(owner == me, k, jnp.where(owner == (me ^ mirror), half + k, spare))
            put(cell, image - owner * images)
        away = over(list_ref[me, r], images) ^ me
        put(shards + jnp.where(away < half, away, half + (away ^ mirror)), r)


def slot_tables(me, lists, half, cap, images):
    return pl.pallas_call(
        functools.partial(table_kernel, half, cap, images),
        out_shape=jax.ShapeDtypeStruct(((4 * half + 1) * cap,), jnp.int32),
        in_specs=[SMEM, SMEM],
        out_specs=SMEM,
        scratch_shapes=[pltpu.SMEM((4 * half + 1,), jnp.int32)],
        cost_estimate=COST,
        name="slot_tables",
    )(me, lists)


def pack_kernel(first, half, tab_ref, *refs):
    map_refs, slot_refs = refs[:-half], refs[-half:]
    for k, slot_ref in enumerate(slot_refs):

        @pl.loop(0, slot_ref.shape[0])
        def _(c):
            image = jnp.maximum(tab_ref[first + k * slot_ref.shape[0] + c], 0)
            first_row = 0
            for map_ref in map_refs:
                rows = map_ref.shape[1]
                slot_ref[c, first_row : first_row + rows] = map_ref[image]
                first_row += rows


def pack_slots(table, maps, first, half, cap):
    rows = sum(part.shape[1] for part in maps)
    return pl.pallas_call(
        functools.partial(pack_kernel, first, half),
        out_shape=[jax.ShapeDtypeStruct((cap, rows, LANES), INTS)] * half,
        in_specs=[SMEM] + [VMEM] * len(maps),
        out_specs=[VMEM] * half,
        compiler_params=PARAMS,
        cost_estimate=COST,
        name="pack_slots",
    )(table, *maps)


def columns_and_lines(top):
    across = WIDTH // LANES
    line = lax.broadcasted_iota(jnp.int32, (16, LANES), 0)
    lane = lax.broadcasted_iota(jnp.int32, (16, LANES), 1)
    columns = ((line % across) * LANES + lane).astype(jnp.float32) + (0.5 - 0.5 * WIDTH)
    return columns, (line // across).astype(jnp.float32) + top


def ray_start(columns, lines, coef):
    ray = [columns * coef(j) + (lines * coef(3 + j) + coef(6 + j)) for j in range(3)]
    step = [coef(3 + j) * (16.0 * LANES / WIDTH) for j in range(3)]
    return ray, step


def prepare_kernel(row_ref, coef_ref, point_ref, weight_ref, view_ref, slope_ref, wide):
    rows = view_ref.shape[2]
    columns, lines = columns_and_lines(row_ref[0])

    @pl.loop(0, point_ref.shape[0])
    def _(pair):
        for q in range(4):
            source = point_ref.at[pair, q] if q < 3 else weight_ref.at[pair]
            wide[q] = source[...].astype(jnp.float32)
        for v in range(2):
            view = 2 * pair + v

            def coef(i):
                return coef_ref[view, i]

            ray, step = ray_start(columns, lines, coef)
            shift = [coef(9 + j) for j in range(3)]
            gain = coef(12)
            for t in range(0, rows, 16):
                here = slice(t, t + 16)
                part = [wide[q, pl.ds(2 * t + v, 16, stride=2), :] for q in range(4)]
                for q in range(4):
                    view_ref[view, q, here] = part[q].astype(jnp.bfloat16)
                weight = part[3] * gain
                slope = weight * (ray[0] * ray[0] + ray[1] * ray[1] + ray[2] * ray[2])
                rest = [ray[j] * (shift[j] - part[j]) for j in range(3)]
                slope_ref[view, 0, here] = slope * DEPTH_STEP
                slope_ref[view, 1, here] = slope * DEPTH_MID + weight * (
                    rest[0] + rest[1] + rest[2]
                )
                ray = [ray[j] + step[j] for j in range(3)]


def prepare_views(row, coefs, points, weights):
    pairs, _, _, pixels = points.shape
    rows = pixels // LANES
    points = (
        points.transpose(0, 2, 1, 3)
        .reshape(pairs, 3, 2, rows, LANES)
        .transpose(0, 1, 3, 2, 4)
        .reshape(pairs, 3, 2 * rows, LANES)
    )
    weights = (
        weights.reshape(pairs, 2, rows, LANES).transpose(0, 2, 1, 3).reshape(pairs, 2 * rows, LANES)
    )
    return pl.pallas_call(
        prepare_kernel,
        out_shape=[
            jax.ShapeDtypeStruct((2 * pairs, 4, rows, LANES), jnp.bfloat16),
            jax.ShapeDtypeStruct((2 * pairs, 2, rows, LANES), jnp.float32),
        ],
        in_specs=[SMEM, SMEM, VMEM, VMEM],
        out_specs=[VMEM, VMEM],
        scratch_shapes=[pltpu.VMEM((4, 2 * rows, LANES), jnp.float32)],
        compiler_params=PARAMS,
        cost_estimate=COST,
        name="prepare_views",
    )(row, coefs, points, weights)


def slots_at(refs, k, tab_ref):
    return refs[k] if len(refs) > 1 else refs[0].at[k ^ tab_ref[tab_ref.shape[0] - 1]]


def grad_kernel(first, ks, cap, tab_ref, slope_ref, *refs):
    depth_refs, grad_refs = refs[: len(ks)], refs[len(ks) :]
    rows = slope_ref.shape[2]
    for k, depth_ref, grad_ref in zip(ks, depth_refs, grad_refs):

        @pl.loop(0, cap)
        def _(c):
            view = tab_ref[first + k * cap + c]

            @pl.when(view >= 0)
            def _():
                for t in range(0, rows, 16):
                    here = slice(t, t + 16)
                    code = depth_ref[c, here].astype(jnp.int32).astype(jnp.float32)
                    along = code * slope_ref[view, 0, here] + slope_ref[view, 1, here]
                    grad_ref[c, here] = encode_slot(along)


def depth_grads(table, slopes, depths, first, ks, cap):
    rows = slopes.shape[2]
    return pl.pallas_call(
        functools.partial(grad_kernel, first, ks, cap),
        out_shape=[jax.ShapeDtypeStruct((cap, rows, LANES), INTS)] * len(ks),
        in_specs=[SMEM] + [VMEM] * (1 + len(ks)),
        out_specs=[VMEM] * len(ks),
        compiler_params=PARAMS,
        cost_estimate=COST,
        name="depth_grads",
    )(table, slopes, *depths)


def sum_kernel(first, half, cap, tab_ref, coef_ref, row_ref, view_ref, *refs):
    depth_refs = refs[:-2]
    sum_ref, depth_all = refs[-2:]
    slots, rows, _ = depth_all.shape
    for k in range(half):
        depth_ref = depth_refs[k]
        depth_all[k * cap : (k + 1) * cap] = depth_ref[...]
    sum_ref[...] = jnp.zeros_like(sum_ref)
    columns, lines = columns_and_lines(row_ref[0])

    @pl.loop(0, slots)
    def _(s):
        view = tab_ref[first + s]

        @pl.when(view >= 0)
        def _():
            def coef(i):
                return coef_ref[view, i]

            ray, step = ray_start(columns, lines, coef)
            shift = [coef(9 + j) for j in range(3)]
            totals = [None] * SUMS

            def add(i, value):
                value = value[:8] + value[8:]
                totals[i] = value if totals[i] is None else totals[i] + value

            for t in range(0, rows, 16):
                here = slice(t, t + 16)
                point = [view_ref[view, j, here].astype(jnp.float32) for j in range(3)]
                weight = view_ref[view, 3, here].astype(jnp.float32)
                depth = (
                    depth_all[s, here].astype(jnp.int32).astype(jnp.float32) * DEPTH_STEP
                    + DEPTH_MID
                )
                pull = [weight * (depth * ray[j] + (shift[j] - point[j])) for j in range(3)]
                along = pull[0] * ray[0] + pull[1] * ray[1] + pull[2] * ray[2]
                for j in range(3):
                    add(j, pull[j])
                    add(8 + j, depth * pull[j])
                    a, b = (j + 1) % 3, (j + 2) % 3
                    add(3 + j, point[a] * pull[b] - point[b] * pull[a])
                add(6, point[0] * pull[0] + point[1] * pull[1] + point[2] * pull[2])
                add(7, depth * along)
                ray = [ray[j] + step[j] for j in range(3)]
            for i in range(SUMS):
                sum_ref[view, i : i + 1] = jnp.sum(totals[i], axis=0, keepdims=True)


def view_sums(table, coefs, row, views, depths, first, half, cap):
    rows = depths[0].shape[1]
    return pl.pallas_call(
        functools.partial(sum_kernel, first, half, cap),
        out_shape=jax.ShapeDtypeStruct((views.shape[0], COEFS, LANES), jnp.float32),
        in_specs=[SMEM, SMEM, SMEM] + [VMEM] * (1 + len(depths)),
        out_specs=VMEM,
        scratch_shapes=[pltpu.VMEM((half * cap, rows, LANES), INTS)],
        compiler_params=PARAMS,
        cost_estimate=COST,
        name="view_sums",
    )(table, coefs, row, views, *depths)


def fold(first, ks, cap, tab_ref, slot_refs, total_ref):
    for k, slot_ref in zip(ks, slot_refs):

        @pl.loop(0, cap)
        def _(c):
            image = tab_ref[first + k * cap + c]

            @pl.when(image >= 0)
            def _():
                total_ref[image] += decode_slot(slot_ref[c])


def total_kernel(first, ks, cap, tab_ref, *refs):
    refs[-1][...] = jnp.zeros_like(refs[-1])
    fold(first, ks, cap, tab_ref, refs[:-1], refs[-1])


def fold_totals(table, slots, first, ks, images, cap):
    rows = slots[0].shape[1]
    return pl.pallas_call(
        functools.partial(total_kernel, first, ks, cap),
        out_shape=jax.ShapeDtypeStruct((images, rows, LANES), jnp.float32),
        in_specs=[SMEM] + [VMEM] * len(slots),
        out_specs=VMEM,
        compiler_params=PARAMS,
        cost_estimate=COST,
        name="fold_totals",
    )(table, *slots)


def add_code_kernel(first, ks, cap, bound, tab_ref, total_ref, *refs):
    slot_refs, out_ref, more = refs[:-2], refs[-2], refs[-1]
    more[...] = total_ref[...]
    fold(first, ks, cap, tab_ref, slot_refs, more)

    @pl.loop(0, more.shape[0])
    def _(i):
        value = more[i]
        out_ref[i] = encode(jnp.abs(value) * (SLOT_UNIT / CODE_UNIT), value < 0.0, bound)


def fold_codes(table, totals, slots, first, ks, cap, bound):
    return pl.pallas_call(
        functools.partial(add_code_kernel, first, ks, cap, bound),
        out_shape=jax.ShapeDtypeStruct(totals.shape, INTS),
        in_specs=[SMEM] + [VMEM] * (1 + len(slots)),
        out_specs=VMEM,
        scratch_shapes=[pltpu.VMEM(totals.shape, jnp.float32)],
        compiler_params=PARAMS,
        cost_estimate=COST,
        name="fold_codes",
    )(table, totals, *slots)


def adam_step(values, moment, second, gradient, step_rate):
    step_count = START + 1
    moment = beta_one * moment + (1.0 - beta_one) * gradient
    second = beta_two * second + (1.0 - beta_two) * gradient * gradient
    pace = step_rate / (1.0 - beta_one**step_count)
    grown = second * (1.0 / (1.0 - beta_two**step_count))
    values = values - (moment * pace) / (grown * lax.rsqrt(grown) + adam_eps)
    return (values, moment, second)


def depth_kernel(bound, local_ref, far_ref, x_ref, m_ref, s_ref, *refs):
    nx_ref, nm_ref, ns_ref, grad = refs[-4:]
    images, rows, _ = local_ref.shape
    for i in range(images):
        grad[i * rows : (i + 1) * rows] = local_ref[i] * SLOT_UNIT + decode(
            far_ref[i], bound
        )
    for t in range(rows):
        here = slice(t * LANES, (t + 1) * LANES)
        gradient = grad[pl.ds(t, images, stride=rows), :]
        nx_ref[:, here], nm_ref[:, here], ns_ref[:, here] = adam_step(
            x_ref[:, here], m_ref[:, here], s_ref[:, here], gradient, depth_rate
        )


def update_depths(local, far, values, moment, second, bound, chunk, done):
    images, rows, _ = far.shape
    block = 96
    steps = rows // block
    first = chunk * steps
    wide = pl.BlockSpec((images, block * LANES), lambda t: (0, first + t))
    return pl.pallas_call(
        functools.partial(depth_kernel, bound),
        grid=(steps,),
        out_shape=[jax.ShapeDtypeStruct(values.shape, jnp.float32)] * 3,
        in_specs=[
            pl.BlockSpec((images, block, LANES), lambda t: (0, first + t, 0)),
            pl.BlockSpec((images, block, LANES), lambda t: (0, t, 0)),
            wide,
            wide,
            wide,
        ]
        + [pl.BlockSpec(memory_space=pl.ANY)] * len(done),
        out_specs=[wide, wide, wide],
        input_output_aliases={5 + i: i for i in range(len(done))},
        scratch_shapes=[pltpu.VMEM((images * block, LANES), jnp.float32)],
        compiler_params=PARAMS,
        cost_estimate=COST,
        name="update_depths",
    )(local, far, values, moment, second, *done)


def rotation(first, middle, last):
    inverse = 1.0 / (1.0 + first * first + middle * middle + last * last)
    return (
        (1.0 + first * first - middle * middle - last * last) * inverse,
        2.0 * (first * middle - last) * inverse,
        2.0 * (first * last + middle) * inverse,
        2.0 * (first * middle + last) * inverse,
        (1.0 - first * first + middle * middle - last * last) * inverse,
        2.0 * (middle * last - first) * inverse,
        2.0 * (first * last - middle) * inverse,
        2.0 * (middle * last + first) * inverse,
        (1.0 - first * first - middle * middle + last * last) * inverse,
    )


def cross(a, b):
    return [a[(j + 1) % 3] * b[(j + 2) % 3] - a[(j + 2) % 3] * b[(j + 1) % 3] for j in range(3)]


def turn_gradient(spin, torque):
    factor = 2.0 / (1.0 + spin[0] * spin[0] + spin[1] * spin[1] + spin[2] * spin[2])
    swing = cross(spin, torque)
    return [factor * (torque[j] + swing[j]) for j in range(3)]


def view_parts(cam_ref, pose_ref):
    cams = [cam_ref[:, i : i + 1] for i in range(7)]
    poses = [pose_ref[:, i : i + 1] for i in range(7)]
    cam = rotation(cams[1], cams[2], cams[3])
    pose = rotation(poses[0], poses[1], poses[2])
    scale = jnp.exp(poses[6])
    back = jnp.exp(-poses[6])
    gap = [cams[4 + k] - poses[3 + k] for k in range(3)]
    both = [
        [sum(pose[3 * k + j] * cam[3 * k + i] for k in range(3)) for i in range(3)] for j in range(3)
    ]
    matrix = [[both[j][i] * back for i in range(3)] for j in range(3)]
    shift = [sum(pose[3 * k + j] * gap[k] for k in range(3)) * back for j in range(3)]
    return cams, poses, both, pose, scale, matrix, shift


def coef_kernel(images, image_ref, all_ref, pair_ref, out_ref, cam_ref, pose_ref):
    views = cam_ref.shape[0]
    for r in range(views):
        image = image_ref[r % 2, r // 2]
        owner = over(image, images)
        cam_ref[r : r + 1, :] = all_ref[owner, pl.ds(image - owner * images, 1), 0:7]
        pose_ref[r : r + 1, :] = pair_ref[r // 2 : r // 2 + 1, :]
    cams, _, _, _, scale, matrix, shift = view_parts(cam_ref, pose_ref)
    inverse_focal = jnp.exp(-cams[0]) * (1.0 / WIDTH)
    rows = [matrix[j][0] * inverse_focal for j in range(3)]
    rows += [matrix[j][1] * inverse_focal for j in range(3)]
    rows += [matrix[j][2] for j in range(3)]
    rows += shift
    rows += [scale * scale * (1.0 / SLOT_UNIT)]
    for i, row in enumerate(rows):
        out_ref[:, i : i + 1] = row


def view_coefs(pair_images, mail, pair_poses, images):
    views = 2 * pair_poses.shape[0]
    return pl.pallas_call(
        functools.partial(coef_kernel, images),
        out_shape=[
            jax.ShapeDtypeStruct((views, COEFS), jnp.float32),
            jax.ShapeDtypeStruct((views, 7), jnp.float32),
            jax.ShapeDtypeStruct((views, 7), jnp.float32),
        ],
        in_specs=[SMEM, VMEM, VMEM],
        out_specs=[VMEM, VMEM, VMEM],
        cost_estimate=COST,
        name="view_coefs",
    )(pair_images, mail, pair_poses)


def term_kernel(image_ref, cam_ref, pose_ref, *refs):
    cams, poses, both, pose, scale, matrix, shift = view_parts(cam_ref, pose_ref)
    sum_refs, (small_ref, terms, turns) = refs[:-3], refs[-3:]
    views = cam_ref.shape[0]
    sums = jnp.sum(sum(ref[...] for ref in sum_refs), axis=2)
    sums = [sums[:, i : i + 1] for i in range(SUMS)]
    square = scale * scale
    force, torque, stretch, drawn, lever = sums[0:3], sums[3:6], sums[6], sums[7], sums[8:11]
    push = [scale * sum(pose[3 * k + j] * force[j] for j in range(3)) for k in range(3)]
    swing = cross(shift, force)
    arm = [torque[j] - swing[j] for j in range(3)]
    camera_torque = [square * sum(both[j][i] * arm[j] for j in range(3)) for i in range(3)]
    pose_torque = [-square * torque[j] for j in range(3)]
    focal = -square * (drawn - sum(matrix[j][2] * lever[j] for j in range(3)))
    camera = [focal] + turn_gradient(cams[1:4], camera_torque) + push
    posed = (
        turn_gradient(poses[0:3], pose_torque) + [-value for value in push] + [-square * stretch]
    )
    terms[...] = jnp.zeros_like(terms)
    turns[...] = jnp.zeros_like(turns)
    for i in range(7):
        terms[:, i : i + 1] = camera[i]
        turns[:, i : i + 1] = posed[i]
    both_views = turns[pl.ds(0, views // 2, stride=2), :] + turns[pl.ds(1, views // 2, stride=2), :]
    images = small_ref.shape[0] - views // 2
    small_ref[0:images] = jnp.zeros((images, 7), jnp.float32)
    for r in range(views):
        here = pl.ds(image_ref[r % 2, r // 2], 1)
        small_ref[here, :] += terms[r : r + 1, 0:7]
    small_ref[images:] = both_views[:, 0:7]


def view_terms(pair_images, cams, poses, sums, images):
    views = cams.shape[0]
    return pl.pallas_call(
        term_kernel,
        out_shape=jax.ShapeDtypeStruct((images + views // 2, 7), jnp.float32),
        in_specs=[SMEM] + [VMEM] * (2 + len(sums)),
        out_specs=VMEM,
        scratch_shapes=[pltpu.VMEM((views, LANES), jnp.float32)] * 2,
        cost_estimate=COST,
        name="view_terms",
    )(pair_images, cams, poses, *sums)


def small_kernel(mail_ref, pose_ref, *refs):
    values, outs = refs[:6], refs[6:]
    camera_grad = jnp.sum(mail_ref[...], axis=0) * (1.0 / NPIX)
    pose_grad = pose_ref[...] * (1.0 / NPIX)
    for i, (gradient, rate) in enumerate(((camera_grad, camera_rate), (pose_grad, pose_rate))):
        new = adam_step(*(ref[...] for ref in values[3 * i : 3 * i + 3]), gradient, rate)
        for ref, value in zip(outs[3 * i : 3 * i + 3], new):
            ref[...] = value


def update_small(mail, pose_grad, cameras, poses):
    return pl.pallas_call(
        small_kernel,
        out_shape=[jax.ShapeDtypeStruct(value.shape, jnp.float32) for value in cameras + poses],
        in_specs=[VMEM] * 8,
        out_specs=[VMEM] * 6,
        cost_estimate=COST,
        name="update_small",
    )(mail, pose_grad, *cameras, *poses)


def body(
    pair_images,
    depths,
    depth_moment,
    depth_second,
    cameras,
    camera_moment,
    camera_second,
    pair_poses,
    pair_moment,
    pair_second,
    pointmaps,
    confidence,
):
    shards = lax.axis_size("img")
    half = shards // 2
    me = lax.axis_index("img")
    rep = lax.axis_index("rep")
    images, row_len = depths.shape
    pairs = pair_images.shape[0]
    requests = 2 * pairs
    cap = max(2, 3 * pairs // shards)
    rows = row_len // LANES
    far_bound = VIEW_BOUND * half * cap

    def swap(value, k):
        return lax.ppermute(value, "img", [(i, i ^ k) for i in range(shards)])

    slots = half * cap

    def exchange(values):
        return [values[0]] + [swap(values[k], k) for k in range(1, half)]

    tie = lax.optimization_barrier

    names = pair_images.T
    letters = letters_of(names, cameras, shards)
    codes = jnp.round((depths - DEPTH_MID) * (1.0 / DEPTH_STEP)).astype(INTS)
    codes = codes.reshape(images, rows, LANES)
    first = rows // 2
    parts = [codes[:, :first], codes[:, first:]]
    mail = lax.all_to_all(letters, "img", 0, 0, tiled=True)
    mail, parts = tie((mail, parts))
    mirror = half + half // 2
    far = [swap(part, mirror) for part in parts]

    lists = mail[:, images, :requests].astype(jnp.int32)
    table = slot_tables(me.reshape(1), lists, half, cap, images)
    near = pack_slots(table, [codes], 0, half, cap)
    mail, near = tie((mail, near))
    near = exchange(near)
    coefs, cams, poses = view_coefs(names, mail, pair_poses, images)
    row = rep * (row_len // WIDTH)
    row = (row.astype(jnp.float32) + (0.5 - 0.5 * HEIGHT)).reshape(1)
    views, slopes = prepare_views(row, coefs, pointmaps, confidence)
    far, slopes = tie((far, slopes))
    asked = exchange(pack_slots(table, far, slots, half, cap))

    near_sums = view_sums(table, coefs, row, views, near, 2 * slots, half, cap)
    every, early, late = range(half), range(half - 1), range(half - 1, half)
    near_grads = depth_grads(table, slopes, near, 2 * slots, every, cap)
    first_asked, near_sums, near_grads = tie((asked[:-1], near_sums, near_grads))
    far_grads = depth_grads(table, slopes, first_asked, 3 * slots, early, cap)
    last_asked, _ = tie((asked[-1:], far_grads))
    last_grads = depth_grads(table, slopes, last_asked, 3 * slots, late, cap)
    back = exchange([*far_grads, *last_grads])
    asked, _ = tie((asked, last_grads))
    far_sums = view_sums(table, coefs, row, views, asked, 3 * slots, half, cap)
    first_back, far_sums = tie((back[:-1], far_sums))
    totals = fold_totals(table, first_back, slots, early, images, cap)
    last_back, totals = tie((back[-1:], totals))
    folded = [fold_codes(table, totals, last_back, slots, late, cap, far_bound)]
    folded, far_sums = tie((folded, far_sums))
    far_codes = [swap(part, mirror) for part in folded]
    small = view_terms(names, cams, poses, [near_sums, far_sums], shards * images)
    near_grads, _ = tie((near_grads, totals))
    near_total = fold_totals(table, exchange(near_grads), 0, every, images, cap)
    done = []
    for c in range(1):
        done = update_depths(
            near_total, far_codes[c], depths, depth_moment, depth_second, far_bound, c, done
        )

    bit = 1
    while bit < lax.axis_size("rep"):
        small = small + lax.ppermute(
            small, "rep", [(i, i ^ bit) for i in range(lax.axis_size("rep"))]
        )
        bit *= 2
    camera_mail = lax.all_to_all(
        small[: shards * images].reshape(shards, images, 7), "img", 0, 0, tiled=True
    )
    camera_mail, done = tie((camera_mail, done))
    new = update_small(
        camera_mail,
        small[shards * images :].T,
        [cameras, camera_moment, camera_second],
        [pair_poses.T, pair_moment.T, pair_second.T],
    )
    return (*done, *new[:3], *(value.T for value in new[3:]))


def solution(mesh):
    return jax.shard_map(
        body,
        mesh=mesh,
        in_specs=(
            P("img", None),
            P("img", "rep"),
            P("img", "rep"),
            P("img", "rep"),
            P("img", None),
            P("img", None),
            P("img", None),
            P("img", None),
            P("img", None),
            P("img", None),
            P("img", None, None, "rep"),
            P("img", None, "rep"),
        ),
        out_specs=(
            P("img", "rep"),
            P("img", "rep"),
            P("img", "rep"),
            P("img", None),
            P("img", None),
            P("img", None),
            P("img", None),
            P("img", None),
            P("img", None),
        ),
        check_vma=False,
    )
```
